32 devices in a mesh: seq: 4 (over z), fsdp: 8 (over y, x, core).
Axes of the slice: x: 2, y: 2, z: 4, core: 2. Of those that a mesh axis runs over, the one named last changes fastest.
Arguments:
- inputs: bfloat16 [8, 1024, 1024], P('fsdp', 'seq'), may hold values from -6 to 6
- lengths: int32 [8, 3], P('fsdp'), may hold values from 1 to 1022, as said below
- ffn_in: bfloat16 [1, 2, 1024, 4096], P(None, None, ('seq', 'fsdp')), may hold values from -0.1875 to 0.1875
- ffn_out: bfloat16 [1, 2, 4096, 1024], P(None, None, None, ('seq', 'fsdp')), may hold values from -0.09375 to 0.09375
- qkv_weight: bfloat16 [1, 1024, 3072], P(None, ('seq', 'fsdp')), may hold values from -0.1875 to 0.1875
- out_weight: bfloat16 [1, 1024, 1024], P(None, ('seq', 'fsdp')), may hold values from -1 to 1
- conv_in: bfloat16 [1, 1024, 2048], P(None, ('seq', 'fsdp')), may hold values from -0.1875 to 0.1875
- conv_depth: bfloat16 [1, 31, 1024], P(None, None, ('seq', 'fsdp')), may hold values from -1 to 1
- conv_out: bfloat16 [1, 1024, 1024], P(None, ('seq', 'fsdp')), may hold values from -0.1875 to 0.1875
- norm_gain: bfloat16 [1, 6, 1024], P(None, None, ('seq', 'fsdp')), may hold values from 0.5 to 1.5
- norm_bias: bfloat16 [1, 6, 1024], P(None, None, ('seq', 'fsdp')), may hold values from -4 to 4
- rel_key: bfloat16 [1, 73, 64], replicated, may hold values from -6 to 6
- cotangent: bfloat16 [8, 1024, 1024], P('fsdp', 'seq'), may hold values from -6 to 6
Outputs:
- output: bfloat16 [8, 1024, 1024], P('fsdp', 'seq')
- input_grad: float32 [8, 1024, 1024], P('fsdp', 'seq')
- ffn_in_grad: float32 [1, 2, 1024, 4096], P(None, None, ('seq', 'fsdp'))
- ffn_out_grad: float32 [1, 2, 4096, 1024], P(None, None, None, ('seq', 'fsdp'))
- qkv_grad: float32 [1, 1024, 3072], P(None, ('seq', 'fsdp'))
- out_grad: float32 [1, 1024, 1024], P(None, ('seq', 'fsdp'))
- conv_in_grad: float32 [1, 1024, 2048], P(None, ('seq', 'fsdp'))
- conv_depth_grad: float32 [1, 31, 1024], P(None, None, ('seq', 'fsdp'))
- conv_out_grad: float32 [1, 1024, 1024], P(None, ('seq', 'fsdp'))
- gain_grad: float32 [1, 6, 1024], P(None, None, ('seq', 'fsdp'))
- bias_grad: float32 [1, 6, 1024], P(None, None, ('seq', 'fsdp'))
- rel_grad: float32 [1, 73, 64], replicated
The draws below stay inside these ranges and needn't reach their ends.
Inputs may be any that keep to these rules, and one draw needn't show every extreme that they name: In each group the 3 clip lengths sum to 1024; one clip, which one drawn from the seed, starts among the group's first 256 positions and ends among its last 256; the other clips are shorter than half of 256. In one group, drawn from the seed, the other clips have length 1, so that its long clip has 1022 tokens.
All inputs are finite; a program needn't handle non-finite values.
Results may differ from the reference program's by a relative error of at most 0.015.
Values may be sent and summed in bfloat16 or wider, within the bound.
No kernel may reach another device: no remote copies, remote signals or barrier semaphores. Data moves between devices by JAX's collectives and lax.ppermute only.
A program may use at most 256 MiB of HBM per device.

```python
import jax
import jax.numpy as jnp
from jax import lax

D = 1024
HEADS = 16
HEAD_DIM = 64
FF = 4096
KERNEL = 31
LEFT = 64
RIGHT = 8
LAYERS = 1
CLIPS = 3
TOK_DEV = 256
WIN = 73
GROUP_TOK = 1024
GROUPS = 8
N_SEQ = 4


def draw_lengths(key, part):
    short_key, pick_key, group_key = jax.random.split(jax.random.fold_in(key, 11), 3)
    shorts = jax.random.randint(short_key, (GROUPS, CLIPS), 1, TOK_DEV // 2)
    unit_group = jax.random.randint(group_key, (), 0, GROUPS)
    shorts = jnp.where(jnp.arange(GROUPS)[:, None] == unit_group, 1, shorts)
    chosen = jax.random.randint(pick_key, (GROUPS, 1), 0, CLIPS)
    is_long = jnp.arange(CLIPS)[None, :] == chosen
    rest_sum = jnp.sum(jnp.where(is_long, 0, shorts), axis=1, keepdims=True)
    return jnp.where(is_long, GROUP_TOK - rest_sum, shorts).astype(jnp.int32)


def raised(values, own_key, source, target, parts, factor):
    def block_of(axis_at):
        return (jnp.arange(values.shape[axis_at]) // (values.shape[axis_at] // parts)).reshape((-1,) + (1,) * (values.ndim - 1 - axis_at))

    first = jax.random.permutation(own_key, parts)[block_of(target)]
    far = (block_of(target) + parts // 2) % parts
    return jnp.where((block_of(source) == first) | (block_of(source) == far), factor * values, values)


def levels(rng, dims, shards, smallest, top_value):
    def one(position, shards_of):
        heights = jax.random.uniform(jax.random.fold_in(jax.random.fold_in(rng, 6), position), (shards_of,), jnp.float32, smallest / len(shards), top_value / len(shards))
        return jnp.repeat(jnp.exp(heights), dims[position] // shards_of).reshape((-1,) + (1,) * (len(dims) - position - 1))

    gain = one(*shards[0])
    for cut in shards[1:]:
        gain = gain * one(*cut)
    return gain


def scatter_about(key, extent, scale, bound, cuts=(), kind=jnp.bfloat16):
    drawn = scale * jax.random.normal(key, extent, jnp.float32)
    if cuts:
        drawn = drawn * levels(key, extent, cuts, -0.22, 0.18)
    return jnp.clip(drawn, -bound, bound).astype(kind)


def gaussian_with(own_key, extent, scale, most, cuts, heavy, held_as=jnp.bfloat16):
    values = scale * jax.random.normal(own_key, extent, jnp.float32)
    if cuts:
        values = values * levels(own_key, extent, cuts, -0.22, 0.18)
    return jnp.clip(raised(values, jax.random.fold_in(own_key, 3), *heavy), -most, most).astype(held_as)


def setup_inputs(seed: int = 0) -> dict:
    seeds = jax.random.split(jax.random.key(seed), 14)
    return {
        "inputs": scatter_about(seeds[0], (GROUPS, GROUP_TOK, D), 1.0, 6.0, ((0, 8), (1, 4))),
        "lengths": draw_lengths(jax.random.fold_in(seeds[13], 71), 0),
        "ffn_in": scatter_about(seeds[2], (LAYERS, 2, D, FF), D ** -0.5, 0.1875, ((2, 32),)),
        "ffn_out": scatter_about(seeds[3], (LAYERS, 2, FF, D), FF ** -0.5, 0.09375, ((3, 32),)),
        "qkv_weight": scatter_about(seeds[4], (LAYERS, D, 3 * D), D ** -0.5, 0.1875, ((1, 32),)),
        "out_weight": scatter_about(seeds[5], (LAYERS, D, D), (D // 32) ** -0.5, 1.0, ((1, 32),)),
        "conv_in": scatter_about(seeds[6], (LAYERS, D, 2 * D), D ** -0.5, 0.1875, ((1, 32),)),
        "conv_depth": scatter_about(seeds[7], (LAYERS, KERNEL, D), KERNEL ** -0.5, 1.0, ((2, 32),)),
        "conv_out": scatter_about(seeds[8], (LAYERS, D, D), D ** -0.5, 0.1875, ((1, 32),)),
        "norm_gain": jnp.clip(1.0 + 0.1 * jax.random.normal(seeds[9], (LAYERS, 6, D), jnp.float32), 0.5, 1.5).astype(jnp.bfloat16),
        "norm_bias": scatter_about(seeds[10], (LAYERS, 6, D), 0.3, 4.0, ((2, 32),)),
        "rel_key": scatter_about(seeds[11], (LAYERS, WIN, HEAD_DIM), 1.0, 6.0),
        "cotangent": gaussian_with(seeds[12], (GROUPS, GROUP_TOK, D), 1.0, 6.0, ((0, 8), (1, 4)), (0, 2, 8, 2.0)),
    }


@jax.custom_vjp
def low(v):
    return lax.optimization_barrier(v.astype(jnp.bfloat16)).astype(jnp.float32)

@jax.custom_vjp
def low_back(v):
    return v

def low_keep(v):
    return (low(v), None)

def low_pass(kept, grad):
    return (grad,)

def back_keep(v):
    return (v, None)

def back_low(kept, grad):
    return (low(grad),)
low.defvjp(low_keep, low_pass)
low_back.defvjp(back_keep, back_low)

def matmul(left_side, right_side):
    return jnp.dot(left_side, right_side, precision=lax.Precision.HIGHEST, preferred_element_type=jnp.float32)

def layer_norm(values, gain_row, bias_row):
    centered = values - lax.optimization_barrier(jnp.mean(values, axis=-1, keepdims=True))
    variance = lax.optimization_barrier(jnp.mean(centered * centered, axis=-1, keepdims=True))
    return centered * lax.rsqrt(variance + 1e-05) * gain_row + bias_row

def swish_act(values):
    return values * jax.nn.sigmoid(values)

def skew_band(rel_scores, key_count):
    head_count, row_count, band_width = rel_scores.shape
    padded = jnp.pad(rel_scores, ((0, 0), (0, 0), (0, key_count + 1 - band_width)))
    flattened = padded.reshape(head_count, row_count * (key_count + 1))[:, :row_count * key_count]
    return flattened.reshape(head_count, row_count, key_count)

def attend(queries, keys_in, values_in, relative, clip_ids):
    key_count = TOK_DEV + LEFT + RIGHT
    keys_padded = jnp.pad(keys_in, ((LEFT, RIGHT), (0, 0)))
    values_padded = jnp.pad(values_in, ((LEFT, RIGHT), (0, 0)))
    ids_padded = jnp.concatenate([jnp.full((LEFT,), -1, jnp.int32), clip_ids, jnp.full((RIGHT,), CLIPS, jnp.int32)])
    offsets = jnp.arange(key_count, dtype=jnp.int32)[None, :] - jnp.arange(TOK_DEV, dtype=jnp.int32)[:, None]
    in_band = (offsets >= 0) & (offsets <= LEFT + RIGHT)

    def block_out(first_row):
        query_block = lax.dynamic_slice_in_dim(queries, first_row, TOK_DEV, 0).reshape(TOK_DEV, HEADS, HEAD_DIM)
        key_block = lax.dynamic_slice_in_dim(keys_padded, first_row, key_count, 0).reshape(key_count, HEADS, HEAD_DIM)
        value_block = lax.dynamic_slice_in_dim(values_padded, first_row, key_count, 0).reshape(key_count, HEADS, HEAD_DIM)
        query_ids = lax.dynamic_slice_in_dim(clip_ids, first_row, TOK_DEV, 0)
        key_ids = lax.dynamic_slice_in_dim(ids_padded, first_row, key_count, 0)
        allowed = in_band & (query_ids[:, None] == key_ids[None, :])
        content = jnp.einsum('ihd,jhd->hij', query_block, key_block, precision=lax.Precision.HIGHEST)
        positional = jnp.einsum('ihd,rd->hir', query_block, relative, precision=lax.Precision.HIGHEST)
        scores = low_back((content + skew_band(positional, key_count)) * HEAD_DIM ** (-0.5))
        masked = jnp.where(allowed[None], scores, -1e+30)
        highest = lax.optimization_barrier(jnp.max(masked, axis=-1, keepdims=True))
        expanded = jnp.exp(masked - highest)
        weights = expanded / lax.optimization_barrier(jnp.sum(expanded, axis=-1, keepdims=True))
        blended = jnp.einsum('hij,jhd->ihd', low(weights), value_block, precision=lax.Precision.HIGHEST)
        return blended.reshape(TOK_DEV, D)
    starts = jnp.arange(N_SEQ, dtype=jnp.int32) * TOK_DEV
    return lax.map(jax.checkpoint(block_out), starts).reshape(GROUP_TOK, D)

def depthwise(gated_glu, tap_weights, clip_ids):
    margin = KERNEL - 1
    padded = jnp.pad(gated_glu, ((margin, 0), (0, 0)))
    ids_padded = jnp.concatenate([jnp.full((margin,), -1, jnp.int32), clip_ids])
    summed = jnp.zeros(gated_glu.shape, jnp.float32)
    for tap_index in range(KERNEL):
        same_clip = ids_padded[tap_index:tap_index + GROUP_TOK] == clip_ids
        summed = summed + jnp.where(same_clip[:, None], padded[tap_index:tap_index + GROUP_TOK], 0.0) * tap_weights[tap_index]
    return summed

def conformer(values, weights, relative, clip_ids):
    weight_in, weight_down, weight_qkv, weight_out, conv_first, conv_taps, conv_second, gains, biases = weights

    def feed_forward(stream, which_net, norm_index):
        normed = low(layer_norm(stream, gains[norm_index], biases[norm_index]))
        hidden_pre = low_back(matmul(normed, weight_in[which_net]))
        branch = low_back(matmul(low(swish_act(hidden_pre)), weight_down[which_net]))
        return stream + 0.5 * branch
    after_ffn = feed_forward(values, 0, 0)
    normed = low(layer_norm(after_ffn, gains[1], biases[1]))
    projected = low(low_back(matmul(normed, weight_qkv)))
    attended = attend(projected[:, :D], projected[:, D:2 * D], projected[:, 2 * D:], relative, clip_ids)
    second = after_ffn + low_back(matmul(low(low_back(attended)), weight_out))
    normed = low(layer_norm(second, gains[2], biases[2]))
    spread = low_back(matmul(normed, conv_first))
    gated_glu = low(spread[:, :D] * jax.nn.sigmoid(spread[:, D:]))
    filtered = layer_norm(depthwise(gated_glu, conv_taps, clip_ids), gains[3], biases[3])
    after_conv = second + low_back(matmul(low(swish_act(filtered)), conv_second))
    fourth = feed_forward(after_conv, 1, 4)
    return layer_norm(fourth, gains[5], biases[5])

def reference(inputs, lengths, ffn_in, ffn_out, qkv_weight, out_weight, conv_in, conv_depth, conv_out, norm_gain, norm_bias, rel_key, cotangent):
    params = tuple((weight.astype(jnp.float32) for weight in (ffn_in, ffn_out, qkv_weight, out_weight, conv_in, conv_depth, conv_out, norm_gain, norm_bias, rel_key)))
    positions = jnp.arange(GROUP_TOK, dtype=jnp.int32)

    def one_group(totals, group_item):
        stream, clip_lengths, incoming = group_item
        clip_ends = jnp.cumsum(clip_lengths).astype(jnp.int32)
        clip_ids = lax.optimization_barrier(jnp.sum((positions[:, None] >= clip_ends[None, :]).astype(jnp.int32), axis=1)).astype(jnp.int32)

        def forward(start_values, weights):
            current = start_values
            for layer_index in range(LAYERS):
                current = conformer(current, tuple((weight[layer_index] for weight in weights[:9])), weights[9][layer_index], clip_ids)
            return current
        result, pullback = jax.vjp(forward, stream.astype(jnp.float32), params)
        grad_input, grad_params = pullback(incoming.astype(jnp.float32))
        totals = tuple((running + gradient for running, gradient in zip(totals, grad_params)))
        return (totals, (result.astype(jnp.bfloat16), grad_input))
    zero_grads = tuple((jnp.zeros(parameter.shape, jnp.float32) for parameter in params))
    totals, (outputs, input_grads) = lax.scan(one_group, zero_grads, (inputs, lengths, cotangent))
    return (outputs, input_grads, totals[0], totals[1], totals[2], totals[3], totals[4], totals[5], totals[6], totals[7], totals[8], totals[9])
```

```python
import jax
import jax.numpy as jnp
from jax import lax
from jax.sharding import PartitionSpec as P

HEAD_DIM = 64
KERNEL = 31
LEFT = 64
RIGHT = 8
BF = jnp.bfloat16
F32 = jnp.float32


class Place:
    def __init__(self):
        self.seq_size = lax.axis_size("seq")
        self.fsdp_size = lax.axis_size("fsdp")
        self.chips = self.fsdp_size // 2
        self.seq = lax.axis_index("seq")
        fsdp = lax.axis_index("fsdp")
        self.core = lax.rem(fsdp, 2)
        self.chip = lax.div(fsdp, 2)
        self.bits = self.chips.bit_length() - 1
        self.half = self.seq_size // 2

    def sibling(self, shard):
        return lax.ppermute(shard, "fsdp", [(i, i ^ 1) for i in range(self.fsdp_size)])

    def hop(self, shard, bit):
        return lax.ppermute(shard, "fsdp", [(i, i ^ (2 << bit)) for i in range(self.fsdp_size)])

    def along(self, shard, by):
        pairs = [(i, i + by) for i in range(self.seq_size) if 0 <= i + by < self.seq_size]
        return lax.ppermute(shard, "seq", pairs)

    def swap_seq(self, blocks):
        return lax.all_to_all(blocks, "seq", 0, 0, tiled=True)

    def bit(self, bit):
        return lax.rem(lax.div(self.chip, 1 << bit), 2)

    def both(self, mine):
        return jnp.stack([mine, self.sibling(mine)])

    def mine_of(self, partial):
        return partial[0] + self.sibling(partial[1].astype(BF)).astype(F32)

    def by_core(self, mine, other, axis):
        return jnp.where(
            self.core == 0,
            jnp.concatenate([mine, other], axis),
            jnp.concatenate([other, mine], axis),
        )

    def core_part(self, array, axis, which):
        size = array.shape[axis] // 2
        return lax.dynamic_slice_in_dim(array, which * size, size, axis)


def tie(array, *marks):
    ready = None
    for mark in marks:
        if mark is None:
            continue
        equal = mark == mark
        ready = equal if ready is None else jnp.logical_and(ready, equal)
    return array if ready is None else jnp.where(ready, array, jnp.zeros_like(array))


def tip(array):
    return array[(0,) * array.ndim]


def gather_plane(place, part, turn, marks):
    bits = place.bits
    current = part.reshape((part.shape[0],) + (1,) * bits + part.shape[1:])
    for step in range(bits):
        bit = (turn + step) % bits
        axis = bits - bit
        other = place.hop(current, bit)
        marks.append(tip(other))
        current = jnp.where(
            place.bit(bit) == 0,
            jnp.concatenate([current, other], axis),
            jnp.concatenate([other, current], axis),
        )
    return current.reshape((part.shape[0], place.chips) + part.shape[1:])


def scatter_plane(place, full, turn, marks):
    bits = place.bits
    current = full.reshape((full.shape[0],) + (2,) * bits + full.shape[2:])
    for step in range(bits):
        bit = (turn + step) % bits
        axis = bits - bit
        me = place.bit(bit)
        keep = lax.dynamic_slice_in_dim(current, me, 1, axis)
        sent = lax.dynamic_slice_in_dim(current, 1 - me, 1, axis)
        got = place.hop(sent, bit)
        marks.append(tip(got))
        current = (keep.astype(F32) + got.astype(F32)).astype(BF)
    return current.reshape((full.shape[0],) + full.shape[2:])


def wide_to_seq(wide, half):
    n = wide.shape[-1] // 2
    return jnp.stack([wide[..., :n], wide[..., n:]], 1).reshape((2 * half,) + wide.shape[1:-1] + (n,))


def seq_to_wide(narrow, half):
    pairs = narrow.reshape((half, 2) + narrow.shape[1:])
    return jnp.concatenate([pairs[:, 0], pairs[:, 1]], -1)


def layer_norm(values, gain_row, bias_row):
    centered = values - jnp.mean(values, axis=-1, keepdims=True)
    variance = jnp.mean(centered * centered, axis=-1, keepdims=True)
    inverse = lax.rsqrt(variance + 1e-05)
    normal_part = centered * inverse
    return (normal_part * gain_row + bias_row, (normal_part, inverse))


def norm_back(gradient, cached, gain_row):
    normal_part, inverse = cached
    scaled = gradient * gain_row
    inner = jnp.mean(scaled * normal_part, axis=-1, keepdims=True)
    input_grad = inverse * (scaled - jnp.mean(scaled, axis=-1, keepdims=True) - normal_part * inner)
    return (input_grad, jnp.sum(gradient * normal_part, axis=0), jnp.sum(gradient, axis=0))


def split_layer_norm(place, values, gain_row, bias_row):
    count = values.shape[-1]
    own_mean = jnp.mean(values, axis=-1, keepdims=True)
    own_square = jnp.sum((values - own_mean) ** 2, axis=-1, keepdims=True)
    stats = jnp.concatenate([own_mean, own_square], -1)
    others = place.sibling(stats)[::-1]
    mean = 0.5 * (own_mean + others[..., :1])
    square = own_square + others[..., 1:]
    square = square + count * ((own_mean - mean) ** 2 + (others[..., :1] - mean) ** 2)
    inverse = lax.rsqrt(square / (2 * count) + 1e-05)
    normal_part = (values - mean) * inverse
    return (normal_part * gain_row + bias_row, (normal_part, inverse))


def split_norm_back(place, gradient, cached, gain_row):
    normal_part, inverse = cached
    count = gradient.shape[-1]
    scaled = gradient * gain_row
    sums = jnp.concatenate(
        [
            jnp.sum(scaled, axis=-1, keepdims=True),
            jnp.sum(scaled * normal_part, axis=-1, keepdims=True),
        ],
        -1,
    )
    sums = (sums + place.sibling(sums)[::-1]) / (2 * count)
    input_grad = inverse * (scaled - sums[..., :1] - normal_part * sums[..., 1:])
    return (
        input_grad,
        jnp.sum(gradient * normal_part, axis=(0, 1)),
        jnp.sum(gradient, axis=(0, 1)),
    )


def swish_slope(values):
    sigmoid_val = jax.nn.sigmoid(values)
    return sigmoid_val * (1.0 + values * (1.0 - sigmoid_val))


def skew_band(rel_scores, key_count):
    head_count, row_count, band_width = rel_scores.shape
    padded = jnp.pad(rel_scores, ((0, 0), (0, 0), (0, key_count + 1 - band_width)))
    flattened = padded.reshape(head_count, row_count * (key_count + 1))[:, : row_count * key_count]
    return flattened.reshape(head_count, row_count, key_count)


def unskew_band(grads, band_width):
    head_count, row_count, key_count = grads.shape
    flattened = jnp.pad(grads.reshape(head_count, row_count * key_count), ((0, 0), (0, row_count)))
    return flattened.reshape(head_count, row_count, key_count + 1)[:, :, :band_width]


def dot(left, right, left_axis, right_axis):
    return lax.dot_general(
        left, right, (((left_axis,), (right_axis,)), ((), ())), preferred_element_type=F32
    )


def band_scores(query_heads, key_heads, relative, allowed):
    content = jnp.einsum("hid,hjd->hij", query_heads, key_heads, preferred_element_type=F32)
    positional = jnp.einsum("hid,rd->hir", query_heads, relative, preferred_element_type=F32)
    scores = (content + skew_band(positional, key_heads.shape[1])) * HEAD_DIM ** (-0.5)
    return jnp.where(allowed, scores, -1e30)


def local(
    inputs,
    lengths,
    ffn_in,
    ffn_out,
    qkv_weight,
    out_weight,
    conv_in,
    conv_depth,
    conv_out,
    norm_gain,
    norm_bias,
    rel_key,
    cotangent,
):
    place = Place()
    seq_size, chips, half = place.seq_size, place.chips, place.half
    core = place.core
    row_count, dim = inputs.shape[1:]
    hid = ffn_in.shape[3] // 2
    quarter = hid // 2
    width = dim // 2
    rows = 2 * ffn_in.shape[2]
    margin = KERNEL - 1
    key_count = row_count + LEFT + RIGHT
    scale = HEAD_DIM ** (-0.5)
    tap_first, tap_last = 12, 12 + KERNEL

    small = jnp.concatenate([norm_gain[0], norm_bias[0], conv_depth[0]], 0)
    small_count = small.shape[0]
    small = jnp.pad(small, ((0, 128 - small_count), (0, 0))).T
    out_rows = jnp.swapaxes(ffn_out[0], 1, 2)

    def halves(which):
        qkv3 = qkv_weight[0].reshape(-1, 3, dim)
        conv2 = conv_in[0].reshape(-1, 2, dim)
        pick = lambda array: place.core_part(array, array.ndim - 1, which)
        flat = lambda array: array.reshape(array.shape[0], -1)
        return [
            pick(ffn_in[0, 0]),
            pick(out_rows[0]),
            flat(pick(qkv3)),
            flat(pick(conv2)),
            pick(ffn_in[0, 1]),
            pick(out_rows[1]),
        ]

    sent_parts = halves(1 - core) + [out_weight[0], conv_out[0], small]
    kept_parts = halves(core) + [out_weight[0], conv_out[0], small]
    received = place.sibling(jnp.concatenate(sent_parts, 1))
    block_parts, start = [], 0
    for kept in kept_parts:
        stop = start + kept.shape[1]
        block_parts.append(place.by_core(kept, received[:, start:stop], 0))
        start = stop
    b_in0, b_down0, b_qkv, b_first, b_in1, b_down1, b_out, b_second, b_small = block_parts

    chunks = [
        ([b_in0[:, :quarter], b_small], [b_down0[:, :quarter]], ()),
        ([b_in0[:, quarter:]], [b_down0[:, quarter:]], ()),
        ([b_qkv], [b_first], (b_out, b_second)),
        ([b_in1[:, :quarter]], [b_down1[:, :quarter]], ()),
        ([b_in1[:, quarter:]], [b_down1[:, quarter:]], ()),
    ]
    gathered, z_mark, hop_marks = [], None, []
    for index, (left, right, wide) in enumerate(chunks):
        block = jnp.concatenate(list(left) + list(right) + list(wide), 1)
        waits = [z_mark]
        if index >= 2:
            waits += hop_marks[index - 2][0::place.bits]
        if index >= 3:
            waits += hop_marks[index - 3]
        block = tie(block, *waits)
        spread = place.swap_seq(jnp.broadcast_to(block[None], (seq_size,) + block.shape))
        z_mark = tip(spread)
        marks = []
        n_left = sum(part.shape[1] for part in left)
        n_right = sum(part.shape[1] for part in right)
        left_part, right_part = spread[..., :n_left], spread[..., n_left : n_left + n_right]
        if wide:
            chosen = lax.dynamic_slice_in_dim(spread[..., n_left + n_right :], core * half, half, 0)
            w0, w1 = chosen[..., :dim], chosen[..., dim:]
            left_part = jnp.concatenate([left_part, wide_to_seq(w0, half)], -1)
            right_part = jnp.concatenate([right_part, wide_to_seq(w1, half)], -1)
        left_full = gather_plane(place, left_part, 0, marks)
        right_full = gather_plane(place, right_part, 1, marks)
        hop_marks.append(marks)
        gathered.append((left_full, right_full))

    def as_rows(full):
        return full.reshape(-1, full.shape[-1])

    w_in = [[None, None], [None, None]]
    w_down = [[None, None], [None, None]]
    for net, base in ((0, 0), (1, 3)):
        for part in range(2):
            w_in[net][part] = as_rows(gathered[base + part][0][..., :quarter])
            w_down[net][part] = as_rows(gathered[base + part][1])
    small_all = as_rows(gathered[0][0][..., quarter:])[:, :small_count].T.astype(F32)
    n_qkv, n_first = b_qkv.shape[1], b_first.shape[1]
    w_qkv = as_rows(gathered[2][0][..., :n_qkv])
    w_out = as_rows(seq_to_wide(gathered[2][0][..., n_qkv:], half))
    w_first = as_rows(gathered[2][1][..., :n_first])
    w_second = as_rows(seq_to_wide(gathered[2][1][..., n_first:], half))
    gains, biases = small_all[:6], small_all[6:12]
    tap_values = place.core_part(small_all[tap_first:tap_last], 1, core)
    gain3 = place.core_part(gains[3], 0, core)
    bias3 = place.core_part(biases[3], 0, core)

    group_lengths = jnp.concatenate([lengths, place.sibling(lengths)], 0)
    clips = group_lengths.shape[1]
    order = jnp.arange(clips)
    clip_ends = jnp.sum(
        jnp.where(order[None, :, None] >= order[None, None, :], group_lengths[:, None, :], 0), axis=2
    )
    first_row = place.seq * row_count

    def clip_of(offset, count_rows):
        positions = first_row + offset + jnp.arange(count_rows, dtype=jnp.int32)
        inside = jnp.sum(
            (positions[None, :, None] >= clip_ends[:, None, :]).astype(jnp.int32), axis=2
        )
        return jnp.where(positions[None] < 0, -1, inside)

    own_ids = clip_of(0, row_count)
    key_ids = clip_of(-LEFT, key_count)
    conv_ids = clip_of(-margin, row_count + margin)
    offsets = jnp.arange(key_count)[None, :] - jnp.arange(row_count)[:, None]
    allowed = ((offsets >= 0) & (offsets <= LEFT + RIGHT))[None] & (
        own_ids[:, :, None] == key_ids[:, None, :]
    )
    heads = width // HEAD_DIM
    allowed = jnp.broadcast_to(allowed[:, None], (2, heads, row_count, key_count)).reshape(
        2 * heads, row_count, key_count
    )
    tap_masks = [
        (conv_ids[:, tap : tap + row_count] == own_ids)[:, :, None] for tap in range(KERNEL)
    ]

    def to_heads(array):
        count = array.shape[1]
        return (
            array.reshape(2, count, heads, HEAD_DIM)
            .transpose(0, 2, 1, 3)
            .reshape(2 * heads, count, HEAD_DIM)
        )

    def from_heads(array):
        count = array.shape[1]
        return (
            array.reshape(2, heads, count, HEAD_DIM)
            .transpose(0, 2, 1, 3)
            .reshape(2, count, heads * HEAD_DIM)
        )

    def flat2(array):
        return array.reshape(2 * row_count, -1)

    def pair2(array):
        return array.reshape(2, row_count, -1)

    def feed_forward(values, net, norm_index):
        normed, norm_cache = layer_norm(values, gains[norm_index], biases[norm_index])
        normed_low = flat2(place.both(normed.astype(BF)))
        pres, acts, branch = [], [], 0.0
        for part in range(2):
            pre_act = dot(normed_low, w_in[net][part], 1, 0)
            act_low = (pre_act * jax.nn.sigmoid(pre_act)).astype(BF)
            branch = branch + dot(act_low, w_down[net][part], 1, 1)
            pres.append(pre_act)
            acts.append(act_low)
        total = place.mine_of(pair2(branch))
        return (values + 0.5 * total, (norm_cache, normed_low, pres, acts))

    stream = inputs[0].astype(F32)
    after_ffn, ffn_first = feed_forward(stream, 0, 0)
    normed, attn_norm = layer_norm(after_ffn, gains[1], biases[1])
    attn_input = flat2(place.both(normed.astype(BF)))
    projected = pair2(dot(attn_input, w_qkv, 1, 0).astype(BF))
    key_values = projected[..., width:]
    from_left = place.along(key_values[:, row_count - LEFT :], 1)
    from_right = place.along(key_values[:, :RIGHT], -1)
    window_kv = jnp.concatenate([from_left, key_values, from_right], axis=1)
    query_heads = to_heads(projected[..., :width])
    key_heads = to_heads(window_kv[..., :width])
    value_heads = to_heads(window_kv[..., width:])
    relative = rel_key[0]
    masked = band_scores(query_heads, key_heads, relative, allowed)
    highest = jnp.max(masked, axis=-1, keepdims=True)
    expanded = jnp.exp(masked - highest)
    summed = jnp.sum(expanded, axis=-1, keepdims=True)
    log_total = highest + jnp.log(summed)
    probs_low = (expanded / summed).astype(BF)
    attended = from_heads(
        jnp.einsum("hij,hjd->hid", probs_low, value_heads, preferred_element_type=F32).astype(BF)
    )
    attended = flat2(attended)
    after_attn = after_ffn + place.mine_of(pair2(dot(attended, w_out, 1, 0)))
    normed, conv_norm = layer_norm(after_attn, gains[2], biases[2])
    conv_input = flat2(place.both(normed.astype(BF)))
    spread_pre = pair2(dot(conv_input, w_first, 1, 0))
    value_part, gate_sig = spread_pre[..., :width], jax.nn.sigmoid(spread_pre[..., width:])
    gated_low = (value_part * gate_sig).astype(BF)
    from_prev = place.along(gated_low[:, row_count - margin :], 1)
    extended = jnp.concatenate([from_prev, gated_low], axis=1)
    filtered = jnp.zeros((2, row_count, width), F32)
    for tap in range(KERNEL):
        filtered = (
            filtered
            + jnp.where(tap_masks[tap], extended[:, tap : tap + row_count], 0) * tap_values[tap]
        )
    normed_conv, depth_norm = split_layer_norm(place, filtered, gain3, bias3)
    swished = (normed_conv * jax.nn.sigmoid(normed_conv)).astype(BF)
    after_conv = after_attn + place.mine_of(pair2(dot(flat2(swished), w_second, 1, 0)))
    fourth, ffn_second = feed_forward(after_conv, 1, 4)
    result, final_norm = layer_norm(fourth, gains[5], biases[5])
    outputs = result.astype(BF)[None]

    reduced, first_mark, second_marks = [], None, []

    def blocks_of(array):
        return array.reshape(seq_size, chips, rows, array.shape[1])

    def wide_blocks_of(array):
        return wide_to_seq(array.reshape(half, chips, rows, array.shape[1]), half)

    def scatter(left, right, wide_left, wide_right):
        nonlocal first_mark
        index = len(second_marks)
        outs, marks = [], []
        for turn, (plain, wide) in enumerate(((left, wide_left), (right, wide_right))):
            parts = [blocks_of(array) for array in plain] + [wide_blocks_of(array) for array in wide]
            full = jnp.concatenate(parts, -1) if len(parts) > 1 else parts[0]
            full = tie(full, first_mark, second_marks[index - 2] if index >= 2 else None)
            outs.append(scatter_plane(place, full, turn, marks))
        first_mark = marks[0]
        second_marks.append(marks[place.bits - 1])
        to_swap, splits = [], []
        for part, plain, wide in ((outs[0], left, wide_left), (outs[1], right, wide_right)):
            n_plain = sum(array.shape[1] for array in plain)
            if n_plain:
                to_swap.append(part[..., :n_plain])
                splits += [array.shape[1] for array in plain]
            if wide:
                chosen = seq_to_wide(part[..., n_plain:], half)
                placed = jnp.zeros((seq_size,) + chosen.shape[1:], BF)
                to_swap.append(lax.dynamic_update_slice_in_dim(placed, chosen, core * half, 0))
                splits += [array.shape[1] for array in wide]
        swapped = place.swap_seq(jnp.concatenate(to_swap, -1))
        total = jnp.sum(swapped.astype(F32), 0)
        results, start = [], 0
        for n in splits:
            results.append(total[:, start : start + n])
            start += n
        return results

    grad_stream = cotangent[0].astype(F32)
    gain_grads = [None] * 6
    bias_grads = [None] * 6

    def feed_back(gradient, net, norm_index, cached):
        norm_cache, normed_low, pres, acts = cached
        branch_grad = flat2(place.both((0.5 * gradient).astype(BF)))
        downs, ins, normed_grad = [], [], 0.0
        for part in range(2):
            downs.append(dot(branch_grad, acts[part], 0, 0).astype(BF))
        pre_grads = []
        for part in range(2):
            act_grad = dot(branch_grad, w_down[net][part], 1, 0)
            pre_grads.append((act_grad * swish_slope(pres[part])).astype(BF))
        for part in range(2):
            normed_grad = normed_grad + dot(pre_grads[part], w_in[net][part], 1, 1)
        for part in range(2):
            ins.append(dot(normed_low, pre_grads[part], 0, 0).astype(BF))
        normed_grad = place.mine_of(pair2(normed_grad))
        input_grad, gain_grad, bias_grad = norm_back(normed_grad, norm_cache, gains[norm_index])
        reduced_down = scatter([downs[0]], [downs[1]], [], [])
        reduced_in = scatter([ins[0]], [ins[1]], [], [])
        return (
            gradient + input_grad,
            jnp.concatenate(reduced_in, 1),
            jnp.concatenate(reduced_down, 1),
            gain_grad,
            bias_grad,
        )

    grad_fourth, gain_grads[5], bias_grads[5] = norm_back(grad_stream, final_norm, gains[5])
    grad_conv_out, in_second, down_second, gain_grads[4], bias_grads[4] = feed_back(
        grad_fourth, 1, 4, ffn_second
    )
    branch_grad = flat2(place.both(grad_conv_out.astype(BF)))
    second_grad = dot(flat2(swished), branch_grad, 0, 0).astype(BF)
    swish_grad = pair2(dot(branch_grad, w_second, 1, 1))
    filter_grad, gain3_grad, bias3_grad = split_norm_back(
        place, swish_grad * swish_slope(normed_conv), depth_norm, gain3
    )
    tap_grads = []
    extended_grad = jnp.zeros((2, row_count + margin, width), F32)
    for tap in range(KERNEL):
        masked_grad = jnp.where(tap_masks[tap], filter_grad, 0.0)
        tap_grads.append(
            jnp.sum(masked_grad * extended[:, tap : tap + row_count], axis=(0, 1))
        )
        extended_grad = extended_grad + jnp.pad(
            masked_grad * tap_values[tap], ((0, 0), (tap, margin - tap), (0, 0))
        )
    to_prev = place.along(extended_grad[:, :margin].astype(BF), -1).astype(F32)
    gated_grad = extended_grad[:, margin:] + jnp.pad(
        to_prev, ((0, 0), (row_count - margin, 0), (0, 0))
    )
    spread_grad = flat2(
        jnp.concatenate(
            [gated_grad * gate_sig, gated_grad * value_part * gate_sig * (1.0 - gate_sig)], axis=2
        ).astype(BF)
    )
    first_grad = dot(conv_input, spread_grad, 0, 0).astype(BF)
    normed_grad = place.mine_of(pair2(dot(spread_grad, w_first, 1, 1)))
    input_grad, gain_grads[2], bias_grads[2] = norm_back(normed_grad, conv_norm, gains[2])
    first_sum, second_sum = scatter([first_grad], [], [], [second_grad])
    grad_attn_out = grad_conv_out + input_grad
    branch_grad = flat2(place.both(grad_attn_out.astype(BF)))
    out_grad = dot(attended, branch_grad, 0, 0).astype(BF)
    attended_grad = to_heads(pair2(dot(branch_grad, w_out, 1, 1).astype(BF)))
    probs = jnp.exp(band_scores(query_heads, key_heads, relative, allowed) - log_total)
    backward_probs_low = probs.astype(BF)
    prob_grads = jnp.einsum("hid,hjd->hij", attended_grad, value_heads, preferred_element_type=F32)
    score_grads = (
        probs * (prob_grads - jnp.sum(prob_grads * probs, axis=-1, keepdims=True))
    ).astype(BF)
    band_grads = unskew_band(score_grads, LEFT + RIGHT + 1)
    query_grad = (
        jnp.einsum("hij,hjd->hid", score_grads, key_heads, preferred_element_type=F32)
        + jnp.einsum("hir,rd->hid", band_grads, relative, preferred_element_type=F32)
    ) * scale
    relative_grad = (
        jnp.einsum("hir,hid->rd", band_grads, query_heads, preferred_element_type=F32) * scale
    )
    key_grad = (
        jnp.einsum("hij,hid->hjd", score_grads, query_heads, preferred_element_type=F32) * scale
    )
    value_grad = jnp.einsum(
        "hij,hid->hjd", backward_probs_low, attended_grad, preferred_element_type=F32
    )
    window_grad = jnp.concatenate([from_heads(key_grad), from_heads(value_grad)], axis=2)
    to_left = place.along(window_grad[:, :LEFT].astype(BF), -1).astype(F32)
    to_right = place.along(window_grad[:, LEFT + row_count :].astype(BF), 1).astype(F32)
    own_grad = (
        window_grad[:, LEFT : LEFT + row_count]
        + jnp.pad(to_left, ((0, 0), (row_count - LEFT, 0), (0, 0)))
        + jnp.pad(to_right, ((0, 0), (0, row_count - RIGHT), (0, 0)))
    )
    projected_grad = flat2(jnp.concatenate([from_heads(query_grad), own_grad], axis=2).astype(BF))
    qkv_grad = dot(attn_input, projected_grad, 0, 0).astype(BF)
    normed_grad = place.mine_of(pair2(dot(projected_grad, w_qkv, 1, 1)))
    input_grad, gain_grads[1], bias_grads[1] = norm_back(normed_grad, attn_norm, gains[1])
    qkv_a, qkv_b, out_sum = scatter(
        [qkv_grad[:, : 2 * width]], [qkv_grad[:, 2 * width :]], [], [out_grad]
    )
    grad_ffn_out = grad_attn_out + input_grad
    grad_input, in_first, down_first, gain_grads[0], bias_grads[0] = feed_back(
        grad_ffn_out, 0, 0, ffn_first
    )

    def spread_core(half_rows):
        return place.by_core(half_rows, jnp.zeros_like(half_rows), 1)

    gain_grads[3] = spread_core(gain3_grad[None])[0]
    bias_grads[3] = spread_core(bias3_grad[None])[0]
    small_grads = jnp.concatenate(
        [jnp.stack(gain_grads), jnp.stack(bias_grads), spread_core(jnp.stack(tap_grads))], 0
    )
    small_grads = jnp.pad(small_grads, ((0, 128 - small_count), (0, 0))).T
    small_full = small_grads.reshape((seq_size,) + (2,) * place.bits + (rows, 128))
    for bit in range(place.bits):
        axis = place.bits - bit
        me = place.bit(bit)
        keep = lax.dynamic_slice_in_dim(small_full, me, 1, axis)
        sent = lax.dynamic_slice_in_dim(small_full, 1 - me, 1, axis)
        small_full = keep + place.hop(sent, bit)
    small_total = jnp.sum(place.swap_seq(small_full.reshape(seq_size, rows, 128)), 0)
    small_sum = place.core_part(small_total, 0, core) + place.sibling(
        place.core_part(small_total, 0, 1 - core)
    )
    small_sum = small_sum[:, :small_count].T

    rel_total = relative_grad + place.sibling(relative_grad)
    for bit in range(place.bits):
        rel_total = rel_total + place.hop(rel_total, bit)
    rel_total = jnp.sum(
        place.swap_seq(jnp.broadcast_to(rel_total[None], (seq_size,) + rel_total.shape)), 0
    )

    def own_rows(total):
        other = place.sibling(place.core_part(total, 0, 1 - core))
        return place.core_part(total, 0, core), other

    def join(total, count):
        mine, other = own_rows(total)
        n = mine.shape[1] // count
        mine = mine.reshape(-1, count, n)
        other = other.reshape(-1, count, n)
        return place.by_core(mine, other, 2).reshape(mine.shape[0], -1)

    def owner_rows(total):
        mine, other = own_rows(total)
        return jnp.where(lax.div(place.seq, half) == core, mine, other)

    ffn_in_grad = jnp.stack([join(in_first, 1), join(in_second, 1)])
    ffn_out_grad = jnp.swapaxes(jnp.stack([join(down_first, 1), join(down_second, 1)]), 1, 2)
    return (
        outputs,
        grad_input[None],
        ffn_in_grad[None],
        ffn_out_grad[None],
        join(jnp.concatenate([qkv_a, qkv_b], 1), 3)[None],
        owner_rows(out_sum)[None],
        join(first_sum, 2)[None],
        small_sum[None, tap_first:tap_last],
        owner_rows(second_sum)[None],
        small_sum[None, :6],
        small_sum[None, 6:12],
        rel_total[None],
    )


def solution(mesh):
    spread = ("seq", "fsdp")
    split_rows = P(None, spread, None)
    split_last = P(None, None, spread)
    placed = (
        P("fsdp", "seq", None),
        P("fsdp", None),
        P(None, None, spread, None),
        P(None, None, None, spread),
        split_rows,
        split_rows,
        split_rows,
        split_last,
        split_rows,
        split_last,
        split_last,
        P(),
        P("fsdp", "seq", None),
    )
    return jax.shard_map(
        local,
        mesh=mesh,
        in_specs=placed,
        out_specs=(
            P("fsdp", "seq", None),
            P("fsdp", "seq", None),
            P(None, None, spread, None),
            P(None, None, None, spread),
            split_rows,
            split_rows,
            split_rows,
            split_last,
            split_rows,
            split_last,
            split_last,
            P(),
        ),
        check_vma=False,
    )
```

```python
import functools

import jax
import jax.numpy as jnp
from jax import lax
from jax.experimental import pallas as pl
from jax.experimental.layout import Layout, with_layout_constraint
from jax.experimental.pallas import tpu as pltpu
from jax.sharding import Mesh
from jax.sharding import PartitionSpec as P

HEAD_DIM = 64
KERNEL = 31
LEFT = 64
RIGHT = 8
BLOCK = 128
SPAN = 256
EDGE = 32
BF = jnp.bfloat16
F32 = jnp.float32


class Place:
    def __init__(self):
        self.seq_size = lax.axis_size("seq")
        self.chips = lax.axis_size("plane")
        self.seq = lax.axis_index("seq")
        self.chip = lax.axis_index("plane")
        self.core = lax.axis_index("core")
        self.bits = self.chips.bit_length() - 1

    def sibling(self, shard):
        return lax.ppermute(shard, "core", [(0, 1), (1, 0)])

    def hop(self, shard, bit):
        return lax.ppermute(shard, "plane", [(i, i ^ (1 << bit)) for i in range(self.chips)])

    def along(self, shard, by):
        pairs = [(i, i + by) for i in range(self.seq_size) if 0 <= i + by < self.seq_size]
        return lax.ppermute(shard, "seq", pairs)

    def swap_seq(self, blocks):
        return lax.all_to_all(blocks, "seq", 0, 0, tiled=True)

    def bit(self, bit):
        return lax.rem(lax.div(self.chip, 1 << bit), 2)

    def both(self, mine):
        return jnp.stack([mine, self.sibling(mine)])

    def from_sibling(self, partial):
        return self.sibling(partial[1].astype(BF))

    def by_core(self, mine, other, axis):
        return jnp.where(
            self.core == 0,
            jnp.concatenate([mine, other], axis),
            jnp.concatenate([other, mine], axis),
        )

    def core_part(self, array, axis, which):
        size = array.shape[axis] // 2
        return lax.dynamic_slice_in_dim(array, which * size, size, axis)


def tie(array, *marks):
    ready = None
    for mark in marks:
        if mark is None:
            continue
        equal = mark == mark
        ready = equal if ready is None else jnp.logical_and(ready, equal)
    return array if ready is None else jnp.where(ready, array, jnp.zeros_like(array))


def tip(array):
    return array[(0,) * array.ndim]


def gather_plane(place, part, turn, marks):
    bits = place.bits
    current = part.reshape((part.shape[0],) + (1,) * bits + part.shape[1:])
    for step in range(bits):
        bit = (turn + step) % bits
        axis = bits - bit
        other = place.hop(current, bit)
        marks.append(tip(other))
        current = jnp.where(
            place.bit(bit) == 0,
            jnp.concatenate([current, other], axis),
            jnp.concatenate([other, current], axis),
        )
    return current.reshape((part.shape[0], place.chips) + part.shape[1:])


def scatter_plane(place, full, turn, marks):
    bits = place.bits
    current = full.reshape((full.shape[0],) + (2,) * bits + full.shape[2:])
    for step in range(bits):
        bit = (turn + step) % bits
        axis = bits - bit
        me = place.bit(bit)
        keep = lax.dynamic_slice_in_dim(current, me, 1, axis)
        sent = lax.dynamic_slice_in_dim(current, 1 - me, 1, axis)
        got = place.hop(sent, bit)
        marks.append(tip(got))
        current = (keep.astype(F32) + got.astype(F32)).astype(full.dtype)
    return current.reshape((full.shape[0],) + full.shape[2:])


def clip_index(positions, ends_ref, group, clips):
    inside = jnp.zeros(positions.shape, jnp.int32)
    for clip in range(clips):
        inside = inside + (positions >= ends_ref[group, clip]).astype(jnp.int32)
    return jnp.where(positions < 0, -1, inside)


def dot_nt(left, right):
    return lax.dot_general(left, right, (((1,), (1,)), ((), ())), preferred_element_type=F32)


def dot_nn(left, right):
    return lax.dot_general(left, right, (((1,), (0,)), ((), ())), preferred_element_type=F32)


def dot_tn(left, right):
    return lax.dot_general(left, right, (((0,), (0,)), ((), ())), preferred_element_type=F32)


def band_mask(ends_ref, base_ref, block, clips):
    group = pl.program_id(0)
    start = base_ref[0] + block * BLOCK
    query_at = start + lax.broadcasted_iota(jnp.int32, (BLOCK, 1), 0)
    key_at = start - LEFT + lax.broadcasted_iota(jnp.int32, (1, SPAN), 1)
    apart = lax.broadcasted_iota(jnp.int32, (BLOCK, SPAN), 1) - lax.broadcasted_iota(
        jnp.int32, (BLOCK, SPAN), 0
    )
    query_ids = clip_index(query_at, ends_ref, group, clips)
    key_ids = clip_index(key_at, ends_ref, group, clips)
    return (apart >= 0) & (apart <= LEFT + RIGHT) & (query_ids == key_ids)


def fill_window(window, left_ref, own_ref, right_ref):
    count = own_ref.shape[1]
    window[0:LEFT] = left_ref[0]
    window[LEFT : LEFT + count] = own_ref[0]
    window[LEFT + count :] = right_ref[0]


def band_probs(query, keys, relative, mask):
    scores = dot_nt(query, keys)
    positional = pltpu.roll(dot_nt(query, relative), 0, 1, stride=1, stride_axis=0)
    scores = jnp.where(mask, (scores + positional) * HEAD_DIM ** (-0.5), -1e30)
    expanded = jnp.exp(scores - jnp.max(scores, axis=1, keepdims=True))
    return expanded / jnp.sum(expanded, axis=1, keepdims=True)


def attend_kernel(
    clips, ends_ref, base_ref, q_ref, k_ref, v_ref, kl_ref, vl_ref, kr_ref, vr_ref, rel_ref,
    out_ref, probs_ref, keys, values,
):
    fill_window(keys, kl_ref, k_ref, kr_ref)
    fill_window(values, vl_ref, v_ref, vr_ref)
    low_lane = lax.broadcasted_iota(jnp.int32, (BLOCK, 2 * HEAD_DIM), 1) < HEAD_DIM
    for block in range(q_ref.shape[1] // BLOCK):
        at = block * BLOCK
        mask = band_mask(ends_ref, base_ref, block, clips)
        query = q_ref[0, at : at + BLOCK]
        zero = jnp.zeros_like(query)
        outs = []
        queries = jnp.where(low_lane, query, zero), jnp.where(low_lane, zero, query)
        for one, query_one in enumerate(queries):
            probs = band_probs(query_one, keys[at : at + SPAN], rel_ref[...], mask).astype(BF)
            probs_ref[0, 0, block, one] = probs
            outs.append(dot_nn(probs, values[at : at + SPAN]))
        out_ref[0, at : at + BLOCK] = jnp.where(low_lane, outs[0], outs[1]).astype(BF)


def attend_back_kernel(
    q_ref, k_ref, v_ref, kl_ref, vl_ref, kr_ref, vr_ref, rel_ref, do_ref, probs_ref,
    dq_ref, dk_ref, dv_ref, dkl_ref, dvl_ref, dkr_ref, dvr_ref, drel_ref,
    keys, values, key_sum, value_sum,
):
    scale = HEAD_DIM ** (-0.5)
    count = q_ref.shape[1]
    fill_window(keys, kl_ref, k_ref, kr_ref)
    fill_window(values, vl_ref, v_ref, vr_ref)
    key_sum[...] = jnp.zeros_like(key_sum)
    value_sum[...] = jnp.zeros_like(value_sum)

    @pl.when((pl.program_id(0) == 0) & (pl.program_id(1) == 0))
    def _():
        drel_ref[...] = jnp.zeros_like(drel_ref)

    low_lane = lax.broadcasted_iota(jnp.int32, (BLOCK, 2 * HEAD_DIM), 1) < HEAD_DIM
    row = lax.broadcasted_iota(jnp.int32, (BLOCK, BLOCK), 0)
    column = lax.broadcasted_iota(jnp.int32, (BLOCK, BLOCK), 1)
    flip = (row + column == BLOCK - 1).astype(F32).astype(BF)
    for block in range(count // BLOCK):
        at = block * BLOCK
        query = q_ref[0, at : at + BLOCK]
        grad = do_ref[0, at : at + BLOCK]
        zero = jnp.zeros_like(query)
        some_keys = keys[at : at + SPAN]
        outs, key_part, value_part, rel_part = [], None, None, None
        for low in (True, False):
            pick = (lambda a: jnp.where(low_lane, a, zero)) if low else (
                lambda a: jnp.where(low_lane, zero, a)
            )
            query_one, grad_one = pick(query), pick(grad)
            probs_low = probs_ref[0, 0, block, 0 if low else 1]
            probs = probs_low.astype(F32)
            prob_grads = dot_nt(grad_one, values[at : at + SPAN])
            inner = jnp.sum(prob_grads * probs, axis=1, keepdims=True)
            score_grads = (probs * (prob_grads - inner)).astype(BF)
            turned = pltpu.roll(
                dot_nn(flip, score_grads), SPAN - BLOCK + 1, 1, stride=1, stride_axis=0
            )
            by_offset = dot_nn(flip, turned[:, :BLOCK].astype(BF)).astype(BF)
            outs.append(dot_nn(score_grads, some_keys) + dot_nn(by_offset, rel_ref[0:BLOCK]))
            parts = (
                dot_tn(score_grads, query_one),
                dot_tn(probs_low, grad_one),
                dot_tn(by_offset, query_one),
            )
            if low:
                key_part, value_part, rel_part = parts
            else:
                key_part, value_part, rel_part = (
                    key_part + parts[0],
                    value_part + parts[1],
                    rel_part + parts[2],
                )
        dq_ref[0, at : at + BLOCK] = (jnp.where(low_lane, outs[0], outs[1]) * scale).astype(BF)
        key_sum[at : at + SPAN] += key_part * scale
        value_sum[at : at + SPAN] += value_part
        drel_ref[...] += rel_part * scale
    for total, left, own, right in (
        (key_sum, dkl_ref, dk_ref, dkr_ref),
        (value_sum, dvl_ref, dv_ref, dvr_ref),
    ):
        left[0] = total[0:LEFT].astype(BF)
        own[0] = total[LEFT : LEFT + count]
        right[0] = total[LEFT + count :].astype(BF)


def attend_specs(groups, count, pairs):
    lanes = 2 * HEAD_DIM
    smem = pl.BlockSpec(memory_space=pltpu.SMEM)

    def own(at):
        return pl.BlockSpec((1, count, lanes), lambda g, h: (g, 0, at * pairs + h))

    def edge(at):
        return pl.BlockSpec((1, LEFT, lanes), lambda g, h: (g, 0, at * pairs + h))

    rel = pl.BlockSpec((SPAN, lanes), lambda g, h: (0, 0))
    probs = pl.BlockSpec(
        (1, 1, count // BLOCK, 2, BLOCK, SPAN), lambda g, h: (g, h, 0, 0, 0, 0)
    )
    specs = [smem, smem, own(0), own(1), own(2), edge(0), edge(1), edge(0), edge(1), rel]
    return specs, own, edge, probs


def attend(ends, base, projected, left, right, relative):
    groups, count, _ = projected.shape
    pairs = projected.shape[2] // (6 * HEAD_DIM)
    specs, own, _, probs = attend_specs(groups, count, pairs)
    window = pltpu.VMEM((count + 2 * LEFT, 2 * HEAD_DIM), BF)
    return pl.pallas_call(
        functools.partial(attend_kernel, ends.shape[1]),
        grid=(groups, pairs),
        in_specs=specs,
        out_specs=[own(0), probs],
        out_shape=[
            jax.ShapeDtypeStruct((groups, count, projected.shape[2] // 3), BF),
            jax.ShapeDtypeStruct((groups, pairs, count // BLOCK, 2, BLOCK, SPAN), BF),
        ],
        scratch_shapes=[window, window],
        name="attend",
    )(ends, base, projected, projected, projected, left, left, right, right, relative)


def attend_back(projected, left, right, relative, grad, probs):
    groups, count, _ = projected.shape
    width = projected.shape[2] // 3
    pairs = width // (2 * HEAD_DIM)
    specs, own, edge, saved = attend_specs(groups, count, pairs)
    window = pltpu.VMEM((count + 2 * LEFT, 2 * HEAD_DIM), BF)
    total = pltpu.VMEM((count + 2 * LEFT, 2 * HEAD_DIM), F32)
    rel_sum = pl.BlockSpec((BLOCK, 2 * HEAD_DIM), lambda g, h: (0, 0))
    shape = lambda rows, dtype: jax.ShapeDtypeStruct((groups, rows, width), dtype)
    return pl.pallas_call(
        attend_back_kernel,
        grid=(groups, pairs),
        in_specs=specs[2:] + [own(0), saved],
        out_specs=[own(0), own(0), own(0), edge(0), edge(0), edge(0), edge(0), rel_sum],
        out_shape=[
            shape(count, BF),
            shape(count, F32),
            shape(count, F32),
            shape(LEFT, BF),
            shape(LEFT, BF),
            shape(LEFT, BF),
            shape(LEFT, BF),
            jax.ShapeDtypeStruct((BLOCK, 2 * HEAD_DIM), F32),
        ],
        scratch_shapes=[window, window, total, total],
        name="attend_back",
    )(projected, projected, projected, left, left, right, right, relative, grad, probs)


def products_kernel(steps, first_ref, second_ref, *refs):
    right_refs, out_ref, turned = refs[:-2], refs[-2], refs[-1]
    at = pl.program_id(0)

    @pl.when(at == 0)
    def _():
        turned[...] = first_ref[...].T

    @pl.when(at == 2 * steps)
    def _():
        turned[...] = second_ref[...].T

    for number, right_ref in enumerate(right_refs):

        @pl.when((at >= number * steps) & (at < (number + 1) * steps))
        def _(right_ref=right_ref):
            out_ref[...] = dot_nn(turned[...], right_ref[...]).astype(BF)


def products(first, second, rights):
    count, dim = first.shape
    step = 512
    steps = rights[0].shape[1] // step
    whole = pl.BlockSpec((count, dim), lambda i: (0, 0))

    def part(number):
        return pl.BlockSpec(
            (count, step), lambda i: (0, jnp.clip(i - number * steps, 0, steps - 1))
        )

    return pl.pallas_call(
        functools.partial(products_kernel, steps),
        grid=(4 * steps,),
        in_specs=[whole, whole] + [part(number) for number in range(4)],
        out_specs=pl.BlockSpec((dim, step), lambda i: (0, i)),
        out_shape=jax.ShapeDtypeStruct((dim, 4 * steps * step), BF),
        scratch_shapes=[pltpu.VMEM((dim, count), BF)],
        name="products",
    )(first, second, *rights)


def norm_parts(values):
    centered = values - jnp.mean(values, axis=1, keepdims=True)
    variance = jnp.mean(centered * centered, axis=1, keepdims=True)
    inverse = lax.rsqrt(variance + 1e-05)
    return centered * inverse, inverse


def norm_kernel(share, *refs):
    if share:
        base_ref, own_ref, other_ref, gain_ref, bias_ref, stream_ref, low_ref = refs
        stream = base_ref[...] + share * (own_ref[0] + other_ref[...].astype(F32))
        stream_ref[...] = stream
    else:
        base_ref, gain_ref, bias_ref, low_ref = refs
        stream = base_ref[...]
    normal_part, _ = norm_parts(stream)
    low_ref[...] = (normal_part * gain_ref[...] + bias_ref[...]).astype(BF)


def norm_back_kernel(share, scale, *refs):
    if share:
        stream_ref, own_ref, other_ref, gain_ref, through_ref, grad_ref, low_ref = refs[:7]
        gradient = own_ref[0] + other_ref[...].astype(F32)
    else:
        stream_ref, own_ref, gain_ref, grad_ref, low_ref = refs[:5]
        gradient = own_ref[...].astype(F32)
    gain_grad_ref, bias_grad_ref = refs[-2:]
    normal_part, inverse = norm_parts(stream_ref[...])
    scaled = gradient * gain_ref[...]
    inner = jnp.mean(scaled * normal_part, axis=1, keepdims=True)
    total = inverse * (scaled - jnp.mean(scaled, axis=1, keepdims=True) - normal_part * inner)
    if share:
        total = total + through_ref[...]
    grad_ref[...] = total
    low_ref[...] = (scale * total).astype(BF)

    @pl.when(pl.program_id(0) == 0)
    def _():
        gain_grad_ref[...] = jnp.zeros_like(gain_grad_ref)
        bias_grad_ref[...] = jnp.zeros_like(bias_grad_ref)

    gain_grad_ref[...] += jnp.sum(gradient * normal_part, axis=0, keepdims=True)
    bias_grad_ref[...] += jnp.sum(gradient, axis=0, keepdims=True)


def row_specs(dim):
    step = 64
    rows = pl.BlockSpec((step, dim), lambda i: (i, 0))
    first = pl.BlockSpec((1, step, dim), lambda i: (0, i, 0))
    line = pl.BlockSpec((1, dim), lambda i: (0, 0))
    return step, rows, first, line


def add_and_norm(base, share, own, other, gain, bias):
    count, dim = base.shape
    step, rows, first, line = row_specs(dim)
    low = jax.ShapeDtypeStruct((count, dim), BF)
    if not share:
        return pl.pallas_call(
            functools.partial(norm_kernel, share),
            grid=(count // step,),
            in_specs=[rows, line, line],
            out_specs=rows,
            out_shape=low,
            name="norm",
        )(base, gain, bias)
    return pl.pallas_call(
        functools.partial(norm_kernel, share),
        grid=(count // step,),
        in_specs=[rows, first, rows, line, line],
        out_specs=[rows, rows],
        out_shape=[jax.ShapeDtypeStruct((count, dim), F32), low],
        name="add_and_norm",
    )(base, own, other, gain, bias)


def norm_and_add_back(stream, own, other, gain, through, scale):
    count, dim = stream.shape
    step, rows, first, line = row_specs(dim)
    share = through is not None
    specs = [rows, first, rows, line, rows] if share else [rows, rows, line]
    args = (stream, own, other, gain, through) if share else (stream, own, gain)
    return pl.pallas_call(
        functools.partial(norm_back_kernel, share, scale),
        grid=(count // step,),
        in_specs=specs,
        out_specs=[rows, rows, line, line],
        out_shape=[
            jax.ShapeDtypeStruct((count, dim), F32),
            jax.ShapeDtypeStruct((count, dim), BF),
            jax.ShapeDtypeStruct((1, dim), F32),
            jax.ShapeDtypeStruct((1, dim), F32),
        ],
        name="norm_back",
    )(*args)


def split_layer_norm(place, values, gain_row, bias_row):
    count = values.shape[-1]
    own_mean = jnp.mean(values, axis=-1, keepdims=True)
    own_square = jnp.sum((values - own_mean) ** 2, axis=-1, keepdims=True)
    stats = jnp.concatenate([own_mean, own_square], -1)
    others = place.sibling(stats)[::-1]
    mean = 0.5 * (own_mean + others[..., :1])
    square = own_square + others[..., 1:]
    square = square + count * ((own_mean - mean) ** 2 + (others[..., :1] - mean) ** 2)
    inverse = lax.rsqrt(square / (2 * count) + 1e-05)
    normal_part = (values - mean) * inverse
    return (normal_part * gain_row + bias_row, (normal_part, inverse))


def split_norm_sums(place, gradient, normal_part, gain_row):
    scaled = gradient * gain_row
    sums = jnp.concatenate(
        [
            jnp.sum(scaled, axis=-1, keepdims=True),
            jnp.sum(scaled * normal_part, axis=-1, keepdims=True),
        ],
        -1,
    )
    return (sums + place.sibling(sums)[::-1]) / (2 * gradient.shape[-1])


def swish_slope(values):
    sigmoid_val = jax.nn.sigmoid(values)
    return sigmoid_val * (1.0 + values * (1.0 - sigmoid_val))


def clip_bounds(positions, ends_ref, group, clips):
    start = jnp.zeros(positions.shape, jnp.int32)
    stop = jnp.full(positions.shape, 1 << 30, jnp.int32)
    for clip in range(clips):
        end = ends_ref[group, clip]
        start = jnp.maximum(start, jnp.where(positions >= end, end, 0))
        stop = jnp.minimum(stop, jnp.where(positions < end, end, 1 << 30))
    return start, jnp.where(positions < 0, positions, stop)


def taps_kernel(clips, ends_ref, base_ref, prev_ref, glu_ref, taps_ref, out_ref, window):
    count = glu_ref.shape[1]
    group = pl.program_id(0)
    window[0:EDGE] = prev_ref[0].astype(F32)
    window[EDGE:] = glu_ref[0].astype(F32)
    at = base_ref[0] + lax.broadcasted_iota(jnp.int32, (count, 1), 0)
    start, _ = clip_bounds(at, ends_ref, group, clips)
    age = jnp.broadcast_to(at - start, (count, 128))
    total = jnp.zeros((count, 128), F32)
    for tap in range(KERNEL):
        first = tap + EDGE - KERNEL + 1
        values = window[first : first + count] * taps_ref[tap : tap + 1]
        total = total + jnp.where(age >= KERNEL - 1 - tap, values, 0.0)
    out_ref[0] = total


def taps_back_kernel(
    clips, ends_ref, base_ref, prev_ref, glu_ref, taps_ref, grad_ref, normal_ref, inverse_ref, sums_ref,
    gain_ref, dglu_ref, dprev_ref, dtaps_ref, dgain_ref, dbias_ref, window, spread,
):
    count = glu_ref.shape[1]
    group = pl.program_id(1)

    @pl.when(group == 0)
    def _():
        dtaps_ref[...] = jnp.zeros_like(dtaps_ref)
        dgain_ref[...] = jnp.zeros_like(dgain_ref)
        dbias_ref[...] = jnp.zeros_like(dbias_ref)

    window[0:EDGE] = prev_ref[0].astype(F32)
    window[EDGE:] = glu_ref[0].astype(F32)
    grad, normal_part = grad_ref[0], normal_ref[0]
    dgain_ref[...] += jnp.sum(grad * normal_part, axis=0, keepdims=True)
    dbias_ref[...] += jnp.sum(grad, axis=0, keepdims=True)
    own = inverse_ref[0] * (
        grad * gain_ref[...] - sums_ref[0, :, 0:1] - normal_part * sums_ref[0, :, 1:2]
    )
    spread[0:EDGE] = jnp.zeros((EDGE, 128), F32)
    spread[EDGE : EDGE + count] = own
    spread[EDGE + count :] = jnp.zeros((EDGE, 128), F32)
    at = base_ref[0] + lax.broadcasted_iota(jnp.int32, (count, 1), 0)
    start, _ = clip_bounds(at, ends_ref, group, clips)
    age = jnp.broadcast_to(at - start, (count, 128))
    source = base_ref[0] - EDGE + lax.broadcasted_iota(jnp.int32, (count + EDGE, 1), 0)
    _, stop = clip_bounds(source, ends_ref, group, clips)
    remain = jnp.broadcast_to(stop - source, (count + EDGE, 128))
    total = jnp.zeros((count + EDGE, 128), F32)
    for tap in range(KERNEL):
        back = KERNEL - 1 - tap
        first = EDGE - back
        kept = jnp.where(age >= back, own, 0.0) * window[first : first + count]
        dtaps_ref[tap : tap + 1] += jnp.sum(kept, axis=0, keepdims=True)
        values = spread[back : back + count + EDGE] * taps_ref[tap : tap + 1]
        total = total + jnp.where(remain > back, values, 0.0)
    dprev_ref[0] = total[0:EDGE].astype(BF)
    dglu_ref[0] = total[EDGE:]


def taps_specs(count, order):
    smem = pl.BlockSpec(memory_space=pltpu.SMEM)
    lanes = pl.BlockSpec((1, count, 128), lambda *at: (at[order[0]], 0, at[order[1]]))
    edge = pl.BlockSpec((1, EDGE, 128), lambda *at: (at[order[0]], 0, at[order[1]]))
    taps = pl.BlockSpec((EDGE, 128), lambda *at: (0, at[order[1]]))
    return smem, lanes, edge, taps


def taps_forward(ends, base, prev, glu, taps):
    groups, count, width = glu.shape
    smem, lanes, edge, tap_lanes = taps_specs(count, (0, 1))
    return pl.pallas_call(
        functools.partial(taps_kernel, ends.shape[1]),
        grid=(groups, width // 128),
        in_specs=[smem, smem, edge, lanes, tap_lanes],
        out_specs=lanes,
        out_shape=jax.ShapeDtypeStruct((groups, count, width), F32),
        scratch_shapes=[pltpu.VMEM((count + EDGE, 128), F32)],
        name="taps",
    )(ends, base, prev, glu, taps)


def taps_back(ends, base, prev, glu, taps, grad, normal_part, inverse, sums, gain):
    groups, count, width = glu.shape
    smem, lanes, edge, tap_lanes = taps_specs(count, (1, 0))
    row_one = pl.BlockSpec((1, count, 1), lambda c, g: (g, 0, 0))
    row_two = pl.BlockSpec((1, count, 2), lambda c, g: (g, 0, 0))
    line = pl.BlockSpec((1, 128), lambda c, g: (0, c))
    shape = jax.ShapeDtypeStruct
    return pl.pallas_call(
        functools.partial(taps_back_kernel, ends.shape[1]),
        grid=(width // 128, groups),
        in_specs=[smem, smem, edge, lanes, tap_lanes, lanes, lanes, row_one, row_two, line],
        out_specs=[lanes, edge, tap_lanes, line, line],
        out_shape=[
            shape((groups, count, width), F32),
            shape((groups, EDGE, width), BF),
            shape((EDGE, width), F32),
            shape((1, width), F32),
            shape((1, width), F32),
        ],
        scratch_shapes=[
            pltpu.VMEM((count + EDGE, 128), F32),
            pltpu.VMEM((count + 2 * EDGE, 128), F32),
        ],
        name="taps_back",
    )(ends, base, prev, glu, taps, grad, normal_part, inverse, sums, gain)


def dot(left, right, left_axis, right_axis):
    return lax.dot_general(
        left, right, (((left_axis,), (right_axis,)), ((), ())), preferred_element_type=F32
    )


def row_major(array):
    return with_layout_constraint(array, Layout(tuple(range(array.ndim))))


def local(
    inputs,
    lengths,
    ffn_in,
    ffn_out,
    qkv_weight,
    out_weight,
    conv_in,
    conv_depth,
    conv_out,
    norm_gain,
    norm_bias,
    rel_key,
    cotangent,
):
    place = Place()
    seq_size, chips, core = place.seq_size, place.chips, place.core
    row_count, dim = inputs.shape[1:]
    hid = ffn_in.shape[3] // 2
    quarter = hid // 2
    width = dim // 2
    rows = 2 * ffn_in.shape[2]
    tap_first, tap_last = 12, 12 + KERNEL

    small = jnp.concatenate([norm_gain[0], norm_bias[0], conv_depth[0]], 0)
    small_count = small.shape[0]
    small = jnp.pad(small, ((0, 128 - small_count), (0, 0))).T
    out_rows = jnp.swapaxes(ffn_out[0], 1, 2)

    def pick(array, count, which):
        parts = array.reshape(array.shape[0], count, -1)
        return place.core_part(parts, 2, which).reshape(array.shape[0], -1)

    def ffn_parts(net, part, which):
        span = slice(part * quarter, (part + 1) * quarter)
        return [pick(ffn_in[0, net], 1, which)[:, span], pick(out_rows[net], 1, which)[:, span]]

    def attention_parts(which):
        return [
            pick(qkv_weight[0], 3, which),
            pick(conv_in[0], 2, which),
            pick(out_weight[0], 1, which),
            pick(conv_out[0], 1, which),
        ]

    def chip_block(kept, sent):
        kept, sent = jnp.concatenate(kept, 1), jnp.concatenate(sent, 1)
        return place.by_core(kept, place.sibling(sent), 0)

    other = 1 - core
    first_block = chip_block(
        ffn_parts(0, 0, core) + [small], ffn_parts(0, 0, other) + [small]
    )
    later_block = chip_block(
        ffn_parts(0, 1, core) + attention_parts(core) + ffn_parts(1, 0, core) + ffn_parts(1, 1, core),
        ffn_parts(0, 1, other)
        + attention_parts(other)
        + ffn_parts(1, 0, other)
        + ffn_parts(1, 1, other),
    )
    n_attention = 7 * width
    attention_block = later_block[:, 2 * quarter : 2 * quarter + n_attention]
    attention_all = lax.all_gather(attention_block, ("seq", "plane"), axis=0, tiled=True)
    at = [0, quarter]
    at += [2 * quarter + n_attention + part * quarter for part in range(4)]
    pieces = [later_block[:, start : start + quarter] for start in at]
    chunks = [
        (
            [first_block[:, :quarter], first_block[:, 2 * quarter :]],
            [first_block[:, quarter : 2 * quarter]],
        ),
        ([pieces[0]], [pieces[1]]),
        ([pieces[2]], [pieces[3]]),
        ([pieces[4]], [pieces[5]]),
    ]
    gathered, z_marks, firsts, seconds = [], [], [], []

    def fetch(*waits):
        index = len(gathered)
        left, right = chunks[index]
        block = tie(jnp.concatenate(left + right, 1), *z_marks[-1:], *waits)
        spread = place.swap_seq(jnp.broadcast_to(block[None], (seq_size,) + block.shape))
        z_marks.append(tip(spread))
        marks = []
        n_left = sum(part.shape[1] for part in left)
        parts = tie(spread[..., :n_left], *seconds[-1:]), tie(spread[..., n_left:], *seconds[-1:])
        fulls = [gather_plane(place, part, turn, marks) for turn, part in enumerate(parts)]
        firsts.append(marks[place.bits])
        seconds.append(marks[-1])
        gathered.append([full.reshape(dim, -1) for full in fulls])

    fetch()
    fetch()
    small_all = gathered[0][0][:, quarter:].T.astype(F32)
    gains, biases = small_all[:6, None], small_all[6:12, None]
    tap_values = place.core_part(small_all[tap_first:tap_last], 1, core)
    gain3 = place.core_part(small_all[3], 0, core)
    bias3 = place.core_part(small_all[9], 0, core)
    w_qkv = attention_all[:, : 3 * width]
    w_first = attention_all[:, 3 * width : 5 * width]
    columns = attention_all[:, 5 * width :]
    from_other = place.sibling(place.core_part(columns, 0, other))
    columns = place.core_part(columns, 0, core)
    w_out = place.by_core(columns[:, :width], from_other[:, :width], 1)
    w_second = place.by_core(columns[:, width:], from_other[:, width:], 1)

    group_lengths = jnp.concatenate([lengths, place.sibling(lengths)], 0)
    clips = group_lengths.shape[1]
    order = jnp.arange(clips)
    clip_ends = jnp.sum(
        jnp.where(order[None, :, None] >= order[None, None, :], group_lengths[:, None, :], 0), axis=2
    )
    first_row = place.seq * row_count

    def weights_of(net, part):
        left, right = gathered[2 * net + part]
        return left[:, :quarter], right

    def flat2(array):
        return array.reshape(2 * row_count, -1)

    def pair2(array):
        return array.reshape(2, row_count, -1)

    def feed_forward(normed, net):
        normed_low = flat2(place.both(normed))
        pres, acts, branch = [], [], 0.0
        for part in range(2):
            w_in, w_down = weights_of(net, part)
            pre_act = dot(normed_low, w_in, 1, 0)
            act_low = (pre_act * jax.nn.sigmoid(pre_act)).astype(BF)
            if net == 0 and part == 0:
                fetch(tip(act_low))
            branch = branch + dot(act_low, w_down, 1, 1)
            pres.append(pre_act)
            acts.append(act_low)
        return pair2(branch), (normed_low, pres, acts)

    def joined(base, share, branch, norm_index, *marks):
        received = place.from_sibling(branch)
        gain = tie(gains[norm_index], *marks)
        return add_and_norm(base, share, branch, received, gain, biases[norm_index])

    stream = inputs[0].astype(F32)
    normed = add_and_norm(stream, 0.0, None, None, gains[0], biases[0])
    branch, ffn_first = feed_forward(normed, 0)
    after_ffn, normed = joined(stream, 0.5, branch, 1)
    fetch(tip(normed))
    attn_input = flat2(place.both(normed))
    projected = pair2(dot(attn_input, w_qkv, 1, 0).astype(BF))
    from_left = place.along(projected[:, row_count - LEFT :, width:], 1)
    from_right = place.along(projected[:, :RIGHT, width:], -1)
    from_right = jnp.pad(from_right, ((0, 0), (0, LEFT - RIGHT), (0, 0)))
    relative = jnp.pad(
        jnp.concatenate([rel_key[0], rel_key[0]], 1), ((0, SPAN - rel_key.shape[1]), (0, 0))
    )
    base = jnp.reshape(first_row, (1,))
    attended, probs = attend(clip_ends, tie(base, firsts[2]), projected, from_left, from_right, relative)
    attended = flat2(attended)
    after_attn, normed = joined(after_ffn, 1.0, pair2(dot(attended, w_out, 1, 0)), 2, seconds[2], firsts[3])
    conv_input = flat2(place.both(normed))
    spread_pre = pair2(dot(conv_input, w_first, 1, 0))
    value_part, gate_sig = spread_pre[..., :width], jax.nn.sigmoid(spread_pre[..., width:])
    gated_low = (value_part * gate_sig).astype(BF)
    from_prev = place.along(gated_low[:, row_count - EDGE :], 1)
    tap_rows = jnp.pad(tap_values, ((0, EDGE - KERNEL), (0, 0)))
    filtered = taps_forward(clip_ends, base, from_prev, gated_low, tap_rows)
    normed_conv, depth_norm = split_layer_norm(place, filtered, gain3, bias3)
    swished = (normed_conv * jax.nn.sigmoid(normed_conv)).astype(BF)
    after_conv, normed = joined(after_attn, 1.0, pair2(dot(flat2(swished), w_second, 1, 0)), 4)
    branch, ffn_second = feed_forward(normed, 1)
    fourth, result = joined(after_conv, 0.5, branch, 5)
    outputs = result[None]

    def summed(terms):
        return jnp.sum(place.swap_seq(terms).astype(F32), 0)

    def scatter_early(terms, after):
        terms = jnp.concatenate(terms, 1)
        terms = row_major(terms.reshape(seq_size, chips * rows, terms.shape[1]))
        part = lax.psum_scatter(terms, "plane", scatter_dimension=1, tiled=True)
        return summed(tie(row_major(part), after))

    def plane_sums(pair):
        parts, marks = [], []
        for turn, terms in enumerate(pair):
            blocks = terms.reshape(seq_size, chips, rows, -1)
            parts.append(scatter_plane(place, blocks, turn, marks))
        return jnp.concatenate(parts, -1), marks[:: place.bits]

    gain_grads = [None] * 6
    bias_grads = [None] * 6

    def back_to(norm_index, stream_at, branch, through, share, *marks):
        received = None if through is None else place.from_sibling(branch)
        gain = tie(gains[norm_index], *marks)
        grad, low, gain_grads[norm_index], bias_grads[norm_index] = norm_and_add_back(
            stream_at, branch, received, gain, through, share
        )
        return grad, low

    def feed_back(low, net, cached):
        normed_low, pres, acts = cached
        branch_grad = flat2(place.both(low))
        pre_grads, normed_grad = [], 0.0
        for part in range(2):
            act_grad = dot(branch_grad, weights_of(net, part)[1], 1, 0)
            pre_grads.append((act_grad * swish_slope(pres[part])).astype(BF))
        for part in range(2):
            normed_grad = normed_grad + dot(pre_grads[part], weights_of(net, part)[0], 1, 1)
        return pair2(normed_grad), pre_grads, acts, normed_low, branch_grad

    def exchanged(wide):
        received = place.sibling(place.core_part(wide, 1, other))
        return place.by_core(place.core_part(wide, 1, core), received, 0)

    grad_fourth, low = back_to(5, fourth, cotangent[0], None, 0.5)
    branch, pre_grads, acts, normed_low, branch_grad = feed_back(low, 1, ffn_second)
    second_terms = [products(normed_low, branch_grad, pre_grads + acts)]
    grad_conv_out, low = back_to(4, after_conv, branch, grad_fourth, 1.0)
    branch_grad = flat2(place.both(low))
    conv_out_terms = exchanged(dot(flat2(swished), branch_grad, 0, 0).astype(BF))
    swish_grad = pair2(dot(branch_grad, w_second, 1, 1))
    swish_grad = swish_grad * swish_slope(normed_conv)
    sums = split_norm_sums(place, swish_grad, depth_norm[0], gain3)
    gated_grad, to_prev, tap_grads, gain3_grad, bias3_grad = taps_back(
        clip_ends, base, from_prev, gated_low, tap_rows, swish_grad, *depth_norm, sums, gain3[None]
    )
    to_prev = place.along(to_prev, -1).astype(F32)
    gated_grad = gated_grad + jnp.pad(to_prev, ((0, 0), (row_count - EDGE, 0), (0, 0)))
    spread_grad = flat2(
        jnp.concatenate(
            [gated_grad * gate_sig, gated_grad * value_part * gate_sig * (1.0 - gate_sig)], axis=2
        ).astype(BF)
    )
    branch = pair2(dot(spread_grad, w_first, 1, 1))
    conv_in_terms = dot(conv_input, spread_grad, 0, 0).astype(BF)
    grad_attn_out, low = back_to(2, after_attn, branch, grad_conv_out, 1.0)
    branch_grad = flat2(place.both(low))
    out_terms = exchanged(dot(attended, branch_grad, 0, 0).astype(BF))
    attended_grad = pair2(dot(branch_grad, w_out, 1, 1).astype(BF))
    query_grad, key_grad, value_grad, kl, vl, kr, vr, relative_grad = attend_back(
        projected, from_left, from_right, relative, attended_grad, probs
    )
    second_sum = scatter_early(second_terms, tip(query_grad))
    to_left = place.along(jnp.concatenate([kl, vl], 2), -1).astype(F32)
    to_right = place.along(jnp.concatenate([kr[:, :RIGHT], vr[:, :RIGHT]], 2), 1).astype(F32)
    own_grad = (
        jnp.concatenate([key_grad, value_grad], 2)
        + jnp.pad(to_left, ((0, 0), (row_count - LEFT, 0), (0, 0)))
        + jnp.pad(to_right, ((0, 0), (0, row_count - RIGHT), (0, 0)))
    )
    projected_grad = flat2(jnp.concatenate([query_grad, own_grad.astype(BF)], axis=2))
    branch = pair2(dot(projected_grad, w_qkv, 1, 1))
    qkv_terms = dot(attn_input, projected_grad, 0, 0).astype(BF)
    grad_ffn_out, low = back_to(
        1, after_ffn, branch, grad_attn_out, 0.5
    )
    branch, pre_grads, acts, normed_low, branch_grad = feed_back(low, 0, ffn_first)
    downs = [dot(branch_grad, acts[part], 0, 0).astype(BF) for part in range(2)]
    ins = [dot(normed_low, pre_grads[part], 0, 0).astype(BF) for part in range(2)]
    down_part, down_marks = plane_sums(downs)
    in_part, _ = plane_sums(ins)
    grad_input, _ = back_to(
        0, stream, branch, grad_ffn_out, 1.0, *down_marks, tip(second_sum)
    )
    down_sum = summed(tie(down_part, tip(grad_input)))
    in_sum = summed(tie(in_part, tip(grad_input)))
    attention_sum = scatter_early(
        [qkv_terms, conv_in_terms, out_terms, conv_out_terms], tip(grad_input)
    )
    offsets = LEFT + RIGHT + 1
    relative_grad = relative_grad[:offsets, :HEAD_DIM] + relative_grad[:offsets, HEAD_DIM:]

    def spread_core(half_rows):
        return place.by_core(half_rows, jnp.zeros_like(half_rows), 1)

    gain_grads[3] = spread_core(gain3_grad)
    bias_grads[3] = spread_core(bias3_grad)
    small_grads = jnp.concatenate(
        gain_grads + bias_grads + [spread_core(tap_grads[:KERNEL])], 0
    )
    small_grads = jnp.pad(small_grads, ((0, 128 - small_count), (0, 0))).T
    rel_part = jnp.pad(relative_grad, ((0, -offsets % 8), (0, 128 - HEAD_DIM)))
    rel_part = rel_part + place.sibling(rel_part)
    current = small_grads.reshape((seq_size,) + (2,) * place.bits + (rows, 128))
    for bit in range(place.bits):
        axis = place.bits - bit
        me = place.bit(bit)
        keep = lax.dynamic_slice_in_dim(current, me, 1, axis)
        sent = lax.dynamic_slice_in_dim(current, 1 - me, 1, axis)
        got = place.hop(jnp.concatenate([sent.reshape(-1, 128), rel_part], 0), bit)
        current = keep + got[: -rel_part.shape[0]].reshape(keep.shape)
        rel_part = rel_part + got[-rel_part.shape[0] :]
    rel_all = jnp.broadcast_to(rel_part[None], (seq_size,) + rel_part.shape)
    small_total = summed(
        jnp.concatenate([current.reshape(seq_size, rows, 128), rel_all], 1)
    )
    rel_total = small_total[rows : rows + offsets, :HEAD_DIM]
    small_total = small_total[:rows]
    small_sum = place.core_part(small_total, 0, core) + place.sibling(
        place.core_part(small_total, 0, other)
    )
    small_sum = small_sum[:, :small_count].T

    def own_rows(total, counts):
        received = place.sibling(place.core_part(total, 0, other))
        mine = place.core_part(total, 0, core)
        results, start = [], 0
        for count, n in counts:
            halves = [
                part[:, start : start + n].reshape(-1, count, n // count) for part in (mine, received)
            ]
            results.append(place.by_core(*halves, 2).reshape(mine.shape[0], 2 * n))
            start += n
        return results

    in_second, down_second = own_rows(second_sum, [(1, hid), (1, hid)])
    qkv_sum, first_sum, out_sum, second_sum = own_rows(
        attention_sum, [(3, 3 * width), (2, 2 * width), (1, width), (1, width)]
    )
    (down_first,) = own_rows(down_sum, [(1, hid)])
    (in_first,) = own_rows(in_sum, [(1, hid)])
    return (
        outputs,
        grad_input[None],
        jnp.stack([in_first, in_second])[None],
        jnp.swapaxes(jnp.stack([down_first, down_second]), 1, 2)[None],
        qkv_sum[None],
        out_sum[None],
        first_sum[None],
        small_sum[None, tap_first:tap_last],
        second_sum[None],
        small_sum[None, :6],
        small_sum[None, 6:12],
        rel_total[None],
    )


def solution(mesh):
    seq_size, fsdp_size = mesh.shape["seq"], mesh.shape["fsdp"]
    chips = Mesh(mesh.devices.reshape(seq_size, fsdp_size // 2, 2), ("seq", "plane", "core"))
    fsdp = ("plane", "core")
    spread = ("seq", "plane", "core")
    tokens = P(fsdp, "seq", None)
    split_rows = P(None, spread, None)
    split_last = P(None, None, spread)
    weights = (
        P(None, None, spread, None),
        P(None, None, None, spread),
        split_rows,
        split_rows,
        split_rows,
        split_last,
        split_rows,
        split_last,
        split_last,
        P(),
    )
    return jax.shard_map(
        local,
        mesh=chips,
        in_specs=(tokens, P(fsdp, None)) + weights + (tokens,),
        out_specs=(tokens, tokens) + weights,
        check_vma=False,
    )
```

```python
import functools

import jax
import jax.numpy as jnp
from jax import lax
from jax.experimental import pallas as pl
from jax.experimental.layout import Layout, with_layout_constraint
from jax.experimental.pallas import tpu as pltpu
from jax.sharding import Mesh
from jax.sharding import PartitionSpec as P

HEAD_DIM = 64
KERNEL = 31
LEFT = 64
RIGHT = 8
BLOCK = 128
SPAN = 256
EDGE = 32
BF = jnp.bfloat16
F32 = jnp.float32


class Place:
    def __init__(self):
        self.seq_size = lax.axis_size("seq")
        self.chips = lax.axis_size("plane")
        self.seq = lax.axis_index("seq")
        self.chip = lax.axis_index("plane")
        self.core = lax.axis_index("core")
        self.bits = self.chips.bit_length() - 1

    def sibling(self, shard):
        return lax.ppermute(shard, "core", [(0, 1), (1, 0)])

    def hop(self, shard, bit):
        return lax.ppermute(shard, "plane", [(i, i ^ (1 << bit)) for i in range(self.chips)])

    def along(self, shard, by):
        pairs = [(i, i + by) for i in range(self.seq_size) if 0 <= i + by < self.seq_size]
        return lax.ppermute(shard, "seq", pairs)

    def swap_seq(self, blocks):
        return lax.all_to_all(blocks, "seq", 0, 0, tiled=True)

    def bit(self, bit):
        return lax.rem(lax.div(self.chip, 1 << bit), 2)

    def both(self, mine):
        return jnp.stack([mine, self.sibling(mine)])

    def from_sibling(self, partial):
        return self.sibling(partial[1].astype(BF))

    def by_core(self, mine, other, axis):
        return jnp.where(
            self.core == 0,
            jnp.concatenate([mine, other], axis),
            jnp.concatenate([other, mine], axis),
        )

    def core_part(self, array, axis, which):
        size = array.shape[axis] // 2
        return lax.dynamic_slice_in_dim(array, which * size, size, axis)


def tie(array, *marks):
    ready = None
    for mark in marks:
        if mark is None:
            continue
        equal = mark == mark
        ready = equal if ready is None else jnp.logical_and(ready, equal)
    return array if ready is None else jnp.where(ready, array, jnp.zeros_like(array))


def tip(array):
    return array[(0,) * array.ndim]


def gather_plane(place, part, turn, marks):
    bits = place.bits
    current = part.reshape((part.shape[0],) + (1,) * bits + part.shape[1:])
    for step in range(bits):
        bit = (turn + step) % bits
        axis = bits - bit
        other = place.hop(current, bit)
        marks.append(tip(other))
        current = jnp.where(
            place.bit(bit) == 0,
            jnp.concatenate([current, other], axis),
            jnp.concatenate([other, current], axis),
        )
    return current.reshape((part.shape[0], place.chips) + part.shape[1:])


def scatter_plane(place, full, turn, waits, start):
    bits = place.bits
    current = full.reshape((full.shape[0],) + (2,) * bits + full.shape[2:])
    for step in range(bits):
        bit = (turn + step) % bits
        axis = bits - bit
        me = place.bit(bit)
        keep = lax.dynamic_slice_in_dim(current, me, 1, axis)
        sent = lax.dynamic_slice_in_dim(current, 1 - me, 1, axis)
        got = place.hop(tie(sent, *(waits if step == 1 else start if step == 0 else ())), bit)
        current = (keep.astype(F32) + got.astype(F32)).astype(full.dtype)
    return current.reshape((full.shape[0],) + full.shape[2:])


def clip_index(positions, ends_ref, group, clips):
    inside = jnp.zeros(positions.shape, jnp.int32)
    for clip in range(clips):
        inside = inside + (positions >= ends_ref[group, clip]).astype(jnp.int32)
    return jnp.where(positions < 0, -1, inside)


def dot_nt(left, right):
    return lax.dot_general(left, right, (((1,), (1,)), ((), ())), preferred_element_type=F32)


def dot_nn(left, right):
    return lax.dot_general(left, right, (((1,), (0,)), ((), ())), preferred_element_type=F32)


def dot_tn(left, right):
    return lax.dot_general(left, right, (((0,), (0,)), ((), ())), preferred_element_type=F32)


def band_mask(ends_ref, base_ref, block, clips):
    group = pl.program_id(0)
    start = base_ref[0] + block * BLOCK
    query_at = start + lax.broadcasted_iota(jnp.int32, (BLOCK, 1), 0)
    key_at = start - LEFT + lax.broadcasted_iota(jnp.int32, (1, SPAN), 1)
    apart = lax.broadcasted_iota(jnp.int32, (BLOCK, SPAN), 1) - lax.broadcasted_iota(
        jnp.int32, (BLOCK, SPAN), 0
    )
    query_ids = clip_index(query_at, ends_ref, group, clips)
    key_ids = clip_index(key_at, ends_ref, group, clips)
    return (apart >= 0) & (apart <= LEFT + RIGHT) & (query_ids == key_ids)


def fill_window(window, left_ref, own_ref, right_ref):
    count = own_ref.shape[1]
    window[0:LEFT] = left_ref[0]
    window[LEFT : LEFT + count] = own_ref[0]
    window[LEFT + count :] = right_ref[0]


def band_probs(query, keys, relative, mask):
    scores = dot_nt(query, keys)
    positional = pltpu.roll(dot_nt(query, relative), 0, 1, stride=1, stride_axis=0)
    scores = jnp.where(mask, (scores + positional) * HEAD_DIM ** (-0.5), -1e30)
    expanded = jnp.exp(scores - jnp.max(scores, axis=1, keepdims=True))
    return expanded / jnp.sum(expanded, axis=1, keepdims=True)


def attend_kernel(
    clips, ends_ref, base_ref, q_ref, k_ref, v_ref, kl_ref, vl_ref, kr_ref, vr_ref, rel_ref,
    out_ref, probs_ref, keys, values,
):
    fill_window(keys, kl_ref, k_ref, kr_ref)
    fill_window(values, vl_ref, v_ref, vr_ref)
    low_lane = lax.broadcasted_iota(jnp.int32, (BLOCK, 2 * HEAD_DIM), 1) < HEAD_DIM
    for block in range(q_ref.shape[1] // BLOCK):
        at = block * BLOCK
        mask = band_mask(ends_ref, base_ref, block, clips)
        query = q_ref[0, at : at + BLOCK]
        zero = jnp.zeros_like(query)
        outs = []
        queries = jnp.where(low_lane, query, zero), jnp.where(low_lane, zero, query)
        for one, query_one in enumerate(queries):
            probs = band_probs(query_one, keys[at : at + SPAN], rel_ref[...], mask).astype(BF)
            probs_ref[0, 0, block, one] = probs
            outs.append(dot_nn(probs, values[at : at + SPAN]))
        out_ref[0, at : at + BLOCK] = jnp.where(low_lane, outs[0], outs[1]).astype(BF)


def attend_back_kernel(
    q_ref, k_ref, v_ref, kl_ref, vl_ref, kr_ref, vr_ref, rel_ref, do_ref, probs_ref,
    dq_ref, dk_ref, dv_ref, dkl_ref, dvl_ref, dkr_ref, dvr_ref, drel_ref,
    keys, values, key_sum, value_sum,
):
    scale = HEAD_DIM ** (-0.5)
    count = q_ref.shape[1]
    fill_window(keys, kl_ref, k_ref, kr_ref)
    fill_window(values, vl_ref, v_ref, vr_ref)
    key_sum[...] = jnp.zeros_like(key_sum)
    value_sum[...] = jnp.zeros_like(value_sum)

    @pl.when((pl.program_id(0) == 0) & (pl.program_id(1) == 0))
    def _():
        drel_ref[...] = jnp.zeros_like(drel_ref)

    low_lane = lax.broadcasted_iota(jnp.int32, (BLOCK, 2 * HEAD_DIM), 1) < HEAD_DIM
    row = lax.broadcasted_iota(jnp.int32, (BLOCK, BLOCK), 0)
    column = lax.broadcasted_iota(jnp.int32, (BLOCK, BLOCK), 1)
    flip = (row + column == BLOCK - 1).astype(F32).astype(BF)
    for block in range(count // BLOCK):
        at = block * BLOCK
        query = q_ref[0, at : at + BLOCK]
        grad = do_ref[0, at : at + BLOCK]
        zero = jnp.zeros_like(query)
        some_keys = keys[at : at + SPAN]
        outs, key_part, value_part, rel_part = [], None, None, None
        for low in (True, False):
            pick = (lambda a: jnp.where(low_lane, a, zero)) if low else (
                lambda a: jnp.where(low_lane, zero, a)
            )
            query_one, grad_one = pick(query), pick(grad)
            probs_low = probs_ref[0, 0, block, 0 if low else 1]
            probs = probs_low.astype(F32)
            prob_grads = dot_nt(grad_one, values[at : at + SPAN])
            inner = jnp.sum(prob_grads * probs, axis=1, keepdims=True)
            score_grads = (probs * (prob_grads - inner)).astype(BF)
            turned = pltpu.roll(
                dot_nn(flip, score_grads), SPAN - BLOCK + 1, 1, stride=1, stride_axis=0
            )
            by_offset = dot_nn(flip, turned[:, :BLOCK].astype(BF)).astype(BF)
            outs.append(dot_nn(score_grads, some_keys) + dot_nn(by_offset, rel_ref[0:BLOCK]))
            parts = (
                dot_tn(score_grads, query_one),
                dot_tn(probs_low, grad_one),
                dot_tn(by_offset, query_one),
            )
            if low:
                key_part, value_part, rel_part = parts
            else:
                key_part, value_part, rel_part = (
                    key_part + parts[0],
                    value_part + parts[1],
                    rel_part + parts[2],
                )
        dq_ref[0, at : at + BLOCK] = (jnp.where(low_lane, outs[0], outs[1]) * scale).astype(BF)
        key_sum[at : at + SPAN] += key_part * scale
        value_sum[at : at + SPAN] += value_part
        drel_ref[...] += rel_part * scale
    for total, left, own, right in (
        (key_sum, dkl_ref, dk_ref, dkr_ref),
        (value_sum, dvl_ref, dv_ref, dvr_ref),
    ):
        left[0] = total[0:LEFT].astype(BF)
        own[0] = total[LEFT : LEFT + count]
        right[0] = total[LEFT + count :].astype(BF)


def attend_specs(groups, count, pairs):
    lanes = 2 * HEAD_DIM
    smem = pl.BlockSpec(memory_space=pltpu.SMEM)

    def own(at):
        return pl.BlockSpec((1, count, lanes), lambda g, h: (g, 0, at * pairs + h))

    def edge(at):
        return pl.BlockSpec((1, LEFT, lanes), lambda g, h: (g, 0, at * pairs + h))

    rel = pl.BlockSpec((SPAN, lanes), lambda g, h: (0, 0))
    probs = pl.BlockSpec(
        (1, 1, count // BLOCK, 2, BLOCK, SPAN), lambda g, h: (g, h, 0, 0, 0, 0)
    )
    specs = [smem, smem, own(0), own(1), own(2), edge(0), edge(1), edge(0), edge(1), rel]
    return specs, own, edge, probs


def attend(ends, base, projected, left, right, relative):
    groups, count, _ = projected.shape
    pairs = projected.shape[2] // (6 * HEAD_DIM)
    specs, own, _, probs = attend_specs(groups, count, pairs)
    window = pltpu.VMEM((count + 2 * LEFT, 2 * HEAD_DIM), BF)
    return pl.pallas_call(
        functools.partial(attend_kernel, ends.shape[1]),
        grid=(groups, pairs),
        in_specs=specs,
        out_specs=[own(0), probs],
        out_shape=[
            jax.ShapeDtypeStruct((groups, count, projected.shape[2] // 3), BF),
            jax.ShapeDtypeStruct((groups, pairs, count // BLOCK, 2, BLOCK, SPAN), BF),
        ],
        scratch_shapes=[window, window],
        name="attend",
    )(ends, base, projected, projected, projected, left, left, right, right, relative)


def attend_back(projected, left, right, relative, grad, probs):
    groups, count, _ = projected.shape
    width = projected.shape[2] // 3
    pairs = width // (2 * HEAD_DIM)
    specs, own, edge, saved = attend_specs(groups, count, pairs)
    window = pltpu.VMEM((count + 2 * LEFT, 2 * HEAD_DIM), BF)
    total = pltpu.VMEM((count + 2 * LEFT, 2 * HEAD_DIM), F32)
    rel_sum = pl.BlockSpec((BLOCK, 2 * HEAD_DIM), lambda g, h: (0, 0))
    shape = lambda rows, dtype: jax.ShapeDtypeStruct((groups, rows, width), dtype)
    return pl.pallas_call(
        attend_back_kernel,
        grid=(groups, pairs),
        in_specs=specs[2:] + [own(0), saved],
        out_specs=[own(0), own(0), own(0), edge(0), edge(0), edge(0), edge(0), rel_sum],
        out_shape=[
            shape(count, BF),
            shape(count, F32),
            shape(count, F32),
            shape(LEFT, BF),
            shape(LEFT, BF),
            shape(LEFT, BF),
            shape(LEFT, BF),
            jax.ShapeDtypeStruct((BLOCK, 2 * HEAD_DIM), F32),
        ],
        scratch_shapes=[window, window, total, total],
        name="attend_back",
    )(projected, projected, projected, left, left, right, right, relative, grad, probs)


def products_kernel(steps, first_ref, second_ref, *refs):
    right_refs, out_ref, turned = refs[:-2], refs[-2], refs[-1]
    at = pl.program_id(0)

    @pl.when(at == 0)
    def _():
        turned[...] = first_ref[...].T

    @pl.when(at == 2 * steps)
    def _():
        turned[...] = second_ref[...].T

    for number, right_ref in enumerate(right_refs):

        @pl.when((at >= number * steps) & (at < (number + 1) * steps))
        def _(right_ref=right_ref):
            out_ref[...] = dot_nn(turned[...], right_ref[...]).astype(BF)


def products(first, second, rights):
    count, dim = first.shape
    step = 512
    steps = rights[0].shape[1] // step
    whole = pl.BlockSpec((count, dim), lambda i: (0, 0))

    def part(number):
        return pl.BlockSpec(
            (count, step), lambda i: (0, jnp.clip(i - number * steps, 0, steps - 1))
        )

    return pl.pallas_call(
        functools.partial(products_kernel, steps),
        grid=(4 * steps,),
        in_specs=[whole, whole] + [part(number) for number in range(4)],
        out_specs=pl.BlockSpec((dim, step), lambda i: (0, i)),
        out_shape=jax.ShapeDtypeStruct((dim, 4 * steps * step), BF),
        scratch_shapes=[pltpu.VMEM((dim, count), BF)],
        name="products",
    )(first, second, *rights)


def norm_parts(values):
    centered = values - jnp.mean(values, axis=1, keepdims=True)
    variance = jnp.mean(centered * centered, axis=1, keepdims=True)
    inverse = lax.rsqrt(variance + 1e-05)
    return centered * inverse, inverse


def norm_kernel(share, *refs):
    if share:
        base_ref, own_ref, other_ref, gain_ref, bias_ref, stream_ref, low_ref = refs
        stream = base_ref[...] + share * (own_ref[0] + other_ref[...].astype(F32))
        stream_ref[...] = stream
    else:
        base_ref, gain_ref, bias_ref, low_ref = refs
        stream = base_ref[...]
    normal_part, _ = norm_parts(stream)
    low_ref[...] = (normal_part * gain_ref[...] + bias_ref[...]).astype(BF)


def norm_back_kernel(share, scale, *refs):
    if share:
        stream_ref, own_ref, other_ref, gain_ref, through_ref, grad_ref, low_ref = refs[:7]
        gradient = own_ref[0] + other_ref[...].astype(F32)
    else:
        stream_ref, own_ref, gain_ref, grad_ref, low_ref = refs[:5]
        gradient = own_ref[...].astype(F32)
    gain_grad_ref, bias_grad_ref = refs[-2:]
    normal_part, inverse = norm_parts(stream_ref[...])
    scaled = gradient * gain_ref[...]
    inner = jnp.mean(scaled * normal_part, axis=1, keepdims=True)
    total = inverse * (scaled - jnp.mean(scaled, axis=1, keepdims=True) - normal_part * inner)
    if share:
        total = total + through_ref[...]
    grad_ref[...] = total
    low_ref[...] = (scale * total).astype(BF)

    @pl.when(pl.program_id(0) == 0)
    def _():
        gain_grad_ref[...] = jnp.zeros_like(gain_grad_ref)
        bias_grad_ref[...] = jnp.zeros_like(bias_grad_ref)

    gain_grad_ref[...] += jnp.sum(gradient * normal_part, axis=0, keepdims=True)
    bias_grad_ref[...] += jnp.sum(gradient, axis=0, keepdims=True)


def row_specs(dim):
    step = 128
    rows = pl.BlockSpec((step, dim), lambda i: (i, 0))
    first = pl.BlockSpec((1, step, dim), lambda i: (0, i, 0))
    line = pl.BlockSpec((1, dim), lambda i: (0, 0))
    return step, rows, first, line


def add_and_norm(base, share, own, other, gain, bias):
    count, dim = base.shape
    step, rows, first, line = row_specs(dim)
    low = jax.ShapeDtypeStruct((count, dim), BF)
    if not share:
        return pl.pallas_call(
            functools.partial(norm_kernel, share),
            grid=(count // step,),
            in_specs=[rows, line, line],
            out_specs=rows,
            out_shape=low,
            name="norm",
        )(base, gain, bias)
    return pl.pallas_call(
        functools.partial(norm_kernel, share),
        grid=(count // step,),
        in_specs=[rows, first, rows, line, line],
        out_specs=[rows, rows],
        out_shape=[jax.ShapeDtypeStruct((count, dim), F32), low],
        name="add_and_norm",
    )(base, own, other, gain, bias)


def norm_and_add_back(stream, own, other, gain, through, scale):
    count, dim = stream.shape
    step, rows, first, line = row_specs(dim)
    share = through is not None
    specs = [rows, first, rows, line, rows] if share else [rows, rows, line]
    args = (stream, own, other, gain, through) if share else (stream, own, gain)
    return pl.pallas_call(
        functools.partial(norm_back_kernel, share, scale),
        grid=(count // step,),
        in_specs=specs,
        out_specs=[rows, rows, line, line],
        out_shape=[
            jax.ShapeDtypeStruct((count, dim), F32),
            jax.ShapeDtypeStruct((count, dim), BF),
            jax.ShapeDtypeStruct((1, dim), F32),
            jax.ShapeDtypeStruct((1, dim), F32),
        ],
        name="norm_back",
    )(*args)


def split_layer_norm(place, values, gain_row, bias_row):
    count = values.shape[-1]
    own_mean = jnp.mean(values, axis=-1, keepdims=True)
    own_square = jnp.sum((values - own_mean) ** 2, axis=-1, keepdims=True)
    stats = jnp.concatenate([own_mean, own_square], -1)
    others = place.sibling(stats)[::-1]
    mean = 0.5 * (own_mean + others[..., :1])
    square = own_square + others[..., 1:]
    square = square + count * ((own_mean - mean) ** 2 + (others[..., :1] - mean) ** 2)
    inverse = lax.rsqrt(square / (2 * count) + 1e-05)
    normal_part = (values - mean) * inverse
    return (normal_part * gain_row + bias_row, (normal_part, inverse))


def split_norm_sums(place, gradient, normal_part, gain_row):
    scaled = gradient * gain_row
    sums = jnp.concatenate(
        [
            jnp.sum(scaled, axis=-1, keepdims=True),
            jnp.sum(scaled * normal_part, axis=-1, keepdims=True),
        ],
        -1,
    )
    return (sums + place.sibling(sums)[::-1]) / (2 * gradient.shape[-1])


def swish_slope(values):
    sigmoid_val = jax.nn.sigmoid(values)
    return sigmoid_val * (1.0 + values * (1.0 - sigmoid_val))


def clip_bounds(positions, ends_ref, group, clips):
    start = jnp.zeros(positions.shape, jnp.int32)
    stop = jnp.full(positions.shape, 1 << 30, jnp.int32)
    for clip in range(clips):
        end = ends_ref[group, clip]
        start = jnp.maximum(start, jnp.where(positions >= end, end, 0))
        stop = jnp.minimum(stop, jnp.where(positions < end, end, 1 << 30))
    return start, jnp.where(positions < 0, positions, stop)


def taps_kernel(clips, ends_ref, base_ref, prev_ref, glu_ref, taps_ref, out_ref, window):
    count = glu_ref.shape[1]
    group = pl.program_id(0)
    window[0:EDGE] = prev_ref[0].astype(F32)
    window[EDGE:] = glu_ref[0].astype(F32)
    at = base_ref[0] + lax.broadcasted_iota(jnp.int32, (count, 1), 0)
    start, _ = clip_bounds(at, ends_ref, group, clips)
    age = jnp.broadcast_to(at - start, (count, 128))
    total = jnp.zeros((count, 128), F32)
    for tap in range(KERNEL):
        first = tap + EDGE - KERNEL + 1
        values = window[first : first + count] * taps_ref[tap : tap + 1]
        total = total + jnp.where(age >= KERNEL - 1 - tap, values, 0.0)
    out_ref[0] = total


def taps_back_kernel(
    clips, ends_ref, base_ref, prev_ref, glu_ref, taps_ref, grad_ref, normal_ref, inverse_ref, sums_ref,
    gain_ref, dglu_ref, dprev_ref, dtaps_ref, dgain_ref, dbias_ref, window, spread,
):
    count = glu_ref.shape[1]
    group = pl.program_id(1)

    @pl.when(group == 0)
    def _():
        dtaps_ref[...] = jnp.zeros_like(dtaps_ref)
        dgain_ref[...] = jnp.zeros_like(dgain_ref)
        dbias_ref[...] = jnp.zeros_like(dbias_ref)

    window[0:EDGE] = prev_ref[0].astype(F32)
    window[EDGE:] = glu_ref[0].astype(F32)
    grad, normal_part = grad_ref[0], normal_ref[0]
    dgain_ref[...] += jnp.sum(grad * normal_part, axis=0, keepdims=True)
    dbias_ref[...] += jnp.sum(grad, axis=0, keepdims=True)
    own = inverse_ref[0] * (
        grad * gain_ref[...] - sums_ref[0, :, 0:1] - normal_part * sums_ref[0, :, 1:2]
    )
    spread[0:EDGE] = jnp.zeros((EDGE, 128), F32)
    spread[EDGE : EDGE + count] = own
    spread[EDGE + count :] = jnp.zeros((EDGE, 128), F32)
    at = base_ref[0] + lax.broadcasted_iota(jnp.int32, (count, 1), 0)
    start, _ = clip_bounds(at, ends_ref, group, clips)
    age = jnp.broadcast_to(at - start, (count, 128))
    source = base_ref[0] - EDGE + lax.broadcasted_iota(jnp.int32, (count + EDGE, 1), 0)
    _, stop = clip_bounds(source, ends_ref, group, clips)
    remain = jnp.broadcast_to(stop - source, (count + EDGE, 128))
    total = jnp.zeros((count + EDGE, 128), F32)
    for tap in range(KERNEL):
        back = KERNEL - 1 - tap
        first = EDGE - back
        kept = jnp.where(age >= back, own, 0.0) * window[first : first + count]
        dtaps_ref[tap : tap + 1] += jnp.sum(kept, axis=0, keepdims=True)
        values = spread[back : back + count + EDGE] * taps_ref[tap : tap + 1]
        total = total + jnp.where(remain > back, values, 0.0)
    dprev_ref[0] = total[0:EDGE].astype(BF)
    dglu_ref[0] = total[EDGE:]


def taps_specs(count, order):
    smem = pl.BlockSpec(memory_space=pltpu.SMEM)
    lanes = pl.BlockSpec((1, count, 128), lambda *at: (at[order[0]], 0, at[order[1]]))
    edge = pl.BlockSpec((1, EDGE, 128), lambda *at: (at[order[0]], 0, at[order[1]]))
    taps = pl.BlockSpec((EDGE, 128), lambda *at: (0, at[order[1]]))
    return smem, lanes, edge, taps


def taps_forward(ends, base, prev, glu, taps):
    groups, count, width = glu.shape
    smem, lanes, edge, tap_lanes = taps_specs(count, (0, 1))
    return pl.pallas_call(
        functools.partial(taps_kernel, ends.shape[1]),
        grid=(groups, width // 128),
        in_specs=[smem, smem, edge, lanes, tap_lanes],
        out_specs=lanes,
        out_shape=jax.ShapeDtypeStruct((groups, count, width), F32),
        scratch_shapes=[pltpu.VMEM((count + EDGE, 128), F32)],
        name="taps",
    )(ends, base, prev, glu, taps)


def taps_back(ends, base, prev, glu, taps, grad, normal_part, inverse, sums, gain):
    groups, count, width = glu.shape
    smem, lanes, edge, tap_lanes = taps_specs(count, (1, 0))
    row_one = pl.BlockSpec((1, count, 1), lambda c, g: (g, 0, 0))
    row_two = pl.BlockSpec((1, count, 2), lambda c, g: (g, 0, 0))
    line = pl.BlockSpec((1, 128), lambda c, g: (0, c))
    shape = jax.ShapeDtypeStruct
    return pl.pallas_call(
        functools.partial(taps_back_kernel, ends.shape[1]),
        grid=(width // 128, groups),
        in_specs=[smem, smem, edge, lanes, tap_lanes, lanes, lanes, row_one, row_two, line],
        out_specs=[lanes, edge, tap_lanes, line, line],
        out_shape=[
            shape((groups, count, width), F32),
            shape((groups, EDGE, width), BF),
            shape((EDGE, width), F32),
            shape((1, width), F32),
            shape((1, width), F32),
        ],
        scratch_shapes=[
            pltpu.VMEM((count + EDGE, 128), F32),
            pltpu.VMEM((count + 2 * EDGE, 128), F32),
        ],
        name="taps_back",
    )(ends, base, prev, glu, taps, grad, normal_part, inverse, sums, gain)


def dot(left, right, left_axis, right_axis):
    return lax.dot_general(
        left, right, (((left_axis,), (right_axis,)), ((), ())), preferred_element_type=F32
    )


def row_major(array):
    return with_layout_constraint(array, Layout(tuple(range(array.ndim))))


def local(
    inputs,
    lengths,
    ffn_in,
    ffn_out,
    qkv_weight,
    out_weight,
    conv_in,
    conv_depth,
    conv_out,
    norm_gain,
    norm_bias,
    rel_key,
    cotangent,
):
    place = Place()
    seq_size, chips, core = place.seq_size, place.chips, place.core
    row_count, dim = inputs.shape[1:]
    hid = ffn_in.shape[3] // 2
    quarter = hid // 2
    width = dim // 2
    rows = 2 * ffn_in.shape[2]
    tap_first, tap_last = 12, 12 + KERNEL

    small = jnp.concatenate([norm_gain[0], norm_bias[0], conv_depth[0]], 0)
    small_count = small.shape[0]
    small = jnp.pad(small, ((0, 128 - small_count), (0, 0))).T
    out_rows = jnp.swapaxes(ffn_out[0], 1, 2)

    def pick(array, count, which):
        parts = array.reshape(array.shape[0], count, -1)
        return place.core_part(parts, 2, which).reshape(array.shape[0], -1)

    def ffn_parts(net, part, which):
        span = slice(part * quarter, (part + 1) * quarter)
        return [pick(ffn_in[0, net], 1, which)[:, span], pick(out_rows[net], 1, which)[:, span]]

    def attention_parts(which):
        return [
            pick(qkv_weight[0], 3, which),
            pick(conv_in[0], 2, which),
            pick(out_weight[0], 1, which),
            pick(conv_out[0], 1, which),
        ]

    def chip_block(kept, sent):
        kept, sent = jnp.concatenate(kept, 1), jnp.concatenate(sent, 1)
        return place.by_core(kept, place.sibling(sent), 0)

    other = 1 - core
    first_block = chip_block(
        ffn_parts(0, 0, core) + [small], ffn_parts(0, 0, other) + [small]
    )
    later_block = chip_block(
        ffn_parts(0, 1, core) + attention_parts(core) + ffn_parts(1, 0, core) + ffn_parts(1, 1, core),
        ffn_parts(0, 1, other)
        + attention_parts(other)
        + ffn_parts(1, 0, other)
        + ffn_parts(1, 1, other),
    )
    n_attention = 7 * width
    attention_block = later_block[:, 2 * quarter : 2 * quarter + n_attention]
    attention_all = lax.all_gather(attention_block, ("seq", "plane"), axis=0, tiled=True)
    at = [0, quarter]
    at += [2 * quarter + n_attention + part * quarter for part in range(4)]
    pieces = [later_block[:, start : start + quarter] for start in at]
    chunks = [
        (
            [first_block[:, :quarter], first_block[:, 2 * quarter :]],
            [first_block[:, quarter : 2 * quarter]],
        ),
        ([pieces[0]], [pieces[1]]),
        ([pieces[2]], [pieces[3]]),
        ([pieces[4]], [pieces[5]]),
    ]
    gathered, z_marks, firsts, seconds = [], [], [], []

    def fetch(*waits):
        index = len(gathered)
        left, right = chunks[index]
        block = tie(jnp.concatenate(left + right, 1), *z_marks[-1:], *waits)
        spread = place.swap_seq(jnp.broadcast_to(block[None], (seq_size,) + block.shape))
        z_marks.append(tip(spread))
        marks = []
        n_left = sum(part.shape[1] for part in left)
        parts = tie(spread[..., :n_left], *seconds[-1:]), tie(spread[..., n_left:], *seconds[-1:])
        fulls = [gather_plane(place, part, turn, marks) for turn, part in enumerate(parts)]
        firsts.append(marks[place.bits])
        seconds.append(marks[-1])
        gathered.append([full.reshape(dim, -1) for full in fulls])

    fetch()
    fetch()
    small_all = gathered[0][0][:, quarter:].T.astype(F32)
    gains, biases = small_all[:6, None], small_all[6:12, None]
    tap_values = place.core_part(small_all[tap_first:tap_last], 1, core)
    gain3 = place.core_part(small_all[3], 0, core)
    bias3 = place.core_part(small_all[9], 0, core)
    w_qkv = attention_all[:, : 3 * width]
    w_first = attention_all[:, 3 * width : 5 * width]
    columns = attention_all[:, 5 * width :]
    from_other = place.sibling(place.core_part(columns, 0, other))
    columns = place.core_part(columns, 0, core)
    w_out = place.by_core(columns[:, :width], from_other[:, :width], 1)
    w_second = place.by_core(columns[:, width:], from_other[:, width:], 1)

    group_lengths = jnp.concatenate([lengths, place.sibling(lengths)], 0)
    clips = group_lengths.shape[1]
    order = jnp.arange(clips)
    clip_ends = jnp.sum(
        jnp.where(order[None, :, None] >= order[None, None, :], group_lengths[:, None, :], 0), axis=2
    )
    first_row = place.seq * row_count

    def weights_of(net, part):
        left, right = gathered[2 * net + part]
        return left[:, :quarter], right

    def flat2(array):
        return array.reshape(2 * row_count, -1)

    def pair2(array):
        return array.reshape(2, row_count, -1)

    def feed_forward(normed, net):
        normed_low = flat2(place.both(normed))
        pres, acts, branch = [], [], 0.0
        for part in range(2):
            w_in, w_down = weights_of(net, part)
            pre_act = dot(normed_low, w_in, 1, 0)
            act_low = (pre_act * jax.nn.sigmoid(pre_act)).astype(BF)
            if net == 0 and part == 0:
                fetch(tip(act_low))
            branch = branch + dot(act_low, w_down, 1, 1)
            pres.append(pre_act)
            acts.append(act_low)
        return pair2(branch), (normed_low, pres, acts)

    def joined(base, share, branch, norm_index, *marks):
        received = place.from_sibling(branch)
        gain = tie(gains[norm_index], *marks)
        return add_and_norm(base, share, branch, received, gain, biases[norm_index])

    stream = inputs[0].astype(F32)
    normed = add_and_norm(stream, 0.0, None, None, gains[0], biases[0])
    branch, ffn_first = feed_forward(normed, 0)
    after_ffn, normed = joined(stream, 0.5, branch, 1)
    fetch(tip(normed))
    attn_input = flat2(place.both(normed))
    projected = pair2(dot(attn_input, w_qkv, 1, 0).astype(BF))
    from_left = place.along(projected[:, row_count - LEFT :, width:], 1)
    from_right = place.along(projected[:, :RIGHT, width:], -1)
    from_right = jnp.pad(from_right, ((0, 0), (0, LEFT - RIGHT), (0, 0)))
    relative = jnp.pad(
        jnp.concatenate([rel_key[0], rel_key[0]], 1), ((0, SPAN - rel_key.shape[1]), (0, 0))
    )
    base = jnp.reshape(first_row, (1,))
    attended, probs = attend(clip_ends, tie(base, firsts[2]), projected, from_left, from_right, relative)
    attended = flat2(attended)
    after_attn, normed = joined(after_ffn, 1.0, pair2(dot(attended, w_out, 1, 0)), 2, seconds[2], firsts[3])
    conv_input = flat2(place.both(normed))
    spread_pre = pair2(dot(conv_input, w_first, 1, 0))
    value_part, gate_sig = spread_pre[..., :width], jax.nn.sigmoid(spread_pre[..., width:])
    gated_low = (value_part * gate_sig).astype(BF)
    from_prev = place.along(gated_low[:, row_count - EDGE :], 1)
    tap_rows = jnp.pad(tap_values, ((0, EDGE - KERNEL), (0, 0)))
    filtered = taps_forward(clip_ends, base, from_prev, gated_low, tap_rows)
    normed_conv, depth_norm = split_layer_norm(place, filtered, gain3, bias3)
    swished = (normed_conv * jax.nn.sigmoid(normed_conv)).astype(BF)
    after_conv, normed = joined(after_attn, 1.0, pair2(dot(flat2(swished), w_second, 1, 0)), 4)
    branch, ffn_second = feed_forward(normed, 1)
    fourth, result = joined(after_conv, 0.5, branch, 5)
    outputs = result[None]

    def summed(terms):
        return jnp.sum(place.swap_seq(terms).astype(F32), 0)

    def scatter_early(terms):
        terms = jnp.concatenate(terms, 1)
        terms = row_major(terms.reshape(seq_size, chips * rows, terms.shape[1]))
        return row_major(lax.psum_scatter(terms, "plane", scatter_dimension=1, tiled=True))

    def plane_sums(pair, waits=(), start=()):
        parts = []
        for turn, terms in enumerate(pair):
            blocks = terms.reshape(seq_size, chips, rows, -1)
            parts.append(scatter_plane(place, blocks, turn, waits, start))
        return jnp.concatenate(parts, -1)

    gain_grads = [None] * 6
    bias_grads = [None] * 6

    def back_to(norm_index, stream_at, branch, through, share, *marks):
        received = None if through is None else place.from_sibling(branch)
        gain = tie(gains[norm_index], *marks)
        grad, low, gain_grads[norm_index], bias_grads[norm_index] = norm_and_add_back(
            stream_at, branch, received, gain, through, share
        )
        return grad, low

    def feed_back(low, net, cached):
        normed_low, pres, acts = cached
        branch_grad = flat2(place.both(low))
        pre_grads, normed_grad = [], 0.0
        for part in range(2):
            act_grad = dot(branch_grad, weights_of(net, part)[1], 1, 0)
            pre_grads.append((act_grad * swish_slope(pres[part])).astype(BF))
        for part in range(2):
            normed_grad = normed_grad + dot(pre_grads[part], weights_of(net, part)[0], 1, 1)
        return pair2(normed_grad), pre_grads, acts, normed_low, branch_grad

    def exchanged(wide):
        received = place.sibling(place.core_part(wide, 1, other))
        return place.by_core(place.core_part(wide, 1, core), received, 0)

    grad_fourth, low = back_to(5, fourth, cotangent[0], None, 0.5)
    branch, pre_grads, acts, normed_low, branch_grad = feed_back(low, 1, ffn_second)
    second_terms = [products(normed_low, branch_grad, pre_grads + acts)]
    grad_conv_out, low = back_to(4, after_conv, branch, grad_fourth, 1.0)
    branch_grad = flat2(place.both(low))
    conv_out_terms = exchanged(dot(flat2(swished), branch_grad, 0, 0).astype(BF))
    swish_grad = pair2(dot(branch_grad, w_second, 1, 1))
    swish_grad = swish_grad * swish_slope(normed_conv)
    sums = split_norm_sums(place, swish_grad, depth_norm[0], gain3)
    gated_grad, to_prev, tap_grads, gain3_grad, bias3_grad = taps_back(
        clip_ends, base, from_prev, gated_low, tap_rows, swish_grad, *depth_norm, sums, gain3[None]
    )
    to_prev = place.along(to_prev, -1).astype(F32)
    gated_grad = gated_grad + jnp.pad(to_prev, ((0, 0), (row_count - EDGE, 0), (0, 0)))
    spread_grad = flat2(
        jnp.concatenate(
            [gated_grad * gate_sig, gated_grad * value_part * gate_sig * (1.0 - gate_sig)], axis=2
        ).astype(BF)
    )
    branch = pair2(dot(spread_grad, w_first, 1, 1))
    conv_in_terms = dot(conv_input, spread_grad, 0, 0).astype(BF)
    grad_attn_out, low = back_to(2, after_attn, branch, grad_conv_out, 1.0)
    branch_grad = flat2(place.both(low))
    out_terms = exchanged(dot(attended, branch_grad, 0, 0).astype(BF))
    attended_grad = pair2(dot(branch_grad, w_out, 1, 1).astype(BF))
    query_grad, key_grad, value_grad, kl, vl, kr, vr, relative_grad = attend_back(
        projected, from_left, from_right, relative, attended_grad, probs
    )
    second_sum = summed(tie(scatter_early(second_terms), tip(query_grad)))
    to_left = place.along(jnp.concatenate([kl, vl], 2), -1).astype(F32)
    to_right = place.along(jnp.concatenate([kr[:, :RIGHT], vr[:, :RIGHT]], 2), 1).astype(F32)
    own_grad = (
        jnp.concatenate([key_grad, value_grad], 2)
        + jnp.pad(to_left, ((0, 0), (row_count - LEFT, 0), (0, 0)))
        + jnp.pad(to_right, ((0, 0), (0, row_count - RIGHT), (0, 0)))
    )
    projected_grad = flat2(jnp.concatenate([query_grad, own_grad.astype(BF)], axis=2))
    branch = pair2(dot(projected_grad, w_qkv, 1, 1))
    qkv_terms = dot(attn_input, projected_grad, 0, 0).astype(BF)
    grad_ffn_out, low = back_to(
        1, after_ffn, branch, grad_attn_out, 0.5
    )
    branch, pre_grads, acts, normed_low, branch_grad = feed_back(low, 0, ffn_first)
    downs = [dot(branch_grad, acts[part], 0, 0).astype(BF) for part in range(2)]
    ins = [dot(normed_low, pre_grads[part], 0, 0).astype(BF) for part in range(2)]
    attention_part = scatter_early([qkv_terms, conv_in_terms, out_terms, conv_out_terms])
    grad_input, _ = back_to(0, stream, branch, grad_ffn_out, 1.0)
    down_part = plane_sums(downs, (tip(ins[1]), tip(grad_input)))
    in_part = plane_sums(ins, start=(tip(down_part),))
    down_sum = summed(tie(down_part, tip(second_sum)))
    offsets = LEFT + RIGHT + 1
    relative_grad = relative_grad[:offsets, :HEAD_DIM] + relative_grad[:offsets, HEAD_DIM:]

    def spread_core(half_rows):
        return place.by_core(half_rows, jnp.zeros_like(half_rows), 1)

    gain_grads[3] = spread_core(gain3_grad)
    bias_grads[3] = spread_core(bias3_grad)
    small_grads = jnp.concatenate(
        gain_grads + bias_grads + [spread_core(tap_grads[:KERNEL])], 0
    )
    small_grads = jnp.pad(small_grads, ((0, 128 - small_count), (0, 0))).T
    rel_part = jnp.pad(relative_grad, ((0, -offsets % 8), (0, 128 - HEAD_DIM)))
    rel_part = rel_part + place.sibling(rel_part)
    current = small_grads.reshape((seq_size,) + (2,) * place.bits + (rows, 128))
    for bit in range(place.bits):
        axis = place.bits - bit
        me = place.bit(bit)
        keep = lax.dynamic_slice_in_dim(current, me, 1, axis)
        sent = lax.dynamic_slice_in_dim(current, 1 - me, 1, axis)
        got = place.hop(jnp.concatenate([sent.reshape(-1, 128), rel_part], 0), bit)
        current = keep + got[: -rel_part.shape[0]].reshape(keep.shape)
        rel_part = rel_part + got[-rel_part.shape[0] :]
    rel_all = jnp.broadcast_to(rel_part[None], (seq_size,) + rel_part.shape)
    small_total = summed(
        tie(jnp.concatenate([current.reshape(seq_size, rows, 128), rel_all], 1), tip(down_sum))
    )
    attention_sum = summed(tie(attention_part, tip(small_total)))
    in_sum = summed(tie(in_part, tip(attention_sum)))
    rel_total = small_total[rows : rows + offsets, :HEAD_DIM]
    small_total = small_total[:rows]
    small_sum = place.core_part(small_total, 0, core) + place.sibling(
        place.core_part(small_total, 0, other)
    )
    small_sum = small_sum[:, :small_count].T

    def own_rows(total, counts):
        received = place.sibling(place.core_part(total, 0, other))
        mine = place.core_part(total, 0, core)
        results, start = [], 0
        for count, n in counts:
            halves = [
                part[:, start : start + n].reshape(-1, count, n // count) for part in (mine, received)
            ]
            results.append(place.by_core(*halves, 2).reshape(mine.shape[0], 2 * n))
            start += n
        return results

    in_second, down_second = own_rows(second_sum, [(1, hid), (1, hid)])
    (down_first,) = own_rows(down_sum, [(1, hid)])
    qkv_sum, first_sum, out_sum, second_sum = own_rows(
        attention_sum, [(3, 3 * width), (2, 2 * width), (1, width), (1, width)]
    )
    (in_first,) = own_rows(in_sum, [(1, hid)])
    return (
        outputs,
        grad_input[None],
        jnp.stack([in_first, in_second])[None],
        jnp.swapaxes(jnp.stack([down_first, down_second]), 1, 2)[None],
        qkv_sum[None],
        out_sum[None],
        first_sum[None],
        small_sum[None, tap_first:tap_last],
        second_sum[None],
        small_sum[None, :6],
        small_sum[None, 6:12],
        rel_total[None],
    )


def solution(mesh):
    seq_size, fsdp_size = mesh.shape["seq"], mesh.shape["fsdp"]
    chips = Mesh(mesh.devices.reshape(seq_size, fsdp_size // 2, 2), ("seq", "plane", "core"))
    fsdp = ("plane", "core")
    spread = ("seq", "plane", "core")
    tokens = P(fsdp, "seq", None)
    split_rows = P(None, spread, None)
    split_last = P(None, None, spread)
    weights = (
        P(None, None, spread, None),
        P(None, None, None, spread),
        split_rows,
        split_rows,
        split_rows,
        split_last,
        split_rows,
        split_last,
        split_last,
        P(),
    )
    return jax.shard_map(
        local,
        mesh=chips,
        in_specs=(tokens, P(fsdp, None)) + weights + (tokens,),
        out_specs=(tokens, tokens) + weights,
        check_vma=False,
    )
```

```python
import functools

import jax
import jax.numpy as jnp
from jax import lax
from jax.experimental import pallas as pl
from jax.experimental.layout import Layout, with_layout_constraint
from jax.experimental.pallas import tpu as pltpu
from jax.sharding import Mesh
from jax.sharding import PartitionSpec as P

HEAD_DIM = 64
KERNEL = 31
LEFT = 64
RIGHT = 8
BLOCK = 128
SPAN = 256
EDGE = 32
BF = jnp.bfloat16
F32 = jnp.float32


class Place:
    def __init__(self):
        self.seq_size = lax.axis_size("seq")
        self.chips = lax.axis_size("plane")
        self.seq = lax.axis_index("seq")
        self.chip = lax.axis_index("plane")
        self.core = lax.axis_index("core")
        self.bits = self.chips.bit_length() - 1

    def sibling(self, shard):
        return lax.ppermute(shard, "core", [(0, 1), (1, 0)])

    def hop(self, shard, bit):
        return lax.ppermute(shard, "plane", [(i, i ^ (1 << bit)) for i in range(self.chips)])

    def along(self, shard, by):
        pairs = [(i, i + by) for i in range(self.seq_size) if 0 <= i + by < self.seq_size]
        return lax.ppermute(shard, "seq", pairs)

    def swap_seq(self, blocks):
        return lax.all_to_all(blocks, "seq", 0, 0, tiled=True)

    def bit(self, bit):
        return lax.rem(lax.div(self.chip, 1 << bit), 2)

    def both(self, mine):
        return jnp.stack([mine, self.sibling(mine)])

    def from_sibling(self, partial):
        return self.sibling(partial[1].astype(BF))

    def by_core(self, mine, other, axis):
        return jnp.where(
            self.core == 0,
            jnp.concatenate([mine, other], axis),
            jnp.concatenate([other, mine], axis),
        )

    def core_part(self, array, axis, which):
        size = array.shape[axis] // 2
        return lax.dynamic_slice_in_dim(array, which * size, size, axis)


def tie(array, *marks):
    ready = None
    for mark in marks:
        if mark is None:
            continue
        equal = mark == mark
        ready = equal if ready is None else jnp.logical_and(ready, equal)
    return array if ready is None else jnp.where(ready, array, jnp.zeros_like(array))


def tip(array):
    return array[(0,) * array.ndim]


def gather_plane(place, part, turn, marks):
    bits = place.bits
    current = part.reshape((part.shape[0],) + (1,) * bits + part.shape[1:])
    for step in range(bits):
        bit = (turn + step) % bits
        axis = bits - bit
        other = place.hop(current, bit)
        marks.append(tip(other))
        current = jnp.where(
            place.bit(bit) == 0,
            jnp.concatenate([current, other], axis),
            jnp.concatenate([other, current], axis),
        )
    return current.reshape((part.shape[0], place.chips) + part.shape[1:])


def scatter_plane(place, full, turn, waits, start):
    bits = place.bits
    current = full.reshape((full.shape[0],) + (2,) * bits + full.shape[2:])
    for step in range(bits):
        bit = (turn + step) % bits
        axis = bits - bit
        me = place.bit(bit)
        keep = lax.dynamic_slice_in_dim(current, me, 1, axis)
        sent = lax.dynamic_slice_in_dim(current, 1 - me, 1, axis)
        got = place.hop(tie(sent, *(waits if step == 1 else start if step == 0 else ())), bit)
        current = (keep.astype(F32) + got.astype(F32)).astype(full.dtype)
    return current.reshape((full.shape[0],) + full.shape[2:])


def clip_index(positions, ends_ref, group, clips):
    inside = jnp.zeros(positions.shape, jnp.int32)
    for clip in range(clips):
        inside = inside + (positions >= ends_ref[group, clip]).astype(jnp.int32)
    return jnp.where(positions < 0, -1, inside)


def dot_nt(left, right):
    return lax.dot_general(left, right, (((1,), (1,)), ((), ())), preferred_element_type=F32)


def dot_nn(left, right):
    return lax.dot_general(left, right, (((1,), (0,)), ((), ())), preferred_element_type=F32)


def dot_tn(left, right):
    return lax.dot_general(left, right, (((0,), (0,)), ((), ())), preferred_element_type=F32)


def band_mask(ends_ref, base_ref, block, clips):
    group = pl.program_id(0)
    start = base_ref[0] + block * BLOCK
    query_at = start + lax.broadcasted_iota(jnp.int32, (BLOCK, 1), 0)
    key_at = start - LEFT + lax.broadcasted_iota(jnp.int32, (1, SPAN), 1)
    apart = lax.broadcasted_iota(jnp.int32, (BLOCK, SPAN), 1) - lax.broadcasted_iota(
        jnp.int32, (BLOCK, SPAN), 0
    )
    query_ids = clip_index(query_at, ends_ref, group, clips)
    key_ids = clip_index(key_at, ends_ref, group, clips)
    return (apart >= 0) & (apart <= LEFT + RIGHT) & (query_ids == key_ids)


def fill_window(window, left_ref, own_ref, right_ref):
    count = own_ref.shape[1]
    window[0:LEFT] = left_ref[0]
    window[LEFT : LEFT + count] = own_ref[0]
    window[LEFT + count :] = right_ref[0]


def band_probs(query, keys, relative, mask):
    scores = dot_nt(query, keys)
    positional = pltpu.roll(dot_nt(query, relative), 0, 1, stride=1, stride_axis=0)
    scores = jnp.where(mask, (scores + positional) * HEAD_DIM ** (-0.5), -1e30)
    expanded = jnp.exp(scores - jnp.max(scores, axis=1, keepdims=True))
    return expanded / jnp.sum(expanded, axis=1, keepdims=True)


def attend_kernel(
    clips, ends_ref, base_ref, q_ref, k_ref, v_ref, kl_ref, vl_ref, kr_ref, vr_ref, rel_ref,
    out_ref, probs_ref, keys, values,
):
    fill_window(keys, kl_ref, k_ref, kr_ref)
    fill_window(values, vl_ref, v_ref, vr_ref)
    low_lane = lax.broadcasted_iota(jnp.int32, (BLOCK, 2 * HEAD_DIM), 1) < HEAD_DIM
    for block in range(q_ref.shape[1] // BLOCK):
        at = block * BLOCK
        mask = band_mask(ends_ref, base_ref, block, clips)
        query = q_ref[0, at : at + BLOCK]
        zero = jnp.zeros_like(query)
        outs = []
        queries = jnp.where(low_lane, query, zero), jnp.where(low_lane, zero, query)
        for one, query_one in enumerate(queries):
            probs = band_probs(query_one, keys[at : at + SPAN], rel_ref[...], mask).astype(BF)
            probs_ref[0, 0, block, one] = probs
            outs.append(dot_nn(probs, values[at : at + SPAN]))
        out_ref[0, at : at + BLOCK] = jnp.where(low_lane, outs[0], outs[1]).astype(BF)


def attend_back_kernel(
    q_ref, k_ref, v_ref, kl_ref, vl_ref, kr_ref, vr_ref, rel_ref, do_ref, probs_ref,
    dq_ref, dk_ref, dv_ref, dkl_ref, dvl_ref, dkr_ref, dvr_ref, drel_ref,
    keys, values, key_sum, value_sum,
):
    scale = HEAD_DIM ** (-0.5)
    count = q_ref.shape[1]
    fill_window(keys, kl_ref, k_ref, kr_ref)
    fill_window(values, vl_ref, v_ref, vr_ref)
    key_sum[...] = jnp.zeros_like(key_sum)
    value_sum[...] = jnp.zeros_like(value_sum)

    @pl.when((pl.program_id(0) == 0) & (pl.program_id(1) == 0))
    def _():
        drel_ref[...] = jnp.zeros_like(drel_ref)

    low_lane = lax.broadcasted_iota(jnp.int32, (BLOCK, 2 * HEAD_DIM), 1) < HEAD_DIM
    row = lax.broadcasted_iota(jnp.int32, (BLOCK, BLOCK), 0)
    column = lax.broadcasted_iota(jnp.int32, (BLOCK, BLOCK), 1)
    flip = (row + column == BLOCK - 1).astype(F32).astype(BF)
    for block in range(count // BLOCK):
        at = block * BLOCK
        query = q_ref[0, at : at + BLOCK]
        grad = do_ref[0, at : at + BLOCK]
        zero = jnp.zeros_like(query)
        some_keys = keys[at : at + SPAN]
        outs, key_part, value_part, rel_part = [], None, None, None
        for low in (True, False):
            pick = (lambda a: jnp.where(low_lane, a, zero)) if low else (
                lambda a: jnp.where(low_lane, zero, a)
            )
            query_one, grad_one = pick(query), pick(grad)
            probs_low = probs_ref[0, 0, block, 0 if low else 1]
            probs = probs_low.astype(F32)
            prob_grads = dot_nt(grad_one, values[at : at + SPAN])
            inner = jnp.sum(prob_grads * probs, axis=1, keepdims=True)
            score_grads = (probs * (prob_grads - inner)).astype(BF)
            turned = pltpu.roll(
                dot_nn(flip, score_grads), SPAN - BLOCK + 1, 1, stride=1, stride_axis=0
            )
            by_offset = dot_nn(flip, turned[:, :BLOCK].astype(BF)).astype(BF)
            outs.append(dot_nn(score_grads, some_keys) + dot_nn(by_offset, rel_ref[0:BLOCK]))
            parts = (
                dot_tn(score_grads, query_one),
                dot_tn(probs_low, grad_one),
                dot_tn(by_offset, query_one),
            )
            if low:
                key_part, value_part, rel_part = parts
            else:
                key_part, value_part, rel_part = (
                    key_part + parts[0],
                    value_part + parts[1],
                    rel_part + parts[2],
                )
        dq_ref[0, at : at + BLOCK] = (jnp.where(low_lane, outs[0], outs[1]) * scale).astype(BF)
        key_sum[at : at + SPAN] += key_part * scale
        value_sum[at : at + SPAN] += value_part
        drel_ref[...] += rel_part * scale
    for total, left, own, right in (
        (key_sum, dkl_ref, dk_ref, dkr_ref),
        (value_sum, dvl_ref, dv_ref, dvr_ref),
    ):
        left[0] = total[0:LEFT].astype(BF)
        own[0] = total[LEFT : LEFT + count]
        right[0] = total[LEFT + count :].astype(BF)


def attend_specs(groups, count, pairs):
    lanes = 2 * HEAD_DIM
    smem = pl.BlockSpec(memory_space=pltpu.SMEM)

    def own(at):
        return pl.BlockSpec((1, count, lanes), lambda g, h: (g, 0, at * pairs + h))

    def edge(at):
        return pl.BlockSpec((1, LEFT, lanes), lambda g, h: (g, 0, at * pairs + h))

    rel = pl.BlockSpec((SPAN, lanes), lambda g, h: (0, 0))
    probs = pl.BlockSpec(
        (1, 1, count // BLOCK, 2, BLOCK, SPAN), lambda g, h: (g, h, 0, 0, 0, 0)
    )
    specs = [smem, smem, own(0), own(1), own(2), edge(0), edge(1), edge(0), edge(1), rel]
    return specs, own, edge, probs


def attend(ends, base, projected, left, right, relative):
    groups, count, _ = projected.shape
    pairs = projected.shape[2] // (6 * HEAD_DIM)
    specs, own, _, probs = attend_specs(groups, count, pairs)
    window = pltpu.VMEM((count + 2 * LEFT, 2 * HEAD_DIM), BF)
    return pl.pallas_call(
        functools.partial(attend_kernel, ends.shape[1]),
        grid=(groups, pairs),
        in_specs=specs,
        out_specs=[own(0), probs],
        out_shape=[
            jax.ShapeDtypeStruct((groups, count, projected.shape[2] // 3), BF),
            jax.ShapeDtypeStruct((groups, pairs, count // BLOCK, 2, BLOCK, SPAN), BF),
        ],
        scratch_shapes=[window, window],
        name="attend",
    )(ends, base, projected, projected, projected, left, left, right, right, relative)


def attend_back(projected, left, right, relative, grad, probs):
    groups, count, _ = projected.shape
    width = projected.shape[2] // 3
    pairs = width // (2 * HEAD_DIM)
    specs, own, edge, saved = attend_specs(groups, count, pairs)
    window = pltpu.VMEM((count + 2 * LEFT, 2 * HEAD_DIM), BF)
    total = pltpu.VMEM((count + 2 * LEFT, 2 * HEAD_DIM), F32)
    rel_sum = pl.BlockSpec((BLOCK, 2 * HEAD_DIM), lambda g, h: (0, 0))
    shape = lambda rows, dtype: jax.ShapeDtypeStruct((groups, rows, width), dtype)
    return pl.pallas_call(
        attend_back_kernel,
        grid=(groups, pairs),
        in_specs=specs[2:] + [own(0), saved],
        out_specs=[own(0), own(0), own(0), edge(0), edge(0), edge(0), edge(0), rel_sum],
        out_shape=[
            shape(count, BF),
            shape(count, F32),
            shape(count, F32),
            shape(LEFT, BF),
            shape(LEFT, BF),
            shape(LEFT, BF),
            shape(LEFT, BF),
            jax.ShapeDtypeStruct((BLOCK, 2 * HEAD_DIM), F32),
        ],
        scratch_shapes=[window, window, total, total],
        name="attend_back",
    )(projected, projected, projected, left, left, right, right, relative, grad, probs)


def products_kernel(steps, first_ref, second_ref, *refs):
    right_refs, out_ref, turned = refs[:-2], refs[-2], refs[-1]
    at = pl.program_id(0)

    @pl.when(at == 0)
    def _():
        turned[...] = first_ref[...].T

    @pl.when(at == 2 * steps)
    def _():
        turned[...] = second_ref[...].T

    for number, right_ref in enumerate(right_refs):

        @pl.when((at >= number * steps) & (at < (number + 1) * steps))
        def _(right_ref=right_ref):
            out_ref[...] = dot_nn(turned[...], right_ref[...]).astype(BF)


def products(first, second, rights):
    count, dim = first.shape
    step = 1024
    steps = rights[0].shape[1] // step
    whole = pl.BlockSpec((count, dim), lambda i: (0, 0))

    def part(number):
        return pl.BlockSpec(
            (count, step), lambda i: (0, jnp.clip(i - number * steps, 0, steps - 1))
        )

    return pl.pallas_call(
        functools.partial(products_kernel, steps),
        grid=(4 * steps,),
        in_specs=[whole, whole] + [part(number) for number in range(4)],
        out_specs=pl.BlockSpec((dim, step), lambda i: (0, i)),
        out_shape=jax.ShapeDtypeStruct((dim, 4 * steps * step), BF),
        scratch_shapes=[pltpu.VMEM((dim, count), BF)],
        name="products",
    )(first, second, *rights)


def norm_parts(values):
    centered = values - jnp.mean(values, axis=1, keepdims=True)
    variance = jnp.mean(centered * centered, axis=1, keepdims=True)
    inverse = lax.rsqrt(variance + 1e-05)
    return centered * inverse, inverse


def norm_kernel(share, *refs):
    if share:
        base_ref, own_ref, other_ref, gain_ref, bias_ref, stream_ref, low_ref = refs
        stream = base_ref[...] + share * (own_ref[0] + other_ref[...].astype(F32))
        stream_ref[...] = stream
    else:
        base_ref, gain_ref, bias_ref, low_ref = refs
        stream = base_ref[...]
    normal_part, _ = norm_parts(stream)
    low_ref[...] = (normal_part * gain_ref[...] + bias_ref[...]).astype(BF)


def norm_back_kernel(share, scale, *refs):
    if share:
        stream_ref, own_ref, other_ref, gain_ref, through_ref, grad_ref, low_ref = refs[:7]
        gradient = own_ref[0] + other_ref[...].astype(F32)
    else:
        stream_ref, own_ref, gain_ref, grad_ref, low_ref = refs[:5]
        gradient = own_ref[...].astype(F32)
    gain_grad_ref, bias_grad_ref = refs[-2:]
    normal_part, inverse = norm_parts(stream_ref[...])
    scaled = gradient * gain_ref[...]
    inner = jnp.mean(scaled * normal_part, axis=1, keepdims=True)
    total = inverse * (scaled - jnp.mean(scaled, axis=1, keepdims=True) - normal_part * inner)
    if share:
        total = total + through_ref[...]
    grad_ref[...] = total
    low_ref[...] = (scale * total).astype(BF)

    @pl.when(pl.program_id(0) == 0)
    def _():
        gain_grad_ref[...] = jnp.zeros_like(gain_grad_ref)
        bias_grad_ref[...] = jnp.zeros_like(bias_grad_ref)

    gain_grad_ref[...] += jnp.sum(gradient * normal_part, axis=0, keepdims=True)
    bias_grad_ref[...] += jnp.sum(gradient, axis=0, keepdims=True)


def row_specs(dim):
    step = 128
    rows = pl.BlockSpec((step, dim), lambda i: (i, 0))
    first = pl.BlockSpec((1, step, dim), lambda i: (0, i, 0))
    line = pl.BlockSpec((1, dim), lambda i: (0, 0))
    return step, rows, first, line


def add_and_norm(base, share, own, other, gain, bias):
    count, dim = base.shape
    step, rows, first, line = row_specs(dim)
    low = jax.ShapeDtypeStruct((count, dim), BF)
    if not share:
        return pl.pallas_call(
            functools.partial(norm_kernel, share),
            grid=(count // step,),
            in_specs=[rows, line, line],
            out_specs=rows,
            out_shape=low,
            name="norm",
        )(base, gain, bias)
    return pl.pallas_call(
        functools.partial(norm_kernel, share),
        grid=(count // step,),
        in_specs=[rows, first, rows, line, line],
        out_specs=[rows, rows],
        out_shape=[jax.ShapeDtypeStruct((count, dim), F32), low],
        name="add_and_norm",
    )(base, own, other, gain, bias)


def norm_and_add_back(stream, own, other, gain, through, scale):
    count, dim = stream.shape
    step, rows, first, line = row_specs(dim)
    share = through is not None
    specs = [rows, first, rows, line, rows] if share else [rows, rows, line]
    args = (stream, own, other, gain, through) if share else (stream, own, gain)
    return pl.pallas_call(
        functools.partial(norm_back_kernel, share, scale),
        grid=(count // step,),
        in_specs=specs,
        out_specs=[rows, rows, line, line],
        out_shape=[
            jax.ShapeDtypeStruct((count, dim), F32),
            jax.ShapeDtypeStruct((count, dim), BF),
            jax.ShapeDtypeStruct((1, dim), F32),
            jax.ShapeDtypeStruct((1, dim), F32),
        ],
        name="norm_back",
    )(*args)


def split_layer_norm(place, values, gain_row, bias_row):
    count = values.shape[-1]
    own_mean = jnp.mean(values, axis=-1, keepdims=True)
    own_square = jnp.sum((values - own_mean) ** 2, axis=-1, keepdims=True)
    stats = jnp.concatenate([own_mean, own_square], -1)
    others = place.sibling(stats)[::-1]
    mean = 0.5 * (own_mean + others[..., :1])
    square = own_square + others[..., 1:]
    square = square + count * ((own_mean - mean) ** 2 + (others[..., :1] - mean) ** 2)
    inverse = lax.rsqrt(square / (2 * count) + 1e-05)
    normal_part = (values - mean) * inverse
    return (normal_part * gain_row + bias_row, (normal_part, inverse))


def split_norm_sums(place, gradient, normal_part, gain_row):
    scaled = gradient * gain_row
    sums = jnp.concatenate(
        [
            jnp.sum(scaled, axis=-1, keepdims=True),
            jnp.sum(scaled * normal_part, axis=-1, keepdims=True),
        ],
        -1,
    )
    return (sums + place.sibling(sums)[::-1]) / (2 * gradient.shape[-1])


def swish_slope(values):
    sigmoid_val = jax.nn.sigmoid(values)
    return sigmoid_val * (1.0 + values * (1.0 - sigmoid_val))


def clip_bounds(positions, ends_ref, group, clips):
    start = jnp.zeros(positions.shape, jnp.int32)
    stop = jnp.full(positions.shape, 1 << 30, jnp.int32)
    for clip in range(clips):
        end = ends_ref[group, clip]
        start = jnp.maximum(start, jnp.where(positions >= end, end, 0))
        stop = jnp.minimum(stop, jnp.where(positions < end, end, 1 << 30))
    return start, jnp.where(positions < 0, positions, stop)


def taps_kernel(clips, ends_ref, base_ref, prev_ref, glu_ref, taps_ref, out_ref, window):
    count = glu_ref.shape[1]
    group = pl.program_id(0)
    window[0:EDGE] = prev_ref[0].astype(F32)
    window[EDGE:] = glu_ref[0].astype(F32)
    at = base_ref[0] + lax.broadcasted_iota(jnp.int32, (count, 1), 0)
    start, _ = clip_bounds(at, ends_ref, group, clips)
    age = jnp.broadcast_to(at - start, (count, 128))
    total = jnp.zeros((count, 128), F32)
    for tap in range(KERNEL):
        first = tap + EDGE - KERNEL + 1
        values = window[first : first + count] * taps_ref[tap : tap + 1]
        total = total + jnp.where(age >= KERNEL - 1 - tap, values, 0.0)
    out_ref[0] = total


def taps_back_kernel(
    clips, ends_ref, base_ref, prev_ref, glu_ref, taps_ref, grad_ref, normal_ref, inverse_ref, sums_ref,
    gain_ref, dglu_ref, dprev_ref, dtaps_ref, dgain_ref, dbias_ref, window, spread,
):
    count = glu_ref.shape[1]
    group = pl.program_id(1)

    @pl.when(group == 0)
    def _():
        dtaps_ref[...] = jnp.zeros_like(dtaps_ref)
        dgain_ref[...] = jnp.zeros_like(dgain_ref)
        dbias_ref[...] = jnp.zeros_like(dbias_ref)

    window[0:EDGE] = prev_ref[0].astype(F32)
    window[EDGE:] = glu_ref[0].astype(F32)
    grad, normal_part = grad_ref[0], normal_ref[0]
    dgain_ref[...] += jnp.sum(grad * normal_part, axis=0, keepdims=True)
    dbias_ref[...] += jnp.sum(grad, axis=0, keepdims=True)
    own = inverse_ref[0] * (
        grad * gain_ref[...] - sums_ref[0, :, 0:1] - normal_part * sums_ref[0, :, 1:2]
    )
    spread[0:EDGE] = jnp.zeros((EDGE, 128), F32)
    spread[EDGE : EDGE + count] = own
    spread[EDGE + count :] = jnp.zeros((EDGE, 128), F32)
    at = base_ref[0] + lax.broadcasted_iota(jnp.int32, (count, 1), 0)
    start, _ = clip_bounds(at, ends_ref, group, clips)
    age = jnp.broadcast_to(at - start, (count, 128))
    source = base_ref[0] - EDGE + lax.broadcasted_iota(jnp.int32, (count + EDGE, 1), 0)
    _, stop = clip_bounds(source, ends_ref, group, clips)
    remain = jnp.broadcast_to(stop - source, (count + EDGE, 128))
    total = jnp.zeros((count + EDGE, 128), F32)
    for tap in range(KERNEL):
        back = KERNEL - 1 - tap
        first = EDGE - back
        kept = jnp.where(age >= back, own, 0.0) * window[first : first + count]
        dtaps_ref[tap : tap + 1] += jnp.sum(kept, axis=0, keepdims=True)
        values = spread[back : back + count + EDGE] * taps_ref[tap : tap + 1]
        total = total + jnp.where(remain > back, values, 0.0)
    dprev_ref[0] = total[0:EDGE].astype(BF)
    dglu_ref[0] = total[EDGE:]


def taps_specs(count, order):
    smem = pl.BlockSpec(memory_space=pltpu.SMEM)
    lanes = pl.BlockSpec((1, count, 128), lambda *at: (at[order[0]], 0, at[order[1]]))
    edge = pl.BlockSpec((1, EDGE, 128), lambda *at: (at[order[0]], 0, at[order[1]]))
    taps = pl.BlockSpec((EDGE, 128), lambda *at: (0, at[order[1]]))
    return smem, lanes, edge, taps


def taps_forward(ends, base, prev, glu, taps):
    groups, count, width = glu.shape
    smem, lanes, edge, tap_lanes = taps_specs(count, (0, 1))
    return pl.pallas_call(
        functools.partial(taps_kernel, ends.shape[1]),
        grid=(groups, width // 128),
        in_specs=[smem, smem, edge, lanes, tap_lanes],
        out_specs=lanes,
        out_shape=jax.ShapeDtypeStruct((groups, count, width), F32),
        scratch_shapes=[pltpu.VMEM((count + EDGE, 128), F32)],
        name="taps",
    )(ends, base, prev, glu, taps)


def taps_back(ends, base, prev, glu, taps, grad, normal_part, inverse, sums, gain):
    groups, count, width = glu.shape
    smem, lanes, edge, tap_lanes = taps_specs(count, (1, 0))
    row_one = pl.BlockSpec((1, count, 1), lambda c, g: (g, 0, 0))
    row_two = pl.BlockSpec((1, count, 2), lambda c, g: (g, 0, 0))
    line = pl.BlockSpec((1, 128), lambda c, g: (0, c))
    shape = jax.ShapeDtypeStruct
    return pl.pallas_call(
        functools.partial(taps_back_kernel, ends.shape[1]),
        grid=(width // 128, groups),
        in_specs=[smem, smem, edge, lanes, tap_lanes, lanes, lanes, row_one, row_two, line],
        out_specs=[lanes, edge, tap_lanes, line, line],
        out_shape=[
            shape((groups, count, width), F32),
            shape((groups, EDGE, width), BF),
            shape((EDGE, width), F32),
            shape((1, width), F32),
            shape((1, width), F32),
        ],
        scratch_shapes=[
            pltpu.VMEM((count + EDGE, 128), F32),
            pltpu.VMEM((count + 2 * EDGE, 128), F32),
        ],
        name="taps_back",
    )(ends, base, prev, glu, taps, grad, normal_part, inverse, sums, gain)


def dot(left, right, left_axis, right_axis):
    return lax.dot_general(
        left, right, (((left_axis,), (right_axis,)), ((), ())), preferred_element_type=F32
    )


def row_major(array):
    return with_layout_constraint(array, Layout(tuple(range(array.ndim))))


def local(
    inputs,
    lengths,
    ffn_in,
    ffn_out,
    qkv_weight,
    out_weight,
    conv_in,
    conv_depth,
    conv_out,
    norm_gain,
    norm_bias,
    rel_key,
    cotangent,
):
    place = Place()
    seq_size, chips, core = place.seq_size, place.chips, place.core
    row_count, dim = inputs.shape[1:]
    hid = ffn_in.shape[3] // 2
    quarter = hid // 2
    width = dim // 2
    rows = 2 * ffn_in.shape[2]
    tap_first, tap_last = 12, 12 + KERNEL

    small = jnp.concatenate([norm_gain[0], norm_bias[0], conv_depth[0]], 0)
    small_count = small.shape[0]
    small = jnp.pad(small, ((0, 128 - small_count), (0, 0))).T
    out_rows = jnp.swapaxes(ffn_out[0], 1, 2)

    def pick(array, count, which):
        parts = array.reshape(array.shape[0], count, -1)
        return place.core_part(parts, 2, which).reshape(array.shape[0], -1)

    def ffn_parts(net, part, which):
        span = slice(part * quarter, (part + 1) * quarter)
        return [pick(ffn_in[0, net], 1, which)[:, span], pick(out_rows[net], 1, which)[:, span]]

    def attention_parts(which):
        return [
            pick(qkv_weight[0], 3, which),
            pick(conv_in[0], 2, which),
            pick(out_weight[0], 1, which),
            pick(conv_out[0], 1, which),
        ]

    def chip_block(kept, sent):
        kept, sent = jnp.concatenate(kept, 1), jnp.concatenate(sent, 1)
        return place.by_core(kept, place.sibling(sent), 0)

    other = 1 - core
    first_block = chip_block(
        ffn_parts(0, 0, core) + [small], ffn_parts(0, 0, other) + [small]
    )
    later_block = chip_block(
        ffn_parts(0, 1, core) + attention_parts(core) + ffn_parts(1, 0, core) + ffn_parts(1, 1, core),
        ffn_parts(0, 1, other)
        + attention_parts(other)
        + ffn_parts(1, 0, other)
        + ffn_parts(1, 1, other),
    )
    n_attention = 7 * width
    attention_block = later_block[:, 2 * quarter : 2 * quarter + n_attention]
    attention_all = lax.all_gather(attention_block, ("seq", "plane"), axis=0, tiled=True)
    at = [0, quarter]
    at += [2 * quarter + n_attention + part * quarter for part in range(4)]
    pieces = [later_block[:, start : start + quarter] for start in at]
    chunks = [
        (
            [first_block[:, :quarter], first_block[:, 2 * quarter :]],
            [first_block[:, quarter : 2 * quarter]],
        ),
        ([pieces[0]], [pieces[1]]),
        ([pieces[2]], [pieces[3]]),
        ([pieces[4]], [pieces[5]]),
    ]
    gathered, z_marks, firsts, seconds = [], [], [], []

    def fetch(*waits):
        index = len(gathered)
        left, right = chunks[index]
        block = tie(jnp.concatenate(left + right, 1), *z_marks[-1:], *waits)
        spread = place.swap_seq(jnp.broadcast_to(block[None], (seq_size,) + block.shape))
        z_marks.append(tip(spread))
        marks = []
        n_left = sum(part.shape[1] for part in left)
        parts = tie(spread[..., :n_left], *seconds[-1:]), tie(spread[..., n_left:], *seconds[-1:])
        fulls = [gather_plane(place, part, turn, marks) for turn, part in enumerate(parts)]
        firsts.append(marks[place.bits])
        seconds.append(marks[-1])
        gathered.append([full.reshape(dim, -1) for full in fulls])

    fetch()
    fetch()
    small_all = gathered[0][0][:, quarter:].T.astype(F32)
    gains, biases = small_all[:6, None], small_all[6:12, None]
    tap_values = place.core_part(small_all[tap_first:tap_last], 1, core)
    gain3 = place.core_part(small_all[3], 0, core)
    bias3 = place.core_part(small_all[9], 0, core)
    w_qkv = attention_all[:, : 3 * width]
    w_first = attention_all[:, 3 * width : 5 * width]
    columns = attention_all[:, 5 * width :]
    from_other = place.sibling(place.core_part(columns, 0, other))
    columns = place.core_part(columns, 0, core)
    w_out = place.by_core(columns[:, :width], from_other[:, :width], 1)
    w_second = place.by_core(columns[:, width:], from_other[:, width:], 1)

    group_lengths = jnp.concatenate([lengths, place.sibling(lengths)], 0)
    clips = group_lengths.shape[1]
    order = jnp.arange(clips)
    clip_ends = jnp.sum(
        jnp.where(order[None, :, None] >= order[None, None, :], group_lengths[:, None, :], 0), axis=2
    )
    first_row = place.seq * row_count

    def weights_of(net, part):
        left, right = gathered[2 * net + part]
        return left[:, :quarter], right

    def flat2(array):
        return array.reshape(2 * row_count, -1)

    def pair2(array):
        return array.reshape(2, row_count, -1)

    def feed_forward(normed, net):
        normed_low = flat2(place.both(normed))
        pres, acts, branch = [], [], 0.0
        for part in range(2):
            w_in, w_down = weights_of(net, part)
            pre_act = dot(normed_low, w_in, 1, 0)
            act_low = (pre_act * jax.nn.sigmoid(pre_act)).astype(BF)
            if net == 0 and part == 0:
                fetch(tip(act_low))
            branch = branch + dot(act_low, w_down, 1, 1)
            pres.append(pre_act)
            acts.append(act_low)
        return pair2(branch), (normed_low, pres, acts)

    def joined(base, share, branch, norm_index, *marks):
        received = place.from_sibling(branch)
        gain = tie(gains[norm_index], *marks)
        return add_and_norm(base, share, branch, received, gain, biases[norm_index])

    stream = inputs[0].astype(F32)
    normed = add_and_norm(stream, 0.0, None, None, gains[0], biases[0])
    branch, ffn_first = feed_forward(normed, 0)
    after_ffn, normed = joined(stream, 0.5, branch, 1)
    fetch(tip(normed))
    attn_input = flat2(place.both(normed))
    projected = pair2(dot(attn_input, w_qkv, 1, 0).astype(BF))
    from_left = place.along(projected[:, row_count - LEFT :, width:], 1)
    from_right = place.along(projected[:, :RIGHT, width:], -1)
    from_right = jnp.pad(from_right, ((0, 0), (0, LEFT - RIGHT), (0, 0)))
    relative = jnp.pad(
        jnp.concatenate([rel_key[0], rel_key[0]], 1), ((0, SPAN - rel_key.shape[1]), (0, 0))
    )
    base = jnp.reshape(first_row, (1,))
    attended, probs = attend(clip_ends, tie(base, firsts[2]), projected, from_left, from_right, relative)
    attended = flat2(attended)
    after_attn, normed = joined(after_ffn, 1.0, pair2(dot(attended, w_out, 1, 0)), 2, seconds[2], firsts[3])
    conv_input = flat2(place.both(normed))
    spread_pre = pair2(dot(conv_input, w_first, 1, 0))
    value_part, gate_sig = spread_pre[..., :width], jax.nn.sigmoid(spread_pre[..., width:])
    gated_low = (value_part * gate_sig).astype(BF)
    from_prev = place.along(gated_low[:, row_count - EDGE :], 1)
    tap_rows = jnp.pad(tap_values, ((0, EDGE - KERNEL), (0, 0)))
    filtered = taps_forward(clip_ends, base, from_prev, gated_low, tap_rows)
    normed_conv, depth_norm = split_layer_norm(place, filtered, gain3, bias3)
    swished = (normed_conv * jax.nn.sigmoid(normed_conv)).astype(BF)
    after_conv, normed = joined(after_attn, 1.0, pair2(dot(flat2(swished), w_second, 1, 0)), 4)
    branch, ffn_second = feed_forward(normed, 1)
    fourth, result = joined(after_conv, 0.5, branch, 5)
    outputs = result[None]

    def summed(terms):
        return jnp.sum(place.swap_seq(terms).astype(F32), 0)

    def scatter_early(terms):
        terms = jnp.concatenate(terms, 1)
        terms = row_major(terms.reshape(seq_size, chips * rows, terms.shape[1]))
        return row_major(lax.psum_scatter(terms, "plane", scatter_dimension=1, tiled=True))

    def plane_sums(pair, waits=(), start=()):
        parts = []
        for turn, terms in enumerate(pair):
            blocks = terms.reshape(seq_size, chips, rows, -1)
            parts.append(scatter_plane(place, blocks, turn, waits, start))
        return jnp.concatenate(parts, -1)

    gain_grads = [None] * 6
    bias_grads = [None] * 6

    def back_to(norm_index, stream_at, branch, through, share, *marks):
        received = None if through is None else place.from_sibling(branch)
        gain = tie(gains[norm_index], *marks)
        grad, low, gain_grads[norm_index], bias_grads[norm_index] = norm_and_add_back(
            stream_at, branch, received, gain, through, share
        )
        return grad, low

    def feed_back(low, net, cached):
        normed_low, pres, acts = cached
        branch_grad = flat2(place.both(low))
        pre_grads, normed_grad = [], 0.0
        for part in range(2):
            act_grad = dot(branch_grad, weights_of(net, part)[1], 1, 0)
            pre_grads.append((act_grad * swish_slope(pres[part])).astype(BF))
        for part in range(2):
            normed_grad = normed_grad + dot(pre_grads[part], weights_of(net, part)[0], 1, 1)
        return pair2(normed_grad), pre_grads, acts, normed_low, branch_grad

    def exchanged(wide):
        received = place.sibling(place.core_part(wide, 1, other))
        return place.by_core(place.core_part(wide, 1, core), received, 0)

    grad_fourth, low = back_to(5, fourth, cotangent[0], None, 0.5)
    branch, pre_grads, acts, normed_low, branch_grad = feed_back(low, 1, ffn_second)
    second_terms = [products(normed_low, branch_grad, pre_grads + acts)]
    grad_conv_out, low = back_to(4, after_conv, branch, grad_fourth, 1.0)
    branch_grad = flat2(place.both(low))
    conv_out_terms = exchanged(dot(flat2(swished), branch_grad, 0, 0).astype(BF))
    swish_grad = pair2(dot(branch_grad, w_second, 1, 1))
    swish_grad = swish_grad * swish_slope(normed_conv)
    sums = split_norm_sums(place, swish_grad, depth_norm[0], gain3)
    gated_grad, to_prev, tap_grads, gain3_grad, bias3_grad = taps_back(
        clip_ends, base, from_prev, gated_low, tap_rows, swish_grad, *depth_norm, sums, gain3[None]
    )
    to_prev = place.along(to_prev, -1).astype(F32)
    gated_grad = gated_grad + jnp.pad(to_prev, ((0, 0), (row_count - EDGE, 0), (0, 0)))
    spread_grad = flat2(
        jnp.concatenate(
            [gated_grad * gate_sig, gated_grad * value_part * gate_sig * (1.0 - gate_sig)], axis=2
        ).astype(BF)
    )
    branch = pair2(dot(spread_grad, w_first, 1, 1))
    conv_in_terms = dot(conv_input, spread_grad, 0, 0).astype(BF)
    grad_attn_out, low = back_to(2, after_attn, branch, grad_conv_out, 1.0)
    branch_grad = flat2(place.both(low))
    out_terms = exchanged(dot(attended, branch_grad, 0, 0).astype(BF))
    attended_grad = pair2(dot(branch_grad, w_out, 1, 1).astype(BF))
    query_grad, key_grad, value_grad, kl, vl, kr, vr, relative_grad = attend_back(
        projected, from_left, from_right, relative, attended_grad, probs
    )
    second_sum = summed(tie(scatter_early(second_terms), tip(query_grad)))
    to_left = place.along(jnp.concatenate([kl, vl], 2), -1).astype(F32)
    to_right = place.along(jnp.concatenate([kr[:, :RIGHT], vr[:, :RIGHT]], 2), 1).astype(F32)
    own_grad = (
        jnp.concatenate([key_grad, value_grad], 2)
        + jnp.pad(to_left, ((0, 0), (row_count - LEFT, 0), (0, 0)))
        + jnp.pad(to_right, ((0, 0), (0, row_count - RIGHT), (0, 0)))
    )
    projected_grad = flat2(jnp.concatenate([query_grad, own_grad.astype(BF)], axis=2))
    branch = pair2(dot(projected_grad, w_qkv, 1, 1))
    qkv_terms = dot(attn_input, projected_grad, 0, 0).astype(BF)
    grad_ffn_out, low = back_to(
        1, after_ffn, branch, grad_attn_out, 0.5
    )
    branch, pre_grads, acts, normed_low, branch_grad = feed_back(low, 0, ffn_first)
    downs = [dot(branch_grad, acts[part], 0, 0).astype(BF) for part in range(2)]
    ins = [dot(normed_low, pre_grads[part], 0, 0).astype(BF) for part in range(2)]
    attention_part = scatter_early([qkv_terms, conv_in_terms, out_terms, conv_out_terms])
    grad_input, _ = back_to(0, stream, branch, grad_ffn_out, 1.0)
    down_part = plane_sums(downs, (tip(ins[1]), tip(grad_input)))
    in_part = plane_sums(ins, start=(tip(down_part),))
    down_sum = summed(tie(down_part, tip(second_sum)))
    offsets = LEFT + RIGHT + 1
    relative_grad = relative_grad[:offsets, :HEAD_DIM] + relative_grad[:offsets, HEAD_DIM:]

    def spread_core(half_rows):
        return place.by_core(half_rows, jnp.zeros_like(half_rows), 1)

    gain_grads[3] = spread_core(gain3_grad)
    bias_grads[3] = spread_core(bias3_grad)
    small_grads = jnp.concatenate(
        gain_grads + bias_grads + [spread_core(tap_grads[:KERNEL])], 0
    )
    small_grads = jnp.pad(small_grads, ((0, 128 - small_count), (0, 0))).T
    rel_part = jnp.pad(relative_grad, ((0, -offsets % 8), (0, 128 - HEAD_DIM)))
    rel_part = rel_part + place.sibling(rel_part)
    current = small_grads.reshape((seq_size,) + (2,) * place.bits + (rows, 128))
    for bit in range(place.bits):
        axis = place.bits - bit
        me = place.bit(bit)
        keep = lax.dynamic_slice_in_dim(current, me, 1, axis)
        sent = lax.dynamic_slice_in_dim(current, 1 - me, 1, axis)
        got = place.hop(jnp.concatenate([sent.reshape(-1, 128), rel_part], 0), bit)
        current = keep + got[: -rel_part.shape[0]].reshape(keep.shape)
        rel_part = rel_part + got[-rel_part.shape[0] :]
    rel_all = jnp.broadcast_to(rel_part[None], (seq_size,) + rel_part.shape)
    small_total = summed(
        tie(jnp.concatenate([current.reshape(seq_size, rows, 128), rel_all], 1), tip(down_sum))
    )
    attention_sum = summed(tie(attention_part, tip(small_total)))
    in_sum = summed(tie(in_part, tip(attention_sum)))
    rel_total = small_total[rows : rows + offsets, :HEAD_DIM]
    small_total = small_total[:rows]
    small_sum = place.core_part(small_total, 0, core) + place.sibling(
        place.core_part(small_total, 0, other)
    )
    small_sum = small_sum[:, :small_count].T

    def own_rows(total, counts):
        received = place.sibling(place.core_part(total, 0, other))
        mine = place.core_part(total, 0, core)
        results, start = [], 0
        for count, n in counts:
            halves = [
                part[:, start : start + n].reshape(-1, count, n // count) for part in (mine, received)
            ]
            results.append(place.by_core(*halves, 2).reshape(mine.shape[0], 2 * n))
            start += n
        return results

    in_second, down_second = own_rows(second_sum, [(1, hid), (1, hid)])
    (down_first,) = own_rows(down_sum, [(1, hid)])
    qkv_sum, first_sum, out_sum, second_sum = own_rows(
        attention_sum, [(3, 3 * width), (2, 2 * width), (1, width), (1, width)]
    )
    (in_first,) = own_rows(in_sum, [(1, hid)])
    return (
        outputs,
        grad_input[None],
        jnp.stack([in_first, in_second])[None],
        jnp.swapaxes(jnp.stack([down_first, down_second]), 1, 2)[None],
        qkv_sum[None],
        out_sum[None],
        first_sum[None],
        small_sum[None, tap_first:tap_last],
        second_sum[None],
        small_sum[None, :6],
        small_sum[None, 6:12],
        rel_total[None],
    )


def solution(mesh):
    seq_size, fsdp_size = mesh.shape["seq"], mesh.shape["fsdp"]
    chips = Mesh(mesh.devices.reshape(seq_size, fsdp_size // 2, 2), ("seq", "plane", "core"))
    fsdp = ("plane", "core")
    spread = ("seq", "plane", "core")
    tokens = P(fsdp, "seq", None)
    split_rows = P(None, spread, None)
    split_last = P(None, None, spread)
    weights = (
        P(None, None, spread, None),
        P(None, None, None, spread),
        split_rows,
        split_rows,
        split_rows,
        split_last,
        split_rows,
        split_last,
        split_last,
        P(),
    )
    return jax.shard_map(
        local,
        mesh=chips,
        in_specs=(tokens, P(fsdp, None)) + weights + (tokens,),
        out_specs=(tokens, tokens) + weights,
        check_vma=False,
    )
```

```python
import functools

import jax
import jax.numpy as jnp
from jax import lax
from jax.experimental import pallas as pl
from jax.experimental.layout import Layout, with_layout_constraint
from jax.experimental.pallas import tpu as pltpu
from jax.sharding import Mesh
from jax.sharding import PartitionSpec as P

HEAD_DIM = 64
KERNEL = 31
LEFT = 64
RIGHT = 8
BLOCK = 128
SPAN = 256
EDGE = 32
BF = jnp.bfloat16
F32 = jnp.float32


class Place:
    def __init__(self):
        self.seq_size = lax.axis_size("seq")
        self.chips = lax.axis_size("plane")
        self.seq = lax.axis_index("seq")
        self.chip = lax.axis_index("plane")
        self.core = lax.axis_index("core")
        self.bits = self.chips.bit_length() - 1

    def sibling(self, shard):
        return lax.ppermute(shard, "core", [(0, 1), (1, 0)])

    def hop(self, shard, bit):
        return lax.ppermute(shard, "plane", [(i, i ^ (1 << bit)) for i in range(self.chips)])

    def along(self, shard, by):
        pairs = [(i, i + by) for i in range(self.seq_size) if 0 <= i + by < self.seq_size]
        return lax.ppermute(shard, "seq", pairs)

    def swap_seq(self, blocks):
        return lax.all_to_all(blocks, "seq", 0, 0, tiled=True)

    def bit(self, bit):
        return lax.rem(lax.div(self.chip, 1 << bit), 2)

    def both(self, mine):
        return jnp.stack([mine, self.sibling(mine)])

    def from_sibling(self, partial):
        return self.sibling(partial[1].astype(BF))

    def by_core(self, mine, other, axis):
        return jnp.where(
            self.core == 0,
            jnp.concatenate([mine, other], axis),
            jnp.concatenate([other, mine], axis),
        )

    def core_part(self, array, axis, which):
        size = array.shape[axis] // 2
        return lax.dynamic_slice_in_dim(array, which * size, size, axis)


def tie(array, *marks):
    ready = None
    for mark in marks:
        if mark is None:
            continue
        equal = mark == mark
        ready = equal if ready is None else jnp.logical_and(ready, equal)
    return array if ready is None else jnp.where(ready, array, jnp.zeros_like(array))


def tip(array):
    return array[(0,) * array.ndim]


def gather_plane(place, part, turn, marks):
    bits = place.bits
    current = part.reshape((part.shape[0],) + (1,) * bits + part.shape[1:])
    for step in range(bits):
        bit = (turn + step) % bits
        axis = bits - bit
        other = place.hop(current, bit)
        marks.append(tip(other))
        current = jnp.where(
            place.bit(bit) == 0,
            jnp.concatenate([current, other], axis),
            jnp.concatenate([other, current], axis),
        )
    return current.reshape((part.shape[0], place.chips) + part.shape[1:])


def scatter_plane(place, full, turn, waits, start):
    bits = place.bits
    current = full.reshape((full.shape[0],) + (2,) * bits + full.shape[2:])
    for step in range(bits):
        bit = (turn + step) % bits
        axis = bits - bit
        me = place.bit(bit)
        keep = lax.dynamic_slice_in_dim(current, me, 1, axis)
        sent = lax.dynamic_slice_in_dim(current, 1 - me, 1, axis)
        got = place.hop(tie(sent, *(waits if step == 1 else start if step == 0 else ())), bit)
        current = (keep.astype(F32) + got.astype(F32)).astype(full.dtype)
    return current.reshape((full.shape[0],) + full.shape[2:])


def clip_index(positions, ends_ref, group, clips):
    inside = jnp.zeros(positions.shape, jnp.int32)
    for clip in range(clips):
        inside = inside + (positions >= ends_ref[group, clip]).astype(jnp.int32)
    return jnp.where(positions < 0, -1, inside)


def dot_nt(left, right):
    return lax.dot_general(left, right, (((1,), (1,)), ((), ())), preferred_element_type=F32)


def dot_nn(left, right):
    return lax.dot_general(left, right, (((1,), (0,)), ((), ())), preferred_element_type=F32)


def dot_tn(left, right):
    return lax.dot_general(left, right, (((0,), (0,)), ((), ())), preferred_element_type=F32)


def band_mask(ends_ref, base_ref, block, clips):
    group = pl.program_id(0)
    start = base_ref[0] + block * BLOCK
    query_at = start + lax.broadcasted_iota(jnp.int32, (BLOCK, 1), 0)
    key_at = start - LEFT + lax.broadcasted_iota(jnp.int32, (1, SPAN), 1)
    apart = lax.broadcasted_iota(jnp.int32, (BLOCK, SPAN), 1) - lax.broadcasted_iota(
        jnp.int32, (BLOCK, SPAN), 0
    )
    query_ids = clip_index(query_at, ends_ref, group, clips)
    key_ids = clip_index(key_at, ends_ref, group, clips)
    return (apart >= 0) & (apart <= LEFT + RIGHT) & (query_ids == key_ids)


def fill_window(window, left_ref, own_ref, right_ref):
    count = own_ref.shape[1]
    window[0:LEFT] = left_ref[0]
    window[LEFT : LEFT + count] = own_ref[0]
    window[LEFT + count :] = right_ref[0]


def band_probs(query, keys, relative, mask):
    scores = dot_nt(query, keys)
    positional = pltpu.roll(dot_nt(query, relative), 0, 1, stride=1, stride_axis=0)
    scores = jnp.where(mask, (scores + positional) * HEAD_DIM ** (-0.5), -1e30)
    expanded = jnp.exp(scores - jnp.max(scores, axis=1, keepdims=True))
    return expanded / jnp.sum(expanded, axis=1, keepdims=True)


def attend_kernel(
    clips, ends_ref, base_ref, q_ref, k_ref, v_ref, kl_ref, vl_ref, kr_ref, vr_ref, rel_ref,
    out_ref, probs_ref, keys, values,
):
    fill_window(keys, kl_ref, k_ref, kr_ref)
    fill_window(values, vl_ref, v_ref, vr_ref)
    low_lane = lax.broadcasted_iota(jnp.int32, (BLOCK, 2 * HEAD_DIM), 1) < HEAD_DIM
    for block in range(q_ref.shape[1] // BLOCK):
        at = block * BLOCK
        mask = band_mask(ends_ref, base_ref, block, clips)
        query = q_ref[0, at : at + BLOCK]
        zero = jnp.zeros_like(query)
        outs = []
        queries = jnp.where(low_lane, query, zero), jnp.where(low_lane, zero, query)
        for one, query_one in enumerate(queries):
            probs = band_probs(query_one, keys[at : at + SPAN], rel_ref[...], mask).astype(BF)
            probs_ref[0, 0, block, one] = probs
            outs.append(dot_nn(probs, values[at : at + SPAN]))
        out_ref[0, at : at + BLOCK] = jnp.where(low_lane, outs[0], outs[1]).astype(BF)


def attend_back_kernel(
    q_ref, k_ref, v_ref, kl_ref, vl_ref, kr_ref, vr_ref, rel_ref, do_ref, probs_ref,
    dq_ref, dk_ref, dv_ref, dkl_ref, dvl_ref, dkr_ref, dvr_ref, drel_ref,
    keys, values, key_sum, value_sum,
):
    scale = HEAD_DIM ** (-0.5)
    count = q_ref.shape[1]
    fill_window(keys, kl_ref, k_ref, kr_ref)
    fill_window(values, vl_ref, v_ref, vr_ref)
    key_sum[...] = jnp.zeros_like(key_sum)
    value_sum[...] = jnp.zeros_like(value_sum)

    @pl.when((pl.program_id(0) == 0) & (pl.program_id(1) == 0))
    def _():
        drel_ref[...] = jnp.zeros_like(drel_ref)

    low_lane = lax.broadcasted_iota(jnp.int32, (BLOCK, 2 * HEAD_DIM), 1) < HEAD_DIM
    row = lax.broadcasted_iota(jnp.int32, (BLOCK, BLOCK), 0)
    column = lax.broadcasted_iota(jnp.int32, (BLOCK, BLOCK), 1)
    flip = (row + column == BLOCK - 1).astype(F32).astype(BF)
    for block in range(count // BLOCK):
        at = block * BLOCK
        query = q_ref[0, at : at + BLOCK]
        grad = do_ref[0, at : at + BLOCK]
        zero = jnp.zeros_like(query)
        some_keys = keys[at : at + SPAN]
        outs, key_part, value_part, rel_part = [], None, None, None
        for low in (True, False):
            pick = (lambda a: jnp.where(low_lane, a, zero)) if low else (
                lambda a: jnp.where(low_lane, zero, a)
            )
            query_one, grad_one = pick(query), pick(grad)
            probs_low = probs_ref[0, 0, block, 0 if low else 1]
            probs = probs_low.astype(F32)
            prob_grads = dot_nt(grad_one, values[at : at + SPAN])
            inner = jnp.sum(prob_grads * probs, axis=1, keepdims=True)
            score_grads = (probs * (prob_grads - inner)).astype(BF)
            turned = pltpu.roll(
                dot_nn(flip, score_grads), SPAN - BLOCK + 1, 1, stride=1, stride_axis=0
            )
            by_offset = dot_nn(flip, turned[:, :BLOCK].astype(BF)).astype(BF)
            outs.append(dot_nn(score_grads, some_keys) + dot_nn(by_offset, rel_ref[0:BLOCK]))
            parts = (
                dot_tn(score_grads, query_one),
                dot_tn(probs_low, grad_one),
                dot_tn(by_offset, query_one),
            )
            if low:
                key_part, value_part, rel_part = parts
            else:
                key_part, value_part, rel_part = (
                    key_part + parts[0],
                    value_part + parts[1],
                    rel_part + parts[2],
                )
        dq_ref[0, at : at + BLOCK] = (jnp.where(low_lane, outs[0], outs[1]) * scale).astype(BF)
        key_sum[at : at + SPAN] += key_part * scale
        value_sum[at : at + SPAN] += value_part
        drel_ref[...] += rel_part * scale
    for total, left, own, right in (
        (key_sum, dkl_ref, dk_ref, dkr_ref),
        (value_sum, dvl_ref, dv_ref, dvr_ref),
    ):
        left[0] = total[0:LEFT].astype(BF)
        own[0] = total[LEFT : LEFT + count]
        right[0] = total[LEFT + count :].astype(BF)


def attend_specs(groups, count, pairs):
    lanes = 2 * HEAD_DIM
    smem = pl.BlockSpec(memory_space=pltpu.SMEM)

    def own(at):
        return pl.BlockSpec((1, count, lanes), lambda g, h: (g, 0, at * pairs + h))

    def edge(at):
        return pl.BlockSpec((1, LEFT, lanes), lambda g, h: (g, 0, at * pairs + h))

    rel = pl.BlockSpec((SPAN, lanes), lambda g, h: (0, 0))
    probs = pl.BlockSpec(
        (1, 1, count // BLOCK, 2, BLOCK, SPAN), lambda g, h: (g, h, 0, 0, 0, 0)
    )
    specs = [smem, smem, own(0), own(1), own(2), edge(0), edge(1), edge(0), edge(1), rel]
    return specs, own, edge, probs


def attend(ends, base, projected, left, right, relative):
    groups, count, _ = projected.shape
    pairs = projected.shape[2] // (6 * HEAD_DIM)
    specs, own, _, probs = attend_specs(groups, count, pairs)
    window = pltpu.VMEM((count + 2 * LEFT, 2 * HEAD_DIM), BF)
    return pl.pallas_call(
        functools.partial(attend_kernel, ends.shape[1]),
        grid=(groups, pairs),
        in_specs=specs,
        out_specs=[own(0), probs],
        out_shape=[
            jax.ShapeDtypeStruct((groups, count, projected.shape[2] // 3), BF),
            jax.ShapeDtypeStruct((groups, pairs, count // BLOCK, 2, BLOCK, SPAN), BF),
        ],
        scratch_shapes=[window, window],
        name="attend",
    )(ends, base, projected, projected, projected, left, left, right, right, relative)


def attend_back(projected, left, right, relative, grad, probs):
    groups, count, _ = projected.shape
    width = projected.shape[2] // 3
    pairs = width // (2 * HEAD_DIM)
    specs, own, edge, saved = attend_specs(groups, count, pairs)
    window = pltpu.VMEM((count + 2 * LEFT, 2 * HEAD_DIM), BF)
    total = pltpu.VMEM((count + 2 * LEFT, 2 * HEAD_DIM), F32)
    rel_sum = pl.BlockSpec((BLOCK, 2 * HEAD_DIM), lambda g, h: (0, 0))
    shape = lambda rows, dtype: jax.ShapeDtypeStruct((groups, rows, width), dtype)
    return pl.pallas_call(
        attend_back_kernel,
        grid=(groups, pairs),
        in_specs=specs[2:] + [own(0), saved],
        out_specs=[own(0), own(0), own(0), edge(0), edge(0), edge(0), edge(0), rel_sum],
        out_shape=[
            shape(count, BF),
            shape(count, F32),
            shape(count, F32),
            shape(LEFT, BF),
            shape(LEFT, BF),
            shape(LEFT, BF),
            shape(LEFT, BF),
            jax.ShapeDtypeStruct((BLOCK, 2 * HEAD_DIM), F32),
        ],
        scratch_shapes=[window, window, total, total],
        name="attend_back",
    )(projected, projected, projected, left, left, right, right, relative, grad, probs)


def products_kernel(steps, first_ref, second_ref, *refs):
    right_refs, out_ref, turned = refs[:-2], refs[-2], refs[-1]
    at = pl.program_id(0)

    @pl.when(at == 0)
    def _():
        turned[...] = first_ref[...].T

    @pl.when(at == 2 * steps)
    def _():
        turned[...] = second_ref[...].T

    for number, right_ref in enumerate(right_refs):

        @pl.when((at >= number * steps) & (at < (number + 1) * steps))
        def _(right_ref=right_ref):
            out_ref[...] = dot_nn(turned[...], right_ref[...]).astype(BF)


def products(first, second, rights):
    count, dim = first.shape
    step = 1024
    steps = rights[0].shape[1] // step
    whole = pl.BlockSpec((count, dim), lambda i: (0, 0))

    def part(number):
        return pl.BlockSpec(
            (count, step), lambda i: (0, jnp.clip(i - number * steps, 0, steps - 1))
        )

    return pl.pallas_call(
        functools.partial(products_kernel, steps),
        grid=(4 * steps,),
        in_specs=[whole, whole] + [part(number) for number in range(4)],
        out_specs=pl.BlockSpec((dim, step), lambda i: (0, i)),
        out_shape=jax.ShapeDtypeStruct((dim, 4 * steps * step), BF),
        scratch_shapes=[pltpu.VMEM((dim, count), BF)],
        name="products",
    )(first, second, *rights)


def norm_parts(values):
    centered = values - jnp.mean(values, axis=1, keepdims=True)
    variance = jnp.mean(centered * centered, axis=1, keepdims=True)
    inverse = lax.rsqrt(variance + 1e-05)
    return centered * inverse, inverse


def norm_kernel(share, *refs):
    if share:
        base_ref, own_ref, other_ref, gain_ref, bias_ref, stream_ref, low_ref = refs
        stream = base_ref[...] + share * (own_ref[0] + other_ref[...].astype(F32))
        stream_ref[...] = stream
    else:
        base_ref, gain_ref, bias_ref, low_ref = refs
        stream = base_ref[...]
    normal_part, _ = norm_parts(stream)
    low_ref[...] = (normal_part * gain_ref[...] + bias_ref[...]).astype(BF)


def norm_back_kernel(share, scale, *refs):
    if share:
        stream_ref, own_ref, other_ref, gain_ref, through_ref, grad_ref, low_ref = refs[:7]
        gradient = own_ref[0] + other_ref[...].astype(F32)
    else:
        stream_ref, own_ref, gain_ref, grad_ref, low_ref = refs[:5]
        gradient = own_ref[...].astype(F32)
    gain_grad_ref, bias_grad_ref = refs[-2:]
    normal_part, inverse = norm_parts(stream_ref[...])
    scaled = gradient * gain_ref[...]
    inner = jnp.mean(scaled * normal_part, axis=1, keepdims=True)
    total = inverse * (scaled - jnp.mean(scaled, axis=1, keepdims=True) - normal_part * inner)
    if share:
        total = total + through_ref[...]
    grad_ref[...] = total
    low_ref[...] = (scale * total).astype(BF)

    @pl.when(pl.program_id(0) == 0)
    def _():
        gain_grad_ref[...] = jnp.zeros_like(gain_grad_ref)
        bias_grad_ref[...] = jnp.zeros_like(bias_grad_ref)

    gain_grad_ref[...] += jnp.sum(gradient * normal_part, axis=0, keepdims=True)
    bias_grad_ref[...] += jnp.sum(gradient, axis=0, keepdims=True)


def row_specs(dim):
    step = 128
    rows = pl.BlockSpec((step, dim), lambda i: (i, 0))
    first = pl.BlockSpec((1, step, dim), lambda i: (0, i, 0))
    line = pl.BlockSpec((1, dim), lambda i: (0, 0))
    return step, rows, first, line


def add_and_norm(base, share, own, other, gain, bias):
    count, dim = base.shape
    step, rows, first, line = row_specs(dim)
    low = jax.ShapeDtypeStruct((count, dim), BF)
    if not share:
        return pl.pallas_call(
            functools.partial(norm_kernel, share),
            grid=(count // step,),
            in_specs=[rows, line, line],
            out_specs=rows,
            out_shape=low,
            name="norm",
        )(base, gain, bias)
    return pl.pallas_call(
        functools.partial(norm_kernel, share),
        grid=(count // step,),
        in_specs=[rows, first, rows, line, line],
        out_specs=[rows, rows],
        out_shape=[jax.ShapeDtypeStruct((count, dim), F32), low],
        name="add_and_norm",
    )(base, own, other, gain, bias)


def norm_and_add_back(stream, own, other, gain, through, scale):
    count, dim = stream.shape
    step, rows, first, line = row_specs(dim)
    share = through is not None
    specs = [rows, first, rows, line, rows] if share else [rows, rows, line]
    args = (stream, own, other, gain, through) if share else (stream, own, gain)
    return pl.pallas_call(
        functools.partial(norm_back_kernel, share, scale),
        grid=(count // step,),
        in_specs=specs,
        out_specs=[rows, rows, line, line],
        out_shape=[
            jax.ShapeDtypeStruct((count, dim), F32),
            jax.ShapeDtypeStruct((count, dim), BF),
            jax.ShapeDtypeStruct((1, dim), F32),
            jax.ShapeDtypeStruct((1, dim), F32),
        ],
        name="norm_back",
    )(*args)


def split_layer_norm(place, values, gain_row, bias_row):
    count = values.shape[-1]
    own_mean = jnp.mean(values, axis=-1, keepdims=True)
    own_square = jnp.sum((values - own_mean) ** 2, axis=-1, keepdims=True)
    stats = jnp.concatenate([own_mean, own_square], -1)
    others = place.sibling(stats)[::-1]
    mean = 0.5 * (own_mean + others[..., :1])
    square = own_square + others[..., 1:]
    square = square + count * ((own_mean - mean) ** 2 + (others[..., :1] - mean) ** 2)
    inverse = lax.rsqrt(square / (2 * count) + 1e-05)
    normal_part = (values - mean) * inverse
    return (normal_part * gain_row + bias_row, (normal_part, inverse))


def split_norm_sums(place, gradient, normal_part, gain_row):
    scaled = gradient * gain_row
    sums = jnp.concatenate(
        [
            jnp.sum(scaled, axis=-1, keepdims=True),
            jnp.sum(scaled * normal_part, axis=-1, keepdims=True),
        ],
        -1,
    )
    return (sums + place.sibling(sums)[::-1]) / (2 * gradient.shape[-1])


def swish_slope(values):
    sigmoid_val = jax.nn.sigmoid(values)
    return sigmoid_val * (1.0 + values * (1.0 - sigmoid_val))


def clip_bounds(positions, ends_ref, group, clips):
    start = jnp.zeros(positions.shape, jnp.int32)
    stop = jnp.full(positions.shape, 1 << 30, jnp.int32)
    for clip in range(clips):
        end = ends_ref[group, clip]
        start = jnp.maximum(start, jnp.where(positions >= end, end, 0))
        stop = jnp.minimum(stop, jnp.where(positions < end, end, 1 << 30))
    return start, jnp.where(positions < 0, positions, stop)


def taps_kernel(clips, ends_ref, base_ref, prev_ref, glu_ref, taps_ref, out_ref, window):
    count = glu_ref.shape[1]
    group = pl.program_id(0)
    window[0:EDGE] = prev_ref[0].astype(F32)
    window[EDGE:] = glu_ref[0].astype(F32)
    at = base_ref[0] + lax.broadcasted_iota(jnp.int32, (count, 1), 0)
    start, _ = clip_bounds(at, ends_ref, group, clips)
    age = jnp.broadcast_to(at - start, (count, 128))
    total = jnp.zeros((count, 128), F32)
    for tap in range(KERNEL):
        first = tap + EDGE - KERNEL + 1
        values = window[first : first + count] * taps_ref[tap : tap + 1]
        total = total + jnp.where(age >= KERNEL - 1 - tap, values, 0.0)
    out_ref[0] = total


def taps_back_kernel(
    clips, ends_ref, base_ref, prev_ref, glu_ref, taps_ref, grad_ref, normal_ref, inverse_ref, sums_ref,
    gain_ref, dglu_ref, dprev_ref, dtaps_ref, dgain_ref, dbias_ref, window, spread,
):
    count = glu_ref.shape[1]
    group = pl.program_id(1)

    @pl.when(group == 0)
    def _():
        dtaps_ref[...] = jnp.zeros_like(dtaps_ref)
        dgain_ref[...] = jnp.zeros_like(dgain_ref)
        dbias_ref[...] = jnp.zeros_like(dbias_ref)

    window[0:EDGE] = prev_ref[0].astype(F32)
    window[EDGE:] = glu_ref[0].astype(F32)
    grad, normal_part = grad_ref[0], normal_ref[0]
    dgain_ref[...] += jnp.sum(grad * normal_part, axis=0, keepdims=True)
    dbias_ref[...] += jnp.sum(grad, axis=0, keepdims=True)
    own = inverse_ref[0] * (
        grad * gain_ref[...] - sums_ref[0, :, 0:1] - normal_part * sums_ref[0, :, 1:2]
    )
    spread[0:EDGE] = jnp.zeros((EDGE, 128), F32)
    spread[EDGE : EDGE + count] = own
    spread[EDGE + count :] = jnp.zeros((EDGE, 128), F32)
    at = base_ref[0] + lax.broadcasted_iota(jnp.int32, (count, 1), 0)
    start, _ = clip_bounds(at, ends_ref, group, clips)
    age = jnp.broadcast_to(at - start, (count, 128))
    source = base_ref[0] - EDGE + lax.broadcasted_iota(jnp.int32, (count + EDGE, 1), 0)
    _, stop = clip_bounds(source, ends_ref, group, clips)
    remain = jnp.broadcast_to(stop - source, (count + EDGE, 128))
    total = jnp.zeros((count + EDGE, 128), F32)
    for tap in range(KERNEL):
        back = KERNEL - 1 - tap
        first = EDGE - back
        kept = jnp.where(age >= back, own, 0.0) * window[first : first + count]
        dtaps_ref[tap : tap + 1] += jnp.sum(kept, axis=0, keepdims=True)
        values = spread[back : back + count + EDGE] * taps_ref[tap : tap + 1]
        total = total + jnp.where(remain > back, values, 0.0)
    dprev_ref[0] = total[0:EDGE].astype(BF)
    dglu_ref[0] = total[EDGE:]


def taps_specs(count, order):
    smem = pl.BlockSpec(memory_space=pltpu.SMEM)
    lanes = pl.BlockSpec((1, count, 128), lambda *at: (at[order[0]], 0, at[order[1]]))
    edge = pl.BlockSpec((1, EDGE, 128), lambda *at: (at[order[0]], 0, at[order[1]]))
    taps = pl.BlockSpec((EDGE, 128), lambda *at: (0, at[order[1]]))
    return smem, lanes, edge, taps


def taps_forward(ends, base, prev, glu, taps):
    groups, count, width = glu.shape
    smem, lanes, edge, tap_lanes = taps_specs(count, (0, 1))
    return pl.pallas_call(
        functools.partial(taps_kernel, ends.shape[1]),
        grid=(groups, width // 128),
        in_specs=[smem, smem, edge, lanes, tap_lanes],
        out_specs=lanes,
        out_shape=jax.ShapeDtypeStruct((groups, count, width), F32),
        scratch_shapes=[pltpu.VMEM((count + EDGE, 128), F32)],
        name="taps",
    )(ends, base, prev, glu, taps)


def taps_back(ends, base, prev, glu, taps, grad, normal_part, inverse, sums, gain):
    groups, count, width = glu.shape
    smem, lanes, edge, tap_lanes = taps_specs(count, (1, 0))
    row_one = pl.BlockSpec((1, count, 1), lambda c, g: (g, 0, 0))
    row_two = pl.BlockSpec((1, count, 2), lambda c, g: (g, 0, 0))
    line = pl.BlockSpec((1, 128), lambda c, g: (0, c))
    shape = jax.ShapeDtypeStruct
    return pl.pallas_call(
        functools.partial(taps_back_kernel, ends.shape[1]),
        grid=(width // 128, groups),
        in_specs=[smem, smem, edge, lanes, tap_lanes, lanes, lanes, row_one, row_two, line],
        out_specs=[lanes, edge, tap_lanes, line, line],
        out_shape=[
            shape((groups, count, width), F32),
            shape((groups, EDGE, width), BF),
            shape((EDGE, width), F32),
            shape((1, width), F32),
            shape((1, width), F32),
        ],
        scratch_shapes=[
            pltpu.VMEM((count + EDGE, 128), F32),
            pltpu.VMEM((count + 2 * EDGE, 128), F32),
        ],
        name="taps_back",
    )(ends, base, prev, glu, taps, grad, normal_part, inverse, sums, gain)


def dot(left, right, left_axis, right_axis):
    return lax.dot_general(
        left, right, (((left_axis,), (right_axis,)), ((), ())), preferred_element_type=F32
    )


def row_major(array):
    return with_layout_constraint(array, Layout(tuple(range(array.ndim))))


def local(
    inputs,
    lengths,
    ffn_in,
    ffn_out,
    qkv_weight,
    out_weight,
    conv_in,
    conv_depth,
    conv_out,
    norm_gain,
    norm_bias,
    rel_key,
    cotangent,
):
    place = Place()
    seq_size, chips, core = place.seq_size, place.chips, place.core
    row_count, dim = inputs.shape[1:]
    hid = ffn_in.shape[3] // 2
    quarter = hid // 2
    width = dim // 2
    rows = 2 * ffn_in.shape[2]
    tap_first, tap_last = 12, 12 + KERNEL

    small = jnp.concatenate([norm_gain[0], norm_bias[0], conv_depth[0]], 0)
    small_count = small.shape[0]
    small = jnp.pad(small, ((0, 128 - small_count), (0, 0))).T
    out_rows = jnp.swapaxes(ffn_out[0], 1, 2)

    def pick(array, count, which):
        parts = array.reshape(array.shape[0], count, -1)
        return place.core_part(parts, 2, which).reshape(array.shape[0], -1)

    def ffn_parts(net, part, which):
        span = slice(part * quarter, (part + 1) * quarter)
        return [pick(ffn_in[0, net], 1, which)[:, span], pick(out_rows[net], 1, which)[:, span]]

    def attention_parts(which):
        return [
            pick(qkv_weight[0], 3, which),
            pick(conv_in[0], 2, which),
            pick(out_weight[0], 1, which),
            pick(conv_out[0], 1, which),
        ]

    def chip_block(kept, sent):
        kept, sent = jnp.concatenate(kept, 1), jnp.concatenate(sent, 1)
        return place.by_core(kept, place.sibling(sent), 0)

    other = 1 - core
    first_block = chip_block(
        ffn_parts(0, 0, core) + [small], ffn_parts(0, 0, other) + [small]
    )
    later_block = chip_block(
        ffn_parts(0, 1, core) + attention_parts(core) + ffn_parts(1, 0, core) + ffn_parts(1, 1, core),
        ffn_parts(0, 1, other)
        + attention_parts(other)
        + ffn_parts(1, 0, other)
        + ffn_parts(1, 1, other),
    )
    n_attention = 7 * width
    attention_block = later_block[:, 2 * quarter : 2 * quarter + n_attention]
    attention_all = lax.all_gather(attention_block, ("seq", "plane"), axis=0, tiled=True)
    at = [0, quarter]
    at += [2 * quarter + n_attention + part * quarter for part in range(4)]
    pieces = [later_block[:, start : start + quarter] for start in at]
    chunks = [
        (
            [first_block[:, :quarter], first_block[:, 2 * quarter :]],
            [first_block[:, quarter : 2 * quarter]],
        ),
        ([pieces[0]], [pieces[1]]),
        ([pieces[2]], [pieces[3]]),
        ([pieces[4]], [pieces[5]]),
    ]
    gathered, z_marks, firsts, seconds = [], [], [], []

    def fetch(*waits):
        index = len(gathered)
        left, right = chunks[index]
        block = tie(jnp.concatenate(left + right, 1), *z_marks[-1:], *waits)
        spread = place.swap_seq(jnp.broadcast_to(block[None], (seq_size,) + block.shape))
        z_marks.append(tip(spread))
        marks = []
        n_left = sum(part.shape[1] for part in left)
        parts = tie(spread[..., :n_left], *seconds[-1:]), tie(spread[..., n_left:], *seconds[-1:])
        fulls = [gather_plane(place, part, turn, marks) for turn, part in enumerate(parts)]
        firsts.append(marks[place.bits])
        seconds.append(marks[-1])
        gathered.append([full.reshape(dim, -1) for full in fulls])

    fetch()
    fetch()
    small_all = gathered[0][0][:, quarter:].T.astype(F32)
    gains, biases = small_all[:6, None], small_all[6:12, None]
    tap_values = place.core_part(small_all[tap_first:tap_last], 1, core)
    gain3 = place.core_part(small_all[3], 0, core)
    bias3 = place.core_part(small_all[9], 0, core)
    w_qkv = attention_all[:, : 3 * width]
    w_first = attention_all[:, 3 * width : 5 * width]
    columns = attention_all[:, 5 * width :]
    from_other = place.sibling(place.core_part(columns, 0, other))
    columns = place.core_part(columns, 0, core)
    w_out = place.by_core(columns[:, :width], from_other[:, :width], 1)
    w_second = place.by_core(columns[:, width:], from_other[:, width:], 1)

    group_lengths = jnp.concatenate([lengths, place.sibling(lengths)], 0)
    clips = group_lengths.shape[1]
    order = jnp.arange(clips)
    clip_ends = jnp.sum(
        jnp.where(order[None, :, None] >= order[None, None, :], group_lengths[:, None, :], 0), axis=2
    )
    first_row = place.seq * row_count

    def weights_of(net, part):
        left, right = gathered[2 * net + part]
        return left[:, :quarter], right

    def flat2(array):
        return array.reshape(2 * row_count, -1)

    def pair2(array):
        return array.reshape(2, row_count, -1)

    def feed_forward(normed, net):
        normed_low = flat2(place.both(normed))
        pres, acts, branch = [], [], 0.0
        for part in range(2):
            w_in, w_down = weights_of(net, part)
            pre_act = dot(normed_low, w_in, 1, 0)
            act_low = (pre_act * jax.nn.sigmoid(pre_act)).astype(BF)
            if net == 0 and part == 0:
                fetch(tip(act_low))
            branch = branch + dot(act_low, w_down, 1, 1)
            pres.append(pre_act)
            acts.append(act_low)
        return pair2(branch), (normed_low, pres, acts)

    def joined(base, share, branch, norm_index, *marks):
        received = place.from_sibling(branch)
        gain = tie(gains[norm_index], *marks)
        return add_and_norm(base, share, branch, received, gain, biases[norm_index])

    stream = inputs[0].astype(F32)
    normed = add_and_norm(stream, 0.0, None, None, gains[0], biases[0])
    branch, ffn_first = feed_forward(normed, 0)
    after_ffn, normed = joined(stream, 0.5, branch, 1)
    fetch(tip(normed))
    attn_input = flat2(place.both(normed))
    projected = pair2(dot(attn_input, w_qkv, 1, 0).astype(BF))
    from_left = place.along(projected[:, row_count - LEFT :, width:], 1)
    from_right = place.along(projected[:, :RIGHT, width:], -1)
    from_right = jnp.pad(from_right, ((0, 0), (0, LEFT - RIGHT), (0, 0)))
    relative = jnp.pad(
        jnp.concatenate([rel_key[0], rel_key[0]], 1), ((0, SPAN - rel_key.shape[1]), (0, 0))
    )
    base = jnp.reshape(first_row, (1,))
    attended, probs = attend(clip_ends, tie(base, firsts[2]), projected, from_left, from_right, relative)
    attended = flat2(attended)
    after_attn, normed = joined(after_ffn, 1.0, pair2(dot(attended, w_out, 1, 0)), 2, seconds[2], firsts[3])
    conv_input = flat2(place.both(normed))
    spread_pre = pair2(dot(conv_input, w_first, 1, 0))
    value_part, gate_sig = spread_pre[..., :width], jax.nn.sigmoid(spread_pre[..., width:])
    gated_low = (value_part * gate_sig).astype(BF)
    from_prev = place.along(gated_low[:, row_count - EDGE :], 1)
    tap_rows = jnp.pad(tap_values, ((0, EDGE - KERNEL), (0, 0)))
    filtered = taps_forward(clip_ends, base, from_prev, gated_low, tap_rows)
    normed_conv, depth_norm = split_layer_norm(place, filtered, gain3, bias3)
    swished = (normed_conv * jax.nn.sigmoid(normed_conv)).astype(BF)
    after_conv, normed = joined(after_attn, 1.0, pair2(dot(flat2(swished), w_second, 1, 0)), 4)
    branch, ffn_second = feed_forward(normed, 1)
    fourth, result = joined(after_conv, 0.5, branch, 5)
    outputs = result[None]

    def summed(terms):
        return jnp.sum(place.swap_seq(terms).astype(F32), 0)

    def scatter_early(terms):
        terms = jnp.concatenate(terms, 1)
        terms = row_major(terms.reshape(seq_size, chips * rows, terms.shape[1]))
        return row_major(lax.psum_scatter(terms, "plane", scatter_dimension=1, tiled=True))

    def plane_sums(pair, waits=(), start=()):
        parts = []
        for turn, terms in enumerate(pair):
            blocks = terms.reshape(seq_size, chips, rows, -1)
            parts.append(scatter_plane(place, blocks, turn, waits, start))
        return jnp.concatenate(parts, -1)

    gain_grads = [None] * 6
    bias_grads = [None] * 6

    def back_to(norm_index, stream_at, branch, through, share, *marks):
        received = None if through is None else place.from_sibling(branch)
        gain = tie(gains[norm_index], *marks)
        grad, low, gain_grads[norm_index], bias_grads[norm_index] = norm_and_add_back(
            stream_at, branch, received, gain, through, share
        )
        return grad, low

    def feed_back(low, net, cached):
        normed_low, pres, acts = cached
        branch_grad = flat2(place.both(low))
        pre_grads, normed_grad = [], 0.0
        for part in range(2):
            act_grad = dot(branch_grad, weights_of(net, part)[1], 1, 0)
            pre_grads.append((act_grad * swish_slope(pres[part])).astype(BF))
        for part in range(2):
            normed_grad = normed_grad + dot(pre_grads[part], weights_of(net, part)[0], 1, 1)
        return pair2(normed_grad), pre_grads, acts, normed_low, branch_grad

    def exchanged(wide):
        received = place.sibling(place.core_part(wide, 1, other))
        return place.by_core(place.core_part(wide, 1, core), received, 0)

    grad_fourth, low = back_to(5, fourth, cotangent[0], None, 0.5)
    branch, pre_grads, acts, normed_low, branch_grad = feed_back(low, 1, ffn_second)
    second_terms = [products(normed_low, branch_grad, pre_grads + acts)]
    grad_conv_out, low = back_to(4, after_conv, branch, grad_fourth, 1.0)
    branch_grad = flat2(place.both(low))
    conv_out_terms = exchanged(dot(flat2(swished), branch_grad, 0, 0).astype(BF))
    swish_grad = pair2(dot(branch_grad, w_second, 1, 1))
    swish_grad = swish_grad * swish_slope(normed_conv)
    sums = split_norm_sums(place, swish_grad, depth_norm[0], gain3)
    gated_grad, to_prev, tap_grads, gain3_grad, bias3_grad = taps_back(
        clip_ends, base, from_prev, gated_low, tap_rows, swish_grad, *depth_norm, sums, gain3[None]
    )
    to_prev = place.along(to_prev, -1).astype(F32)
    gated_grad = gated_grad + jnp.pad(to_prev, ((0, 0), (row_count - EDGE, 0), (0, 0)))
    spread_grad = flat2(
        jnp.concatenate(
            [gated_grad * gate_sig, gated_grad * value_part * gate_sig * (1.0 - gate_sig)], axis=2
        ).astype(BF)
    )
    branch = pair2(dot(spread_grad, w_first, 1, 1))
    conv_in_terms = dot(conv_input, spread_grad, 0, 0).astype(BF)
    grad_attn_out, low = back_to(2, after_attn, branch, grad_conv_out, 1.0)
    branch_grad = flat2(place.both(low))
    out_terms = exchanged(dot(attended, branch_grad, 0, 0).astype(BF))
    attended_grad = pair2(dot(branch_grad, w_out, 1, 1).astype(BF))
    query_grad, key_grad, value_grad, kl, vl, kr, vr, relative_grad = attend_back(
        projected, from_left, from_right, relative, attended_grad, probs
    )
    second_sum = summed(tie(scatter_early(second_terms), tip(query_grad)))
    to_left = place.along(jnp.concatenate([kl, vl], 2), -1).astype(F32)
    to_right = place.along(jnp.concatenate([kr[:, :RIGHT], vr[:, :RIGHT]], 2), 1).astype(F32)
    own_grad = (
        jnp.concatenate([key_grad, value_grad], 2)
        + jnp.pad(to_left, ((0, 0), (row_count - LEFT, 0), (0, 0)))
        + jnp.pad(to_right, ((0, 0), (0, row_count - RIGHT), (0, 0)))
    )
    projected_grad = flat2(jnp.concatenate([query_grad, own_grad.astype(BF)], axis=2))
    branch = pair2(dot(projected_grad, w_qkv, 1, 1))
    qkv_terms = dot(attn_input, projected_grad, 0, 0).astype(BF)
    grad_ffn_out, low = back_to(
        1, after_ffn, branch, grad_attn_out, 0.5
    )
    branch, pre_grads, acts, normed_low, branch_grad = feed_back(low, 0, ffn_first)
    downs = [dot(branch_grad, acts[part], 0, 0).astype(BF) for part in range(2)]
    ins = [dot(normed_low, pre_grads[part], 0, 0).astype(BF) for part in range(2)]
    attention_part = scatter_early([qkv_terms, conv_in_terms, out_terms, conv_out_terms])
    grad_input, _ = back_to(0, stream, branch, grad_ffn_out, 1.0)
    down_part = plane_sums(downs, (tip(ins[1]), tip(grad_input)))
    in_part = plane_sums(ins, start=(tip(down_part),))
    down_sum = summed(tie(down_part, tip(second_sum)))
    offsets = LEFT + RIGHT + 1
    relative_grad = relative_grad[:offsets, :HEAD_DIM] + relative_grad[:offsets, HEAD_DIM:]

    def spread_core(half_rows):
        return place.by_core(half_rows, jnp.zeros_like(half_rows), 1)

    gain_grads[3] = spread_core(gain3_grad)
    bias_grads[3] = spread_core(bias3_grad)
    small_grads = jnp.concatenate(
        gain_grads + bias_grads + [spread_core(tap_grads[:KERNEL])], 0
    )
    small_grads = jnp.pad(small_grads, ((0, 128 - small_count), (0, 0))).T
    rel_part = jnp.pad(relative_grad, ((0, -offsets % 8), (0, 128 - HEAD_DIM)))
    rel_part = rel_part + place.sibling(rel_part)
    current = small_grads.reshape((seq_size,) + (2,) * place.bits + (rows, 128))
    for bit in range(place.bits):
        axis = place.bits - bit
        me = place.bit(bit)
        keep = lax.dynamic_slice_in_dim(current, me, 1, axis)
        sent = lax.dynamic_slice_in_dim(current, 1 - me, 1, axis)
        got = place.hop(jnp.concatenate([sent.reshape(-1, 128), rel_part], 0), bit)
        current = keep + got[: -rel_part.shape[0]].reshape(keep.shape)
        rel_part = rel_part + got[-rel_part.shape[0] :]
    rel_all = jnp.broadcast_to(rel_part[None], (seq_size,) + rel_part.shape)
    small_total = summed(
        tie(jnp.concatenate([current.reshape(seq_size, rows, 128), rel_all], 1), tip(down_sum))
    )
    last_sum = summed(tie(jnp.concatenate([in_part, attention_part], -1), tip(small_total)))
    in_sum, attention_sum = last_sum[:, :hid], last_sum[:, hid:]
    rel_total = small_total[rows : rows + offsets, :HEAD_DIM]
    small_total = small_total[:rows]
    small_sum = place.core_part(small_total, 0, core) + place.sibling(
        place.core_part(small_total, 0, other)
    )
    small_sum = small_sum[:, :small_count].T

    def own_rows(total, counts):
        received = place.sibling(place.core_part(total, 0, other))
        mine = place.core_part(total, 0, core)
        results, start = [], 0
        for count, n in counts:
            halves = [
                part[:, start : start + n].reshape(-1, count, n // count) for part in (mine, received)
            ]
            results.append(place.by_core(*halves, 2).reshape(mine.shape[0], 2 * n))
            start += n
        return results

    in_second, down_second = own_rows(second_sum, [(1, hid), (1, hid)])
    (down_first,) = own_rows(down_sum, [(1, hid)])
    qkv_sum, first_sum, out_sum, second_sum = own_rows(
        attention_sum, [(3, 3 * width), (2, 2 * width), (1, width), (1, width)]
    )
    (in_first,) = own_rows(in_sum, [(1, hid)])
    return (
        outputs,
        grad_input[None],
        jnp.stack([in_first, in_second])[None],
        jnp.swapaxes(jnp.stack([down_first, down_second]), 1, 2)[None],
        qkv_sum[None],
        out_sum[None],
        first_sum[None],
        small_sum[None, tap_first:tap_last],
        second_sum[None],
        small_sum[None, :6],
        small_sum[None, 6:12],
        rel_total[None],
    )


def solution(mesh):
    seq_size, fsdp_size = mesh.shape["seq"], mesh.shape["fsdp"]
    chips = Mesh(mesh.devices.reshape(seq_size, fsdp_size // 2, 2), ("seq", "plane", "core"))
    fsdp = ("plane", "core")
    spread = ("seq", "plane", "core")
    tokens = P(fsdp, "seq", None)
    split_rows = P(None, spread, None)
    split_last = P(None, None, spread)
    weights = (
        P(None, None, spread, None),
        P(None, None, None, spread),
        split_rows,
        split_rows,
        split_rows,
        split_last,
        split_rows,
        split_last,
        split_last,
        P(),
    )
    return jax.shard_map(
        local,
        mesh=chips,
        in_specs=(tokens, P(fsdp, None)) + weights + (tokens,),
        out_specs=(tokens, tokens) + weights,
        check_vma=False,
    )
```
